256 devices in a mesh: dp: 16 (over y, x_lo, core), seq: 16 (over z, x_hi).
Axes of the slice: x: 4 (x_hi: 2, x_lo: 2; x = x_hi * 2 + x_lo), y: 4, z: 8, core: 2. Of those that a mesh axis runs over, the one named last changes fastest.
Arguments:
- queries: bfloat16 [16, 4096, 384], P('dp', 'seq'), may hold values from -8 to 8
- keys: bfloat16 [16, 4096, 384], P('dp', 'seq'), may hold values from -8 to 8
- values: bfloat16 [16, 4096, 384], P('dp', 'seq'), may hold values from -6 to 6
- out_weight: bfloat16 [384, 768], replicated, may hold values from -0.3125 to 0.3125
- out_grad: bfloat16 [16, 4096, 768], P('dp', 'seq'), may hold values from -6 to 6
- offsets: int32 [3, 6], replicated, may hold values from 0 to 7
- counts: int32 [16], P('dp'), may hold values from 2048 to 4096
Outputs:
- attended: bfloat16 [16, 4096, 768], P('dp', 'seq')
- grad_queries: bfloat16 [16, 4096, 384], P('dp', 'seq')
- grad_keys: bfloat16 [16, 4096, 384], P('dp', 'seq')
- grad_values: bfloat16 [16, 4096, 384], P('dp', 'seq')
- grad_weight: float32 [384, 768], P('seq')
The draws below stay inside these ranges and needn't reach their ends.
All inputs are finite; a program needn't handle non-finite values.
Results may differ from the reference program's by a relative error of at most 0.027.
Values may be sent and summed in bfloat16 or wider, within the bound.
No kernel may reach another device: no remote copies, remote signals or barrier semaphores. Data moves between devices by JAX's collectives and lax.ppermute only.
A program may use at most 128 MiB of HBM per device.

```python
import math
import jax
import jax.numpy as jnp
from jax import lax

D = 768
HEADS = 6
HEAD_DIM = 64
WIDTH = 384
LENGTH = 4096
SLIDES = 16


def draw_queries(key, part):
    key = jax.random.fold_in(key, 11)
    base = 2.0 * jnp.clip(jax.random.normal(key, (SLIDES, LENGTH, WIDTH), jnp.float32), -3.9, 3.9)
    return base.astype(jnp.bfloat16)


def draw_keys(key, part):
    key = jax.random.fold_in(key, 23)
    base = 2.0 * jnp.clip(jax.random.normal(key, (SLIDES, LENGTH, WIDTH), jnp.float32), -3.9, 3.9)
    return base.astype(jnp.bfloat16)


def set_ends(array, own_key, low, high):
    dims = array.shape
    place = [jax.random.randint(jax.random.fold_in(own_key, axis), (), 0, dims[axis]) for axis in range(len(dims))]
    array = array.at[tuple(place)].set(low)
    longest = dims.index(max(dims))
    place[longest] = (place[longest] + 1) % dims[longest]
    return array.at[tuple(place)].set(high)


def level_of(key, shape, pieces, smallest, top_value):
    factor_of, own = 1.0, jax.random.fold_in(key, 6)
    for dim, blocks in pieces:
        draws = jnp.exp(jax.random.uniform(jax.random.fold_in(own, dim), (blocks,), jnp.float32, smallest / len(pieces), top_value / len(pieces)))
        factor_of = factor_of * jnp.repeat(draws, shape[dim] // blocks).reshape([-1 if axis == dim else 1 for axis in range(len(shape))])
    return factor_of


def bell_draw(own_key, dims, scale, limit, split=(), kind=jnp.bfloat16):
    drawn = scale * jax.random.normal(own_key, dims, jnp.float32)
    if split:
        drawn = drawn * level_of(own_key, dims, split, -0.22, 0.18)
    return jnp.clip(drawn, -limit, limit).astype(kind)


def setup_inputs(seed: int = 0) -> dict:
    seeds = jax.random.split(jax.random.key(seed), 8)
    queries = draw_queries(jax.random.fold_in(seeds[7], 71), 0)
    keys = draw_keys(jax.random.fold_in(seeds[7], 71), 0)
    values = bell_draw(seeds[2], (SLIDES, LENGTH, WIDTH), 1.0, 6.0, ((0, 16), (1, 16)))
    out_weight = bell_draw(seeds[3], (WIDTH, D), WIDTH ** -0.5, 0.3125)
    out_grad = bell_draw(seeds[4], (SLIDES, LENGTH, D), 1.0, 6.0, ((0, 16), (1, 16)))
    offsets = set_ends(jax.random.randint(seeds[5], (3, HEADS), 0, 8), jax.random.fold_in(seeds[5], 1), 0, 7).astype(jnp.int32)
    counts = set_ends(jax.random.randint(seeds[6], (SLIDES,), LENGTH // 2, LENGTH + 1), jax.random.fold_in(seeds[6], 1), LENGTH // 2, LENGTH).astype(jnp.int32)
    return dict(queries=queries, keys=keys, values=values, out_weight=out_weight, out_grad=out_grad, offsets=offsets, counts=counts)


segment_parts = (16, 4, 2, 1)
dilation_steps = (1, 2, 4, 8)
masked_score = -1e+30

def select_rows(block, spacing, offset_row):
    shaped = block.reshape(block.shape[0] // spacing, spacing, block.shape[1], block.shape[2])
    picks = jnp.arange(spacing, dtype=jnp.int32)[:, None] == offset_row[None, :]
    return lax.optimization_barrier(jnp.sum(jnp.where(picks[None, :, :, None], shaped, jnp.zeros_like(shaped)), axis=1))

def place_rows(picked, spacing, offset_row, filler):
    picks = jnp.arange(spacing, dtype=jnp.int32)[:, None] == offset_row[None, :]
    spread = jnp.where(picks[None, :, :, None], picked[:, None, :, :], filler)
    return spread.reshape(picked.shape[0] * spacing, picked.shape[1], picked.shape[2])

def pair_offsets(offsets, pair_index):
    if pair_index == 0:
        return jnp.zeros((HEADS,), jnp.int32)
    return (offsets[pair_index - 1] % dilation_steps[pair_index]).astype(jnp.int32)

def slide_pass(query_all, key_all, value_all, grad_out, tile_count, out_weight, offsets):
    score_scale = 1.0 / math.sqrt(HEAD_DIM)
    query_heads = query_all.reshape(LENGTH, HEADS, HEAD_DIM)
    key_heads = key_all.reshape(LENGTH, HEADS, HEAD_DIM)
    value_heads = value_all.reshape(LENGTH, HEADS, HEAD_DIM)
    saved = []
    top_list, den_list, num_list = ([], [], [])
    for pair_index in range(4):
        spacing = dilation_steps[pair_index]
        segment = LENGTH // segment_parts[pair_index]
        offset_row = pair_offsets(offsets, pair_index)
        picked = segment // spacing
        segments = LENGTH // segment
        positions = jnp.arange(LENGTH // spacing, dtype=jnp.int32)[:, None] * spacing + offset_row[None, :]
        allowed = (positions < tile_count).reshape(segments, picked, HEADS).transpose(0, 2, 1)[:, :, None, :]
        query_f = select_rows(query_heads, spacing, offset_row).reshape(segments, picked, HEADS, HEAD_DIM).astype(jnp.float32)
        key_f = select_rows(key_heads, spacing, offset_row).reshape(segments, picked, HEADS, HEAD_DIM).astype(jnp.float32)
        value_f = select_rows(value_heads, spacing, offset_row).reshape(segments, picked, HEADS, HEAD_DIM).astype(jnp.float32)
        scores = jnp.einsum('sqhd,skhd->shqk', query_f, key_f) * score_scale
        scores = jnp.where(allowed, scores, masked_score)
        row_max = lax.optimization_barrier(jnp.max(scores, axis=-1))
        exponent = jnp.where(allowed, jnp.exp(scores - row_max[..., None]), 0.0)
        denominator = lax.optimization_barrier(jnp.sum(exponent, axis=-1))
        exponent_low = lax.optimization_barrier(exponent.astype(jnp.bfloat16))
        numerator = jnp.einsum('shqk,skhd->sqhd', exponent_low.astype(jnp.float32), value_f)
        rows_all = LENGTH // spacing
        top_list.append(place_rows(row_max.transpose(0, 2, 1).reshape(rows_all, HEADS, 1), spacing, offset_row, masked_score))
        den_list.append(place_rows(denominator.transpose(0, 2, 1).reshape(rows_all, HEADS, 1), spacing, offset_row, 0.0))
        num_list.append(place_rows(numerator.reshape(rows_all, HEADS, HEAD_DIM), spacing, offset_row, 0.0))
        saved.append((spacing, offset_row, segments, picked, query_f, key_f, value_f, exponent_low))
    top_all = top_list[0]
    for extra in top_list[1:]:
        top_all = jnp.maximum(top_all, extra)
    pair_weights = [jnp.exp(entry - top_all) for entry in top_list]
    den_all = sum((weight_one * den_one for weight_one, den_one in zip(pair_weights, den_list)))
    num_all = sum((weight_one * num_one for weight_one, num_one in zip(pair_weights, num_list)))
    valid = (jnp.arange(LENGTH, dtype=jnp.int32) < tile_count).astype(jnp.float32)[:, None, None]
    norm = valid / (den_all + 1.0 - valid)
    mixed = (num_all * norm).astype(jnp.bfloat16).reshape(LENGTH, WIDTH)
    attended = jnp.dot(mixed, out_weight, preferred_element_type=jnp.float32).astype(jnp.bfloat16)
    grad_mixed = jnp.dot(grad_out, out_weight.T, preferred_element_type=jnp.float32).astype(jnp.bfloat16)
    weight_part = jnp.dot(mixed.T, grad_out, preferred_element_type=jnp.float32)
    grad_heads = grad_mixed.reshape(LENGTH, HEADS, HEAD_DIM)
    delta = lax.optimization_barrier(jnp.sum(grad_heads.astype(jnp.float32) * mixed.reshape(LENGTH, HEADS, HEAD_DIM).astype(jnp.float32), axis=-1, keepdims=True))
    grad_q = jnp.zeros((LENGTH, HEADS, HEAD_DIM), jnp.float32)
    grad_k = jnp.zeros((LENGTH, HEADS, HEAD_DIM), jnp.float32)
    grad_v = jnp.zeros((LENGTH, HEADS, HEAD_DIM), jnp.float32)
    for pair_index in range(4):
        spacing, offset_row, segments, picked, query_f, key_f, value_f, exponent_low = saved[pair_index]
        factor = select_rows(pair_weights[pair_index] * norm, spacing, offset_row).reshape(segments, picked, HEADS).transpose(0, 2, 1)
        delta_sel = select_rows(delta, spacing, offset_row).reshape(segments, picked, HEADS).transpose(0, 2, 1)
        grad_sel = select_rows(grad_heads, spacing, offset_row).reshape(segments, picked, HEADS, HEAD_DIM).astype(jnp.float32)
        prob = exponent_low.astype(jnp.float32) * factor[..., None]
        prob_low = lax.optimization_barrier(prob.astype(jnp.bfloat16))
        value_grad = jnp.einsum('shqk,sqhd->skhd', prob_low.astype(jnp.float32), grad_sel)
        dprob = jnp.einsum('sqhd,skhd->shqk', grad_sel, value_f)
        dscore = lax.optimization_barrier((prob * (dprob - delta_sel[..., None])).astype(jnp.bfloat16)).astype(jnp.float32)
        query_grad = jnp.einsum('shqk,skhd->sqhd', dscore, key_f) * score_scale
        key_grad = jnp.einsum('shqk,sqhd->skhd', dscore, query_f) * score_scale
        rows_all = LENGTH // spacing
        grad_q = grad_q + place_rows(query_grad.reshape(rows_all, HEADS, HEAD_DIM), spacing, offset_row, 0.0)
        grad_k = grad_k + place_rows(key_grad.reshape(rows_all, HEADS, HEAD_DIM), spacing, offset_row, 0.0)
        grad_v = grad_v + place_rows(value_grad.reshape(rows_all, HEADS, HEAD_DIM), spacing, offset_row, 0.0)
    return (attended, grad_q.reshape(LENGTH, WIDTH).astype(jnp.bfloat16), grad_k.reshape(LENGTH, WIDTH).astype(jnp.bfloat16), grad_v.reshape(LENGTH, WIDTH).astype(jnp.bfloat16), weight_part)

def reference(queries, keys, values, out_weight, out_grad, offsets, counts):

    def one_slide(items):
        return slide_pass(items[0], items[1], items[2], items[3], items[4], out_weight, offsets)
    attended, grad_queries, grad_keys, grad_values, weight_parts = lax.map(one_slide, (queries, keys, values, out_grad, counts))
    return (attended, grad_queries, grad_keys, grad_values, lax.optimization_barrier(jnp.sum(weight_parts, axis=0)))
```

```python
import jax
import jax.numpy as jnp
from jax import lax
from jax.experimental import pallas as pl
from jax.experimental.pallas import tpu as pltpu
from jax.sharding import PartitionSpec as P

bf16 = jnp.bfloat16
f32 = jnp.float32
low_bias = -1e30


def dot_nn(a, b):
    return lax.dot_general(a, b, (((1,), (0,)), ((), ())), preferred_element_type=f32)


def dot_nt(a, b):
    return lax.dot_general(a, b, (((1,), (1,)), ((), ())), preferred_element_type=f32)


def dot_tn(a, b):
    return lax.dot_general(a, b, (((0,), (0,)), ((), ())), preferred_element_type=f32)


def first_half(rows):
    return lax.broadcasted_iota(jnp.int32, (rows, 128), 1) < 64


def half_of(x, h):
    m = first_half(x.shape[0])
    z = jnp.zeros_like(x)
    return jnp.where(m, x, z) if h == 0 else jnp.where(m, z, x)


def row_order(back):
    a = lax.broadcasted_iota(jnp.int32, (256, 256), 0 if not back else 1)
    b = lax.broadcasted_iota(jnp.int32, (256, 256), 1 if not back else 0)
    return jnp.where(b == (a & 31) * 8 + (a >> 5), 1.0, 0.0).astype(bf16)


class Place:
    def __init__(self, info, offsets, counts):
        self.j = info[0] & 3
        self.base = (info[0] >> 2) * 1024
        self.quarter = info[0] >> 2
        self.chunk = jnp.minimum(info[1], 2)
        self.count = counts[0]
        self.offsets = offsets

    def offs(self, pair):
        r = 2 << pair
        return [self.offsets[pair, 2 * self.chunk + h] & (r - 1) for h in (0, 1)]

    def bias(self, n, step, o, base):
        kk = lax.broadcasted_iota(jnp.int32, (1, n), 1)
        pos = base + ((self.j ^ ((kk >> 5) & 3)) << 8) + (kk & 31) * 8 + o + step * (kk >> 7)
        return jnp.where(pos < self.count, 0.0, low_bias)

    def bias_slot(self, slot):
        kk = lax.broadcasted_iota(jnp.int32, (1, 256), 1)
        pos = self.base + ((self.j ^ slot) << 8) + (kk & 31) * 8 + (kk >> 5)
        return jnp.where(pos < self.count, 0.0, low_bias)

    def valid(self, res):
        rr = lax.broadcasted_iota(jnp.int32, (128, 128), 0)
        pos = self.base + ((self.j ^ (rr >> 5)) << 8) + (rr & 31) * 8 + res
        return jnp.where(pos < self.count, 1.0, 0.0)


def pick(read, pair, oo):
    r = 2 << pair
    m = first_half(128)
    parts = [jnp.where(m, read(oo[0] + r * i), read(oo[1] + r * i)) for i in range(8 // r)]
    return parts[0] if len(parts) == 1 else jnp.concatenate(parts, axis=0)


def put(read, write, val, pair, oo, add):
    r = 2 << pair
    m = first_half(128)
    for i in range(8 // r):
        blk = val[i * 128 : (i + 1) * 128]
        for h in (0, 1):
            mine = m if h == 0 else ~m
            old = read(oo[h] + r * i)
            write(oo[h] + r * i, jnp.where(mine, old + blk if add else blk, old))


def reader(ref, *lead):
    return lambda i: ref[(*lead, i)]


def writer(ref, *lead):
    def w(i, val):
        ref[(*lead, i)] = val

    return w


def slot_rows(ref, slot, *lead):
    return ref[(*lead, slice(None), slice(slot * 32, slot * 32 + 32), slice(None))].reshape(256, 128)


def attend(q2, k2, v2, bias):
    nk = k2.shape[0]
    out, es, ms = None, [], []
    one = jnp.ones((nk, 128), bf16)
    for h in (0, 1):
        s = dot_nt(q2, half_of(k2, h)) + bias[h]
        m = jnp.max(s, axis=1, keepdims=True)
        e = jnp.exp(s - m).astype(bf16)
        o = dot_nn(e, jnp.concatenate([half_of(v2, h), half_of(one, h)], axis=1))
        out = o if out is None else out + o
        es.append(e)
        ms.append(m)
    n = q2.shape[0]
    top = jnp.where(first_half(n), jnp.broadcast_to(ms[0], (n, 128)), jnp.broadcast_to(ms[1], (n, 128)))
    return es, top, out


def back(q2, k2, v2, gf2, fd2, es):
    dq = dk = dv = None
    for h in (0, 1):
        kh, vh = half_of(k2, h), half_of(v2, h)
        e = es[h]
        dp = dot_nt(gf2, vh)
        ds = (e.astype(f32) * (dp - fd2[:, 64 * h : 64 * h + 1])).astype(bf16)
        a, b, c = dot_nn(ds, kh), dot_tn(ds, half_of(q2, h)), dot_tn(e, half_of(gf2, h))
        dq, dk, dv = (a, b, c) if dq is None else (dq + a, dk + b, dv + c)
    return dq, dk, dv


def prep_body(info, q, k, v, og, w, o0, o1, o2, o3, px):
    order = row_order(False)
    px[0] = (dot_nn(order, q[...]) * 0.125).astype(bf16)
    px[1] = dot_nn(order, k[...]).astype(bf16)
    px[2] = dot_nn(order, v[...]).astype(bf16)
    px[3] = dot_nn(order, dot_nt(og[...], w[...]).astype(bf16)).astype(bf16)
    for d, o in enumerate((o0, o1, o2, o3)):
        c = pl.multiple_of(jnp.minimum(info[1] ^ d, 2) * 128, 128)
        for i in range(4):
            o[i] = px[i, :, pl.ds(c, 128)]


def collect_body(info, offsets, counts, m0, m1, m2, m3, x, s4, s8):
    place = Place(info, offsets, counts)
    for slot, m in enumerate((m0, m1, m2, m3)):
        for i in range(4):
            x[i, :, slot * 32 : slot * 32 + 32, :] = m[i].reshape(8, 32, 128)
    o3, o4 = place.offs(1), place.offs(2)
    for i in (0, 1):
        s4[i, 0:256] = pick(reader(x, i + 1), 1, o3)
        last = pick(reader(x, i + 1), 2, o4)
        s4[i, 256:384] = last
        s8[i] = last


def near_body(info, offsets, counts, x, top, num, den, m1, m2, e1, e2):
    place = Place(info, offsets, counts)
    for slot in range(4):
        b = place.bias_slot(slot)
        sl = slice(slot * 32, slot * 32 + 32)
        es, t, o = attend(*[slot_rows(x, slot, i) for i in range(3)], [b, b])
        e1[slot, 0], e1[slot, 1] = es
        t = t.reshape(8, 32, 128)
        top[:, sl, :] = t
        m1[:, sl, :] = t
        num[:, sl, :] = o[:, :128].reshape(8, 32, 128)
        den[:, sl, :] = o[:, 128:].reshape(8, 32, 128)
    oo = place.offs(0)
    q2, k2, v2 = [pick(reader(x, i), 0, oo) for i in range(3)]
    bias = [place.bias(512, 2, oo[h], place.base) for h in (0, 1)]
    es, t, o = attend(q2, k2, v2, bias)
    e2[0], e2[1] = es
    m2[...] = t
    merge(top, num, den, t, o, 0, oo)


def merge(top, num, den, t, o, pair, oo):
    old = pick(reader(top), pair, oo)
    new = jnp.maximum(old, t)
    a, b = jnp.exp(old - new), jnp.exp(t - new)
    n = pick(reader(num), pair, oo) * a + o[:, :128] * b
    d = pick(reader(den), pair, oo) * a + o[:, 128:] * b
    put(reader(top), writer(top), new, pair, oo, False)
    put(reader(num), writer(num), n, pair, oo, False)
    put(reader(den), writer(den), d, pair, oo, False)


def far_body(
    info, offsets, counts, x, r4, r8, r12, top_in, num_in, den_in,
    top, norm, delta, acc, mx0, mx1, mx2, mx3, d4, d8, d12, num, den,
):
    place = Place(info, offsets, counts)
    top[...] = top_in[...]
    num[...] = num_in[...]
    den[...] = den_in[...]
    o3, o4 = place.offs(1), place.offs(2)
    q3, k3, v3 = [pick(reader(x, i), 1, o3) for i in range(3)]
    q4, k4, v4 = [pick(reader(x, i), 2, o4) for i in range(3)]
    k3, v3 = [jnp.concatenate([own, r4[i, 0:256]], axis=0) for i, own in enumerate((k3, v3))]
    k4, v4 = [
        jnp.concatenate([own, r4[i, 256:384], r8[i], r12[i]], axis=0) for i, own in enumerate((k4, v4))
    ]
    at = [(place.quarter ^ i) * 1024 for i in range(4)]
    b3 = [jnp.concatenate([place.bias(256, 4, o3[h], at[i]) for i in (0, 1)], axis=1) for h in (0, 1)]
    b4 = [jnp.concatenate([place.bias(128, 8, o4[h], at[i]) for i in range(4)], axis=1) for h in (0, 1)]
    es3, t3, out3 = attend(q3, k3, v3, b3)
    es4, t4, out4 = attend(q4, k4, v4, b4)
    merge(top, num, den, t3, out3, 1, o3)
    merge(top, num, den, t4, out4, 2, o4)
    ri = lax.broadcasted_iota(jnp.int32, (128, 128), 0) >> 6
    ci = lax.broadcasted_iota(jnp.int32, (128, 128), 1) >> 6
    same = jnp.where(ri == ci, 1.0, 0.0)
    for res in range(8):
        ok = place.valid(res)
        scale = ok / (den[res] + 1.0 - ok)
        norm[res] = scale
        mixed = (num[res] * scale).astype(bf16)
        for slot, mx in enumerate((mx0, mx1, mx2, mx3)):
            mx[res * 32 : res * 32 + 32] = mixed[slot * 32 : slot * 32 + 32]
        prod = x[3, res].astype(f32) * mixed.astype(f32)
        delta[res] = lax.dot_general(
            prod, same, (((1,), (0,)), ((), ())), precision=lax.Precision.HIGHEST, preferred_element_type=f32
        )
    acc[...] = jnp.zeros_like(acc)
    for pair, oo, q2, k2, v2, t, es, parts in (
        (1, o3, q3, k3, v3, t3, es3, ((d4, 0, 256),)),
        (2, o4, q4, k4, v4, t4, es4, ((d4, 256, 128), (d8, 0, 128), (d12, 0, 128))),
    ):
        f2 = jnp.exp(t - pick(reader(top), pair, oo)) * pick(reader(norm), pair, oo)
        gf2 = (pick(reader(x, 3), pair, oo).astype(f32) * f2).astype(bf16)
        fd2 = f2 * pick(reader(delta), pair, oo)
        grads = back(q2, k2, v2, gf2, fd2, es)
        for i in range(3):
            own = grads[i][: q2.shape[0]]
            put(reader(acc, i), writer(acc, i), own, pair, oo, True)
        at_row = q2.shape[0]
        for ref, start, rows in parts:
            for i in (0, 1):
                ref[i, start : start + rows] = grads[i + 1][at_row : at_row + rows].astype(bf16)
            at_row += rows


def near_back_body(info, offsets, counts, x, top, norm, delta, acc_in, m1, m2, e1, e2, acc):
    place = Place(info, offsets, counts)
    for slot in range(4):
        sl = slice(slot * 32, slot * 32 + 32)
        f2 = jnp.exp(slot_rows(m1, slot) - slot_rows(top, slot)) * slot_rows(norm, slot)
        q2, k2, v2, g2 = [slot_rows(x, slot, i) for i in range(4)]
        gf2 = (g2.astype(f32) * f2).astype(bf16)
        fd2 = f2 * slot_rows(delta, slot)
        grads = back(q2, k2, v2, gf2, fd2, [e1[slot, 0], e1[slot, 1]])
        for i in range(3):
            acc[i, :, sl, :] = acc_in[i, :, sl, :] + grads[i].reshape(8, 32, 128)
    oo = place.offs(0)
    q2, k2, v2, g2 = [pick(reader(x, i), 0, oo) for i in range(4)]
    f2 = jnp.exp(m2[...] - pick(reader(top), 0, oo)) * pick(reader(norm), 0, oo)
    gf2 = (g2.astype(f32) * f2).astype(bf16)
    fd2 = f2 * pick(reader(delta), 0, oo)
    grads = back(q2, k2, v2, gf2, fd2, [e2[0], e2[1]])
    for i in range(3):
        put(reader(acc, i), writer(acc, i), grads[i], 0, oo, True)


def finish_body(info, offsets, counts, acc_in, r4, r8, r12, o0, o1, o2, o3, acc):
    place = Place(info, offsets, counts)
    acc[...] = acc_in[...]
    p3, p4 = place.offs(1), place.offs(2)
    for i in (0, 1):
        rd, wr = reader(acc, i + 1), writer(acc, i + 1)
        put(rd, wr, r4[i, 0:256].astype(f32), 1, p3, True)
        far = r4[i, 256:384].astype(f32) + r8[i].astype(f32) + r12[i].astype(f32)
        put(rd, wr, far, 2, p4, True)
    for slot, o in enumerate((o0, o1, o2, o3)):
        o[0] = (slot_rows(acc, slot, 0) * 0.125).astype(bf16)
        o[1] = slot_rows(acc, slot, 1).astype(bf16)
        o[2] = slot_rows(acc, slot, 2).astype(bf16)


def home_body(info, m0, m1, m2, m3, dq, dk, dv, wide):
    order = row_order(True)
    for d, m in enumerate((m0, m1, m2, m3)):
        c = pl.multiple_of((info[1] ^ d) * 128, 128)
        for i in range(3):
            wide[i, :, pl.ds(c, 128)] = m[i]
    for i, o in enumerate((dq, dk, dv)):
        o[...] = dot_nn(order, wide[i, :, 0:384]).astype(bf16)


def project_body(info, m0, m1, m2, m3, og, w, attended, send, keep, wide):
    order = row_order(True)
    for d, m in enumerate((m0, m1, m2, m3)):
        c = pl.multiple_of((info[1] ^ d) * 128, 128)
        wide[:, pl.ds(c, 128)] = m[...]
    mixed = dot_nn(order, wide[:, 0:384]).astype(bf16)
    there = pl.multiple_of((1 - info[2]) * 384, 128)
    here = pl.multiple_of(info[2] * 384, 128)
    send[...] = dot_tn(mixed, og[:, pl.ds(there, 384)]).astype(bf16)
    keep[...] = dot_tn(mixed, og[:, pl.ds(here, 384)])
    attended[...] = dot_nn(mixed, w[...]).astype(bf16)


smem = pl.BlockSpec(memory_space=pltpu.SMEM)
vmem = pl.BlockSpec(memory_space=pltpu.VMEM)


def call(body, scalars, arrays, outs, scratch=(), flops=0):
    shapes = [jax.ShapeDtypeStruct(s, t) for s, t in outs]
    moved = sum(a.size * a.dtype.itemsize for a in arrays) + sum(s.size * s.dtype.itemsize for s in shapes)
    return pl.pallas_call(
        body,
        out_shape=shapes,
        in_specs=[smem] * len(scalars) + [vmem] * len(arrays),
        out_specs=[vmem] * len(shapes),
        scratch_shapes=[pltpu.VMEM(s, t) for s, t in scratch],
        compiler_params=pltpu.CompilerParams(vmem_limit_bytes=48 * 1024 * 1024),
        cost_estimate=pl.CostEstimate(flops=flops, bytes_accessed=moved, transcendentals=0),
    )(*scalars, *arrays)


def routes(seq_step, keep=None):
    pairs = []
    for dp in range(16):
        for s in range(16):
            t = s ^ seq_step
            if keep is not None and (keep(s, t) & 3) ^ (3 * (dp & 1)) == 3:
                continue
            pairs.append((dp * 16 + s, dp * 16 + t))
    return pairs


def shift(block, pairs):
    return lax.ppermute(block, ("dp", "seq"), pairs)


def dp_step(block, step):
    return lax.ppermute(block, "dp", [(i, i ^ step) for i in range(16)])


def seq_step(block, step):
    return lax.ppermute(block, "seq", [(i, i ^ step) for i in range(16)])


def per_device(queries, keys, values, out_weight, out_grad, offsets, counts):
    seq_rank = lax.axis_index("seq").astype(jnp.int32)
    core = lax.axis_index("dp").astype(jnp.int32) & 1
    info = jnp.stack([seq_rank, (seq_rank & 3) ^ (3 * core), core])
    places = [info, offsets, counts]

    chunk = ((4, 256, 128), bf16)
    msgs = call(
        prep_body,
        [info],
        [queries[0], keys[0], values[0], out_grad[0], out_weight],
        [chunk] * 4,
        [((4, 256, 384), bf16)],
    )
    got = [msgs[0]] + [shift(msgs[d], routes(d, lambda s, t: t)) for d in (1, 2, 3)]
    cube = (8, 128, 128)
    x, s4, s8 = call(
        collect_body, places, got, [((4, *cube), bf16), ((2, 384, 128), bf16), ((2, 128, 128), bf16)]
    )
    active = lambda s, t: s
    r4, r8, r12 = [shift(b, routes(d, active)) for b, d in ((s4, 4), (s8, 8), (s8, 12))]
    top, num, den, m1, m2, e1, e2 = call(
        near_body,
        places,
        [x],
        [(cube, f32)] * 4 + [((512, 128), f32), ((4, 2, 256, 256), bf16), ((2, 512, 512), bf16)],
        flops=10**9,
    )
    top, norm, delta, acc, mx0, mx1, mx2, mx3, d4, d8, d12 = call(
        far_body,
        places,
        [x, r4, r8, r12, top, num, den],
        [(cube, f32)] * 3
        + [((3, *cube), f32)]
        + [((256, 128), bf16)] * 4
        + [((2, 384, 128), bf16), ((2, 128, 128), bf16), ((2, 128, 128), bf16)],
        [(cube, f32)] * 2,
        flops=10**9,
    )
    mixed = [mx0] + [shift(b, routes(d, active)) for d, b in ((1, mx1), (2, mx2), (3, mx3))]
    b4, b8, b12 = [shift(b, routes(d, active)) for b, d in ((d4, 4), (d8, 8), (d12, 12))]
    (acc,) = call(
        near_back_body,
        places,
        [x, top, norm, delta, acc, m1, m2, e1, e2],
        [((3, *cube), f32)],
        flops=2 * 10**9,
    )
    attended, send, keep = call(
        project_body,
        [info],
        mixed + [out_grad[0], out_weight],
        [((256, 768), bf16), ((384, 384), bf16), ((384, 384), f32)],
        [((256, 512), bf16)],
        flops=3 * 10**8,
    )
    back_msgs = call(
        finish_body, places, [acc, b4, b8, b12], [((3, 256, 128), bf16)] * 4, [((3, *cube), f32)]
    )
    home = [back_msgs[0]] + [shift(back_msgs[d], routes(d, active)) for d in (1, 2, 3)]
    grads = call(home_body, [info], home, [((256, 384), bf16)] * 3, [((3, 256, 512), bf16)])

    part = keep + dp_step(send, 1)
    rows = part.reshape(16, 24, 384)
    rest = rows
    for bit in (0, 1, 2, 3):
        pairs_view = rest.reshape(rest.shape[0] // 2, 2, 24, 384)
        upper = ((seq_rank >> bit) & 1) == 1
        stay = jnp.where(upper, pairs_view[:, 1], pairs_view[:, 0])
        leave = jnp.where(upper, pairs_view[:, 0], pairs_view[:, 1]).astype(bf16)
        rest = stay + seq_step(leave, 1 << bit).astype(f32)
    total = rest[0]
    for step in (2, 4, 8):
        low = total.astype(bf16)
        total = low.astype(f32) + dp_step(low, step).astype(f32)
    other = dp_step(total, 1)
    grad_weight = jnp.concatenate(
        [jnp.where(core == 0, total, other), jnp.where(core == 0, other, total)], axis=1
    )
    return (attended[None], grads[0][None], grads[1][None], grads[2][None], grad_weight)


def solution(mesh):
    tiles = P("dp", "seq", None)
    return jax.shard_map(
        per_device,
        mesh=mesh,
        in_specs=(tiles, tiles, tiles, P(), tiles, P(), P("dp")),
        out_specs=(tiles, tiles, tiles, tiles, P("seq", None)),
        check_vma=False,
    )
```

```python
import jax
import jax.numpy as jnp
from jax import lax
from jax.experimental import pallas as pl
from jax.experimental.pallas import tpu as pltpu
from jax.sharding import PartitionSpec as P

bf16 = jnp.bfloat16
f32 = jnp.float32
low_bias = -1e30


def dot_nn(a, b):
    return lax.dot_general(a, b, (((1,), (0,)), ((), ())), preferred_element_type=f32)


def dot_nt(a, b):
    return lax.dot_general(a, b, (((1,), (1,)), ((), ())), preferred_element_type=f32)


def dot_tn(a, b):
    return lax.dot_general(a, b, (((0,), (0,)), ((), ())), preferred_element_type=f32)


def first_half(rows):
    return lax.broadcasted_iota(jnp.int32, (rows, 128), 1) < 64


def half_of(x, h):
    m = first_half(x.shape[0])
    z = jnp.zeros_like(x)
    return jnp.where(m, x, z) if h == 0 else jnp.where(m, z, x)


def row_order(back):
    a = lax.broadcasted_iota(jnp.int32, (256, 256), 0 if not back else 1)
    b = lax.broadcasted_iota(jnp.int32, (256, 256), 1 if not back else 0)
    return jnp.where(b == (a & 31) * 8 + (a >> 5), 1.0, 0.0).astype(bf16)


class Place:
    def __init__(self, info, offsets, counts):
        self.j = info[0] & 3
        self.base = (info[0] >> 2) * 1024
        self.quarter = info[0] >> 2
        self.chunk = jnp.minimum(info[1], 2)
        self.count = counts[0]
        self.offsets = offsets

    def offs(self, pair):
        r = 2 << pair
        return [self.offsets[pair, 2 * self.chunk + h] & (r - 1) for h in (0, 1)]

    def bias(self, n, step, o, base):
        kk = lax.broadcasted_iota(jnp.int32, (1, n), 1)
        pos = base + ((self.j ^ ((kk >> 5) & 3)) << 8) + (kk & 31) * 8 + o + step * (kk >> 7)
        return jnp.where(pos < self.count, 0.0, low_bias)

    def bias_slot(self, slot):
        kk = lax.broadcasted_iota(jnp.int32, (1, 256), 1)
        pos = self.base + ((self.j ^ slot) << 8) + (kk & 31) * 8 + (kk >> 5)
        return jnp.where(pos < self.count, 0.0, low_bias)

    def valid(self, res):
        rr = lax.broadcasted_iota(jnp.int32, (128, 128), 0)
        pos = self.base + ((self.j ^ (rr >> 5)) << 8) + (rr & 31) * 8 + res
        return jnp.where(pos < self.count, 1.0, 0.0)


def pick(read, pair, oo):
    r = 2 << pair
    m = first_half(128)
    parts = [jnp.where(m, read(oo[0] + r * i), read(oo[1] + r * i)) for i in range(8 // r)]
    return parts[0] if len(parts) == 1 else jnp.concatenate(parts, axis=0)


def put(read, write, val, pair, oo, add):
    r = 2 << pair
    m = first_half(128)
    for i in range(8 // r):
        blk = val[i * 128 : (i + 1) * 128]
        for h in (0, 1):
            mine = m if h == 0 else ~m
            old = read(oo[h] + r * i)
            write(oo[h] + r * i, jnp.where(mine, old + blk if add else blk, old))


def reader(ref, *lead):
    return lambda i: ref[(*lead, i)]


def writer(ref, *lead):
    def w(i, val):
        ref[(*lead, i)] = val

    return w


def slot_rows(ref, slot, *lead):
    return ref[(*lead, slice(None), slice(slot * 32, slot * 32 + 32), slice(None))].reshape(256, 128)


def attend(q2, k2, v2, bias):
    nk = k2.shape[0]
    out, es, ms = None, [], []
    one = jnp.ones((nk, 128), bf16)
    for h in (0, 1):
        s = dot_nt(q2, half_of(k2, h)) + bias[h]
        m = jnp.max(s, axis=1, keepdims=True)
        e = jnp.exp(s - m).astype(bf16)
        o = dot_nn(e, jnp.concatenate([half_of(v2, h), half_of(one, h)], axis=1))
        out = o if out is None else out + o
        es.append(e)
        ms.append(m)
    n = q2.shape[0]
    top = jnp.where(first_half(n), jnp.broadcast_to(ms[0], (n, 128)), jnp.broadcast_to(ms[1], (n, 128)))
    return es, top, out


def back(q2, k2, v2, gf2, fd2, es):
    dq = dk = dv = None
    for h in (0, 1):
        kh, vh = half_of(k2, h), half_of(v2, h)
        e = es[h]
        dp = dot_nt(gf2, vh)
        ds = (e.astype(f32) * (dp - fd2[:, 64 * h : 64 * h + 1])).astype(bf16)
        a, b, c = dot_nn(ds, kh), dot_tn(ds, half_of(q2, h)), dot_tn(e, half_of(gf2, h))
        dq, dk, dv = (a, b, c) if dq is None else (dq + a, dk + b, dv + c)
    return dq, dk, dv


def copies(pairs, sems):
    moves = [pltpu.make_async_copy(src, dst, sems.at[i]) for i, (src, dst) in enumerate(pairs)]
    for m in moves:
        m.start()
    return moves


def prep_body(
    info, q_in, k_in, v_in, og_in, w_in, o0, o1, o2, o3, og_out, px, q, k, v, og, w, sems
):
    moves = copies(((og_in, og), (w_in, w), (q_in, q), (k_in, k), (v_in, v)), sems)
    order = row_order(False)
    moves[0].wait()
    ordered = dot_nn(order, og[...]).astype(bf16)
    og_out[...] = ordered
    moves[1].wait()
    px[1] = dot_nt(ordered, w[...]).astype(bf16)
    moves[2].wait()
    px[0] = (dot_nn(order, q[...]) * 0.125).astype(bf16)
    moves[3].wait()
    px[2] = dot_nn(order, k[...]).astype(bf16)
    moves[4].wait()
    px[3] = dot_nn(order, v[...]).astype(bf16)
    for d, o in enumerate((o0, o1, o2, o3)):
        c = pl.multiple_of(jnp.minimum(info[1] ^ d, 2) * 128, 128)
        for i in range(4):
            o[i] = px[i, :, pl.ds(c, 128)]


def collect_body(info, offsets, counts, m0, m1, m2, m3, qg, kv, s4, s8):
    place = Place(info, offsets, counts)
    for slot, m in enumerate((m0, m1, m2, m3)):
        for i in range(4):
            x = (qg, kv)[i // 2]
            x[i % 2, :, slot * 32 : slot * 32 + 32, :] = m[i].reshape(8, 32, 128)
    o3, o4 = place.offs(1), place.offs(2)
    for i in (0, 1):
        s4[i, 0:256] = pick(reader(kv, i), 1, o3)
        last = pick(reader(kv, i), 2, o4)
        s4[i, 256:384] = last
        s8[i] = last


def near_body(
    info, offsets, counts, qg, kv, top, num, den, m1, m2, e1, e2,
):
    place = Place(info, offsets, counts)
    for slot in range(4):
        b = place.bias_slot(slot)
        sl = slice(slot * 32, slot * 32 + 32)
        es, t, o = attend(slot_rows(qg, slot, 0), slot_rows(kv, slot, 0), slot_rows(kv, slot, 1), [b, b])
        e1[slot, 0], e1[slot, 1] = es
        t = t.reshape(8, 32, 128)
        top[:, sl, :] = t
        m1[:, sl, :] = t
        num[:, sl, :] = o[:, :128].reshape(8, 32, 128)
        den[:, sl, :] = o[:, 128:].reshape(8, 32, 128)
    oo = place.offs(0)
    q2, k2, v2 = [pick(r, 0, oo) for r in (reader(qg, 0), reader(kv, 0), reader(kv, 1))]
    bias = [place.bias(512, 2, oo[h], place.base) for h in (0, 1)]
    es, t, o = attend(q2, k2, v2, bias)
    e2[0], e2[1] = es
    m2[...] = t
    merge(top, num, den, t, o, 0, oo)


def merge(top, num, den, t, o, pair, oo):
    old = pick(reader(top), pair, oo)
    new = jnp.maximum(old, t)
    a, b = jnp.exp(old - new), jnp.exp(t - new)
    n = pick(reader(num), pair, oo) * a + o[:, :128] * b
    d = pick(reader(den), pair, oo) * a + o[:, 128:] * b
    put(reader(top), writer(top), new, pair, oo, False)
    put(reader(num), writer(num), n, pair, oo, False)
    put(reader(den), writer(den), d, pair, oo, False)


def far_keys(place, kv, r4, r8, r12):
    o3, o4 = place.offs(1), place.offs(2)
    k3, v3 = [jnp.concatenate([pick(reader(kv, i), 1, o3), r4[i, 0:256]], axis=0) for i in (0, 1)]
    k4, v4 = [
        jnp.concatenate([pick(reader(kv, i), 2, o4), r4[i, 256:384], r8[i], r12[i]], axis=0) for i in (0, 1)
    ]
    return o3, o4, k3, v3, k4, v4


def far_body(
    info, offsets, counts, kv, qg, r4, r8, r12, top_in, num_in, den_in,
    top, norm, delta, mx0, mx1, mx2, mx3, m3, m4, e3, e4, num, den,
):
    place = Place(info, offsets, counts)
    top[...] = top_in[...]
    num[...] = num_in[...]
    den[...] = den_in[...]
    o3, o4, k3, v3, k4, v4 = far_keys(place, kv, r4, r8, r12)
    at = [(place.quarter ^ i) * 1024 for i in range(4)]
    b3 = [jnp.concatenate([place.bias(256, 4, o3[h], at[i]) for i in (0, 1)], axis=1) for h in (0, 1)]
    b4 = [jnp.concatenate([place.bias(128, 8, o4[h], at[i]) for i in range(4)], axis=1) for h in (0, 1)]
    for pair, oo, k2, v2, b, m, e in ((1, o3, k3, v3, b3, m3, e3), (2, o4, k4, v4, b4, m4, e4)):
        es, t, out = attend(pick(reader(qg, 0), pair, oo), k2, v2, b)
        e[0], e[1] = es
        m[...] = t
        merge(top, num, den, t, out, pair, oo)
    ri = lax.broadcasted_iota(jnp.int32, (128, 128), 0) >> 6
    ci = lax.broadcasted_iota(jnp.int32, (128, 128), 1) >> 6
    same = jnp.where(ri == ci, 1.0, 0.0)
    for res in range(8):
        ok = place.valid(res)
        scale = ok / (den[res] + 1.0 - ok)
        norm[res] = scale
        mixed = (num[res] * scale).astype(bf16)
        for slot, mx in enumerate((mx0, mx1, mx2, mx3)):
            mx[res * 32 : res * 32 + 32] = mixed[slot * 32 : slot * 32 + 32]
        prod = qg[1, res].astype(f32) * mixed.astype(f32)
        delta[res] = lax.dot_general(
            prod, same, (((1,), (0,)), ((), ())), precision=lax.Precision.HIGHEST, preferred_element_type=f32
        )


def pair_back(place, kv, qg, top, norm, delta, t, es, pair, oo, k2, v2):
    f2 = jnp.exp(t - pick(reader(top), pair, oo)) * pick(reader(norm), pair, oo)
    gf2 = (pick(reader(qg, 1), pair, oo).astype(f32) * f2).astype(bf16)
    fd2 = f2 * pick(reader(delta), pair, oo)
    return back(pick(reader(qg, 0), pair, oo), k2, v2, gf2, fd2, es)


def far_back_body(
    info, offsets, counts, kv, qg, r4, r8, r12, top, norm, delta, m3, m4, e3, e4,
    acc, d4, d8, d12,
):
    place = Place(info, offsets, counts)
    o3, o4, k3, v3, k4, v4 = far_keys(place, kv, r4, r8, r12)
    acc[...] = jnp.zeros_like(acc)
    for pair, oo, k2, v2, m, e, parts in (
        (1, o3, k3, v3, m3, e3, ((d4, 0, 256),)),
        (2, o4, k4, v4, m4, e4, ((d4, 256, 128), (d8, 0, 128), (d12, 0, 128))),
    ):
        grads = pair_back(place, kv, qg, top, norm, delta, m[...], [e[0], e[1]], pair, oo, k2, v2)
        at_row = m.shape[0]
        for i in range(3):
            put(reader(acc, i), writer(acc, i), grads[i][:at_row], pair, oo, True)
        for ref, start, rows in parts:
            for i in (0, 1):
                ref[i, start : start + rows] = grads[i + 1][at_row : at_row + rows].astype(bf16)
            at_row += rows


def back_two_body(info, offsets, counts, kv, qg, top, norm, delta, acc_in, m2, e2, acc):
    place = Place(info, offsets, counts)
    acc[...] = acc_in[...]
    oo = place.offs(0)
    k2, v2 = pick(reader(kv, 0), 0, oo), pick(reader(kv, 1), 0, oo)
    grads = pair_back(place, kv, qg, top, norm, delta, m2[...], [e2[0], e2[1]], 0, oo, k2, v2)
    for i in range(3):
        put(reader(acc, i), writer(acc, i), grads[i], 0, oo, True)


def back_one_body(info, offsets, counts, kv, qg, top, norm, delta, acc_in, m1, e1, acc):
    for slot in range(4):
        sl = slice(slot * 32, slot * 32 + 32)
        f2 = jnp.exp(slot_rows(m1, slot) - slot_rows(top, slot)) * slot_rows(norm, slot)
        q2, k2, v2, g2 = [slot_rows(r, slot, i) for r, i in ((qg, 0), (kv, 0), (kv, 1), (qg, 1))]
        gf2 = (g2.astype(f32) * f2).astype(bf16)
        fd2 = f2 * slot_rows(delta, slot)
        grads = back(q2, k2, v2, gf2, fd2, [e1[slot, 0], e1[slot, 1]])
        for i in range(3):
            acc[i, :, sl, :] = acc_in[i, :, sl, :] + grads[i].reshape(8, 32, 128)


def cores_body(keep, got, d4, d8, d12, own, f4, f8, f12):
    for u, (d, f) in enumerate(((None, own), (d4, f4), (d8, f8), (d12, f12))):
        part = keep[4 * u : 4 * u + 4] + got[4 * u : 4 * u + 4].astype(f32)
        if u == 0:
            f[...] = part
        else:
            n = d.shape[1]
            f[0:n] = d[0]
            f[n : 2 * n] = d[1]
            f[2 * n : 2 * n + 288] = part.reshape(288, 128).astype(bf16)


def finish_body(info, offsets, counts, acc_in, r4, r8, r12, part, own, o0, o1, o2, o3, acc):
    place = Place(info, offsets, counts)
    acc[...] = acc_in[...]
    p3, p4 = place.offs(1), place.offs(2)
    for i in (0, 1):
        rd, wr = reader(acc, i + 1), writer(acc, i + 1)
        put(rd, wr, r4[i * 384 : i * 384 + 256].astype(f32), 1, p3, True)
        far = r4[i * 384 + 256 : i * 384 + 384].astype(f32)
        far = far + r8[i * 128 : i * 128 + 128].astype(f32) + r12[i * 128 : i * 128 + 128].astype(f32)
        put(rd, wr, far, 2, p4, True)
    grads = [r[n : n + 288].astype(f32).reshape(4, 72, 128) for r, n in ((r4, 768), (r8, 256), (r12, 256))]
    total = part[...] + grads[0] + (grads[1] + grads[2])
    own[...] = total[0]
    for slot, o in enumerate((o0, o1, o2, o3)):
        o[0:256] = (slot_rows(acc, slot, 0) * 0.125).astype(bf16)
        o[256:512] = slot_rows(acc, slot, 1).astype(bf16)
        o[512:768] = slot_rows(acc, slot, 2).astype(bf16)
        o[768:848] = jnp.concatenate([total[slot], jnp.zeros((8, 128), f32)], axis=0).astype(bf16)


def home_body(info, m0, m1, m2, m3, dq, dk, dv, wide):
    order = row_order(True)
    for d, m in enumerate((m0, m1, m2, m3)):
        c = pl.multiple_of((info[1] ^ d) * 128, 128)
        for i in range(3):
            wide[i, :, pl.ds(c, 128)] = m[256 * i : 256 * i + 256]
    for i, o in enumerate((dq, dk, dv)):
        o[...] = dot_nn(order, wide[i, :, 0:384]).astype(bf16)


def near_sum_body(own, m1, m2, m3, o):
    a, b, c = [m[768:848].astype(f32)[0:72] for m in (m1, m2, m3)]
    o[...] = (own[...] + a + (b + c)).astype(bf16)


def widen(info, msgs, wide):
    for d, m in enumerate(msgs):
        wide[:, pl.ds(pl.multiple_of((info[1] ^ d) * 128, 128), 128)] = m[...]


def project_body(info, m0, m1, m2, m3, og, send, keep, wide, both, away):
    widen(info, (m0, m1, m2, m3), wide)
    both[...] = dot_tn(wide[:, 0:384], og[...])
    for s in range(16):
        for t in range(3):
            at = slice(t * 24, t * 24 + 24)
            there = pl.multiple_of((1 - info[2]) * 384 + t * 128, 128)
            here = pl.multiple_of(info[2] * 384 + t * 128, 128)
            away[s ^ info[0], at] = both[s * 24 : s * 24 + 24, pl.ds(there, 128)]
            keep[s ^ info[0], at] = both[s * 24 : s * 24 + 24, pl.ds(here, 128)]
    send[...] = away[...].astype(bf16)


def attended_body(info, m0, m1, m2, m3, w, o, wide):
    widen(info, (m0, m1, m2, m3), wide)
    mixed = dot_nn(row_order(True), wide[:, 0:384]).astype(bf16)
    o[...] = dot_nn(mixed, w[...]).astype(bf16)


def sum_body(a, b, c, d, o):
    one = a[...].astype(f32) + b[...].astype(f32)
    o[...] = (one + (c[...].astype(f32) + d[...].astype(f32))).astype(o.dtype)


def pair_body(a, b, o):
    o[...] = (a[...].astype(f32) + b[...].astype(f32)).astype(o.dtype)


def join_body(info, a, b, o):
    for t in range(3):
        at = slice(t * 24, t * 24 + 24)
        o[:, pl.ds(pl.multiple_of(info[2] * 384 + t * 128, 128), 128)] = a[at]
        o[:, pl.ds(pl.multiple_of((1 - info[2]) * 384 + t * 128, 128), 128)] = b[at]


smem = pl.BlockSpec(memory_space=pltpu.SMEM)
vmem = pl.BlockSpec(memory_space=pltpu.VMEM)
hbm = pl.BlockSpec(memory_space=pltpu.HBM)


def call(body, scalars, arrays, outs, scratch=(), flops=0, space=vmem, sems=0, limit=12):
    shapes = [jax.ShapeDtypeStruct(s, t) for s, t in outs]
    moved = sum(a.size * a.dtype.itemsize for a in arrays) + sum(s.size * s.dtype.itemsize for s in shapes)
    return pl.pallas_call(
        body,
        out_shape=shapes,
        in_specs=[smem] * len(scalars) + [space] * len(arrays),
        out_specs=[vmem] * len(shapes),
        scratch_shapes=[pltpu.VMEM(s, t) for s, t in scratch] + [pltpu.SemaphoreType.DMA((sems,))] * (sems > 0),
        compiler_params=pltpu.CompilerParams(vmem_limit_bytes=limit * 1024 * 1024),
        cost_estimate=pl.CostEstimate(flops=flops, bytes_accessed=moved, transcendentals=0),
    )(*scalars, *arrays)


def routes(seq_step, keep=None):
    pairs = []
    for dp in range(16):
        for s in range(16):
            t = s ^ seq_step
            if keep is not None and (keep(s, t) & 3) ^ (3 * (dp & 1)) == 3:
                continue
            pairs.append((dp * 16 + s, dp * 16 + t))
    return pairs


def shift(block, pairs):
    return lax.ppermute(block, ("dp", "seq"), pairs)


def dp_step(block, step):
    return lax.ppermute(block, "dp", [(i, i ^ step) for i in range(16)])


def seq_step(block, step):
    return lax.ppermute(block, "seq", [(i, i ^ step) for i in range(16)])


def per_device(queries, keys, values, out_weight, out_grad, offsets, counts):
    seq_rank = lax.axis_index("seq").astype(jnp.int32)
    core = lax.axis_index("dp").astype(jnp.int32) & 1
    info = jnp.stack([seq_rank, (seq_rank & 3) ^ (3 * core), core])
    places = [info, offsets, counts]

    chunk = ((4, 256, 128), bf16)
    third = ((256, 384), bf16)
    cube = (8, 128, 128)
    block = (72, 128)
    active = lambda s, t: s

    *msgs, og = call(
        prep_body,
        [info],
        [queries[0], keys[0], values[0], out_grad[0], out_weight],
        [chunk] * 4 + [((256, 768), bf16)],
        [((4, 256, 384), bf16), third, third, third, ((256, 768), bf16), ((384, 768), bf16)],
        space=hbm,
        sems=5,
        limit=60,
    )
    got = [msgs[0]] + [shift(msgs[d], routes(d, lambda s, t: t)) for d in (1, 2, 3)]
    qg, kv, s4, s8 = call(
        collect_body,
        places,
        got,
        [((2, *cube), bf16)] * 2 + [((2, 384, 128), bf16), ((2, 128, 128), bf16)],
    )
    r4 = shift(s4, routes(4, active))
    top, num, den, m1, m2, e1, e2 = call(
        near_body,
        places,
        [qg, kv],
        [(cube, f32)] * 4 + [((512, 128), f32), ((4, 2, 256, 256), bf16), ((2, 512, 512), bf16)],
        flops=10**9,
    )
    s8, top = lax.optimization_barrier((s8, top))
    r8, r12 = [shift(s8, routes(d, active)) for d in (8, 12)]
    top, norm, delta, mx0, mx1, mx2, mx3, m3, m4, e3, e4 = call(
        far_body,
        places,
        [kv, qg, r4, r8, r12, top, num, den],
        [(cube, f32)] * 3
        + [((256, 128), bf16)] * 4
        + [((256, 128), f32), ((128, 128), f32), ((2, 256, 512), bf16), ((2, 128, 512), bf16)],
        [(cube, f32)] * 2,
        flops=10**9,
    )
    mixed = [mx0] + [shift(b, routes(d, active)) for d, b in ((1, mx1), (2, mx2), (3, mx3))]
    state = [kv, qg, top, norm, delta]
    acc, d4, d8, d12 = call(
        far_back_body,
        places,
        [kv, qg, r4, r8, r12, top, norm, delta, m3, m4, e3, e4],
        [((3, *cube), f32), ((2, 384, 128), bf16), ((2, 128, 128), bf16), ((2, 128, 128), bf16)],
        flops=10**9,
    )
    acc, *mixed = lax.optimization_barrier([acc] + mixed)
    send, keep = call(
        project_body,
        [info],
        mixed + [og],
        [((16, *block), bf16), ((16, *block), f32)],
        [((256, 512), bf16), ((384, 768), f32), ((16, *block), f32)],
        flops=3 * 10**8,
    )
    arrived = dp_step(send, 1)
    acc, keep = lax.optimization_barrier((acc, keep))
    (acc,) = call(back_two_body, places, state + [acc, m2, e2], [((3, *cube), f32)], flops=10**9)
    acc, keep = lax.optimization_barrier((acc, keep))
    part, f4, f8, f12 = call(
        cores_body,
        [],
        [keep, arrived, d4, d8, d12],
        [((4, *block), f32), ((1056, 128), bf16), ((544, 128), bf16), ((544, 128), bf16)],
    )
    f4, f8, f12 = [shift(b, routes(d)) for d, b in ((4, f4), (8, f8), (12, f12))]
    acc, part, *mixed = lax.optimization_barrier([acc, part] + mixed)
    (attended,) = call(
        attended_body, [info], mixed + [out_weight], [((256, 768), bf16)], [((256, 512), bf16)], flops=3 * 10**8
    )
    (acc,) = call(back_one_body, places, state + [acc, m1, e1], [((3, *cube), f32)], flops=10**9)
    own, *outs = call(
        finish_body,
        places,
        [acc, f4, f8, f12, part],
        [(block, f32)] + [((848, 128), bf16)] * 4,
        [((3, *cube), f32)],
    )
    home = [outs[0]] + [shift(outs[d], routes(d)) for d in (1, 2, 3)]
    (own,) = call(near_sum_body, [], [own] + home[1:], [(block, bf16)])
    arrived = dp_step(own, 2)
    home = lax.optimization_barrier([own] + home)[1:]
    grads = call(home_body, [info], home, [third] * 3, [((3, 256, 512), bf16)])
    (own,) = call(pair_body, [], [own, arrived], [(block, bf16)])
    rest = [dp_step(own, d) for d in (4, 8, 12)]
    (own,) = call(sum_body, [], [own] + rest, [(block, f32)])
    (grad_weight,) = call(join_body, [info], [own, dp_step(own, 1)], [((24, 768), f32)])
    return (attended[None], grads[0][None], grads[1][None], grads[2][None], grad_weight)


def solution(mesh):
    tiles = P("dp", "seq", None)
    return jax.shard_map(
        per_device,
        mesh=mesh,
        in_specs=(tiles, tiles, tiles, P(), tiles, P(), P("dp")),
        out_specs=(tiles, tiles, tiles, tiles, P("seq", None)),
        check_vma=False,
    )
```

```python
import jax
import jax.numpy as jnp
from jax import lax
from jax.experimental import pallas as pl
from jax.experimental.pallas import tpu as pltpu
from jax.sharding import PartitionSpec as P

bf16 = jnp.bfloat16
f32 = jnp.float32
low_bias = -1e30


def dot_nn(a, b):
    return lax.dot_general(a, b, (((1,), (0,)), ((), ())), preferred_element_type=f32)


def dot_nt(a, b):
    return lax.dot_general(a, b, (((1,), (1,)), ((), ())), preferred_element_type=f32)


def dot_tn(a, b):
    return lax.dot_general(a, b, (((0,), (0,)), ((), ())), preferred_element_type=f32)


def first_half(rows):
    return lax.broadcasted_iota(jnp.int32, (rows, 128), 1) < 64


def half_of(x, h):
    m = first_half(x.shape[0])
    z = jnp.zeros_like(x)
    return jnp.where(m, x, z) if h == 0 else jnp.where(m, z, x)


def row_order(back):
    a = lax.broadcasted_iota(jnp.int32, (256, 256), 0 if not back else 1)
    b = lax.broadcasted_iota(jnp.int32, (256, 256), 1 if not back else 0)
    return jnp.where(b == (a & 31) * 8 + (a >> 5), 1.0, 0.0).astype(bf16)


class Place:
    def __init__(self, info, offsets, counts):
        self.j = info[0] & 3
        self.base = (info[0] >> 2) * 1024
        self.quarter = info[0] >> 2
        self.chunk = jnp.minimum(info[1], 2)
        self.count = counts[0]
        self.offsets = offsets

    def offs(self, pair):
        r = 2 << pair
        return [self.offsets[pair, 2 * self.chunk + h] & (r - 1) for h in (0, 1)]

    def bias(self, n, step, o, base):
        kk = lax.broadcasted_iota(jnp.int32, (1, n), 1)
        pos = base + ((self.j ^ ((kk >> 5) & 3)) << 8) + (kk & 31) * 8 + o + step * (kk >> 7)
        return jnp.where(pos < self.count, 0.0, low_bias)

    def bias_slot(self, slot):
        kk = lax.broadcasted_iota(jnp.int32, (1, 256), 1)
        pos = self.base + ((self.j ^ slot) << 8) + (kk & 31) * 8 + (kk >> 5)
        return jnp.where(pos < self.count, 0.0, low_bias)

    def valid(self, res):
        rr = lax.broadcasted_iota(jnp.int32, (128, 128), 0)
        pos = self.base + ((self.j ^ (rr >> 5)) << 8) + (rr & 31) * 8 + res
        return jnp.where(pos < self.count, 1.0, 0.0)


def pick(read, pair, oo):
    r = 2 << pair
    m = first_half(128)
    parts = [jnp.where(m, read(oo[0] + r * i), read(oo[1] + r * i)) for i in range(8 // r)]
    return parts[0] if len(parts) == 1 else jnp.concatenate(parts, axis=0)


def put(read, write, val, pair, oo, add):
    r = 2 << pair
    m = first_half(128)
    for i in range(8 // r):
        blk = val[i * 128 : (i + 1) * 128]
        for h in (0, 1):
            mine = m if h == 0 else ~m
            old = read(oo[h] + r * i)
            write(oo[h] + r * i, jnp.where(mine, old + blk if add else blk, old))


def reader(ref, *lead):
    return lambda i: ref[(*lead, i)]


def writer(ref, *lead):
    def w(i, val):
        ref[(*lead, i)] = val

    return w


def slot_rows(ref, slot, *lead):
    return ref[(*lead, slice(None), slice(slot * 32, slot * 32 + 32), slice(None))].reshape(256, 128)


def attend(q2, k2, v2, bias):
    nk = k2.shape[0]
    out, es, ms = None, [], []
    one = jnp.ones((nk, 128), bf16)
    for h in (0, 1):
        s = dot_nt(q2, half_of(k2, h)) + bias[h]
        m = jnp.max(s, axis=1, keepdims=True)
        e = jnp.exp(s - m).astype(bf16)
        o = dot_nn(e, jnp.concatenate([half_of(v2, h), half_of(one, h)], axis=1))
        out = o if out is None else out + o
        es.append(e)
        ms.append(m)
    n = q2.shape[0]
    top = jnp.where(first_half(n), jnp.broadcast_to(ms[0], (n, 128)), jnp.broadcast_to(ms[1], (n, 128)))
    return es, top, out


def back(q2, k2, v2, gf2, fd2, es):
    dq = dk = dv = None
    for h in (0, 1):
        kh, vh = half_of(k2, h), half_of(v2, h)
        e = es[h]
        dp = dot_nt(gf2, vh)
        ds = (e.astype(f32) * (dp - fd2[:, 64 * h : 64 * h + 1])).astype(bf16)
        a, b, c = dot_nn(ds, kh), dot_tn(ds, half_of(q2, h)), dot_tn(e, half_of(gf2, h))
        dq, dk, dv = (a, b, c) if dq is None else (dq + a, dk + b, dv + c)
    return dq, dk, dv


def copies(pairs, sems):
    moves = [pltpu.make_async_copy(src, dst, sems.at[i]) for i, (src, dst) in enumerate(pairs)]
    for m in moves:
        m.start()
    return moves


def prep_body(info, q_in, k_in, v_in, o0, o1, o2, o3, px, q, k, v, sems):
    moves = copies(((q_in, q), (k_in, k), (v_in, v)), sems)
    order = row_order(False)
    for i, src in enumerate((q, k, v)):
        moves[i].wait()
        rows = dot_nn(order, src[...])
        px[i] = (rows * 0.125 if i == 0 else rows).astype(bf16)
    for d, o in enumerate((o0, o1, o2, o3)):
        c = pl.multiple_of(jnp.minimum(info[1] ^ d, 2) * 128, 128)
        for i in range(3):
            o[i] = px[i, :, pl.ds(c, 128)]


def grad_body(info, og, w, m_in, og_out, o0, o1, o2, o3, m_out, gx):
    m_out[...] = m_in[...]
    ordered = dot_nn(row_order(False), og[...]).astype(bf16)
    og_out[...] = ordered
    gx[...] = dot_nt(ordered, w[...]).astype(bf16)
    for d, o in enumerate((o0, o1, o2, o3)):
        o[...] = gx[:, pl.ds(pl.multiple_of(jnp.minimum(info[1] ^ d, 2) * 128, 128), 128)]


def collect_body(info, offsets, counts, m0, m1, m2, m3, x, s4, s8):
    place = Place(info, offsets, counts)
    for slot, m in enumerate((m0, m1, m2, m3)):
        for i in range(3):
            x[i, :, slot * 32 : slot * 32 + 32, :] = m[i].reshape(8, 32, 128)
    o3, o4 = place.offs(1), place.offs(2)
    for i in (0, 1):
        s4[i, 0:256] = pick(reader(x, i + 1), 1, o3)
        last = pick(reader(x, i + 1), 2, o4)
        s4[i, 256:384] = last
        s8[i] = last


def relay_body(s8, r4, o):
    for i in (0, 1):
        o[i] = s8[i]
        o[2 + i] = r4[i, 256:384]


def near_body(
    info, offsets, counts, x, top, num, den, m1, m2, e1, e2,
):
    place = Place(info, offsets, counts)
    for slot in range(4):
        b = place.bias_slot(slot)
        sl = slice(slot * 32, slot * 32 + 32)
        es, t, o = attend(*[slot_rows(x, slot, i) for i in range(3)], [b, b])
        e1[slot, 0], e1[slot, 1] = es
        t = t.reshape(8, 32, 128)
        top[:, sl, :] = t
        m1[:, sl, :] = t
        num[:, sl, :] = o[:, :128].reshape(8, 32, 128)
        den[:, sl, :] = o[:, 128:].reshape(8, 32, 128)
    oo = place.offs(0)
    q2, k2, v2 = [pick(reader(x, i), 0, oo) for i in range(3)]
    bias = [place.bias(512, 2, oo[h], place.base) for h in (0, 1)]
    es, t, o = attend(q2, k2, v2, bias)
    e2[0], e2[1] = es
    m2[...] = t
    merge(top, num, den, t, o, 0, oo)


def merge(top, num, den, t, o, pair, oo):
    old = pick(reader(top), pair, oo)
    new = jnp.maximum(old, t)
    a, b = jnp.exp(old - new), jnp.exp(t - new)
    n = pick(reader(num), pair, oo) * a + o[:, :128] * b
    d = pick(reader(den), pair, oo) * a + o[:, 128:] * b
    put(reader(top), writer(top), new, pair, oo, False)
    put(reader(num), writer(num), n, pair, oo, False)
    put(reader(den), writer(den), d, pair, oo, False)


def far_keys(place, x, r4, r12):
    o3, o4 = place.offs(1), place.offs(2)
    k3, v3 = [jnp.concatenate([pick(reader(x, i + 1), 1, o3), r4[i, 0:256]], axis=0) for i in (0, 1)]
    k4, v4 = [
        jnp.concatenate([pick(reader(x, i + 1), 2, o4), r4[i, 256:384], r12[2 + i], r12[i]], axis=0) for i in (0, 1)
    ]
    return o3, o4, k3, v3, k4, v4


def far_body(
    info, offsets, counts, x, r4, r12, top_in, num_in, den_in, g0, g1, g2, g3,
    top, norm, mx0, mx1, mx2, mx3, m3, m4, e3, e4, num, den,
):
    place = Place(info, offsets, counts)
    top[...] = top_in[...]
    num[...] = num_in[...]
    den[...] = den_in[...]
    o3, o4, k3, v3, k4, v4 = far_keys(place, x, r4, r12)
    at = [(place.quarter ^ i) * 1024 for i in range(4)]
    b3 = [jnp.concatenate([place.bias(256, 4, o3[h], at[i]) for i in (0, 1)], axis=1) for h in (0, 1)]
    b4 = [jnp.concatenate([place.bias(128, 8, o4[h], at[i]) for i in range(4)], axis=1) for h in (0, 1)]
    for pair, oo, k2, v2, b, m, e in ((1, o3, k3, v3, b3, m3, e3), (2, o4, k4, v4, b4, m4, e4)):
        es, t, out = attend(pick(reader(x, 0), pair, oo), k2, v2, b)
        e[0], e[1] = es
        m[...] = t
        merge(top, num, den, t, out, pair, oo)
    outs = (mx0, mx1, mx2, mx3)
    for res in range(8):
        ok = place.valid(res)
        scale = ok / (den[res] + 1.0 - ok)
        norm[res] = scale
        mixed = (num[res] * scale).astype(bf16)
        for slot, mx in enumerate(outs):
            mx[res * 32 : res * 32 + 32] = mixed[slot * 32 : slot * 32 + 32]
    for mx, g in zip(outs, (g0, g1, g2, g3)):
        mx[256:512] = g[...]


def pair_back(place, x, g, top, norm, delta, t, es, pair, oo, k2, v2):
    f2 = jnp.exp(t - pick(reader(top), pair, oo)) * pick(reader(norm), pair, oo)
    gf2 = (pick(reader(g), pair, oo).astype(f32) * f2).astype(bf16)
    fd2 = f2 * pick(reader(delta), pair, oo)
    return back(pick(reader(x, 0), pair, oo), k2, v2, gf2, fd2, es)


def far_back_body(
    info, offsets, counts, x, r4, r12, top, norm, m3, m4, e3, e4, mx0, mx1, mx2, mx3, in0, in1, in2, in3,
    g, delta, acc, d4, d8, d12,
):
    place = Place(info, offsets, counts)
    ri = lax.broadcasted_iota(jnp.int32, (128, 128), 0) >> 6
    ci = lax.broadcasted_iota(jnp.int32, (128, 128), 1) >> 6
    same = jnp.where(ri == ci, 1.0, 0.0)
    for slot, (mx, got) in enumerate(((mx0, in0), (mx1, in1), (mx2, in2), (mx3, in3))):
        sl = slice(slot * 32, slot * 32 + 32)
        rows = got[256:512]
        g[:, sl, :] = rows.reshape(8, 32, 128)
        prod = rows.astype(f32) * mx[0:256].astype(f32)
        sums = lax.dot_general(
            prod, same, (((1,), (0,)), ((), ())), precision=lax.Precision.HIGHEST, preferred_element_type=f32
        )
        delta[:, sl, :] = sums.reshape(8, 32, 128)
    o3, o4, k3, v3, k4, v4 = far_keys(place, x, r4, r12)
    acc[...] = jnp.zeros_like(acc)
    for pair, oo, k2, v2, m, e, parts in (
        (1, o3, k3, v3, m3, e3, ((d4, 0, 256),)),
        (2, o4, k4, v4, m4, e4, ((d4, 256, 128), (d8, 0, 128), (d12, 0, 128))),
    ):
        grads = pair_back(place, x, g, top, norm, delta, m[...], [e[0], e[1]], pair, oo, k2, v2)
        at_row = m.shape[0]
        for i in range(3):
            put(reader(acc, i), writer(acc, i), grads[i][:at_row], pair, oo, True)
        for ref, start, rows in parts:
            for i in (0, 1):
                ref[i, start : start + rows] = grads[i + 1][at_row : at_row + rows].astype(bf16)
            at_row += rows


def back_two_body(info, offsets, counts, x, g, top, norm, delta, acc_in, m2, e2, acc):
    place = Place(info, offsets, counts)
    acc[...] = acc_in[...]
    oo = place.offs(0)
    k2, v2 = pick(reader(x, 1), 0, oo), pick(reader(x, 2), 0, oo)
    grads = pair_back(place, x, g, top, norm, delta, m2[...], [e2[0], e2[1]], 0, oo, k2, v2)
    for i in range(3):
        put(reader(acc, i), writer(acc, i), grads[i], 0, oo, True)


def back_one_body(info, offsets, counts, x, g, top, norm, delta, acc_in, m1, e1, acc):
    for slot in range(4):
        sl = slice(slot * 32, slot * 32 + 32)
        f2 = jnp.exp(slot_rows(m1, slot) - slot_rows(top, slot)) * slot_rows(norm, slot)
        q2, k2, v2 = [slot_rows(x, slot, i) for i in range(3)]
        g2 = slot_rows(g, slot)
        gf2 = (g2.astype(f32) * f2).astype(bf16)
        fd2 = f2 * slot_rows(delta, slot)
        grads = back(q2, k2, v2, gf2, fd2, [e1[slot, 0], e1[slot, 1]])
        for i in range(3):
            acc[i, :, sl, :] = acc_in[i, :, sl, :] + grads[i].reshape(8, 32, 128)


def cores_body(keep, got, d4, d8, d12, own, f4, f8, f12):
    for u, (d, f) in enumerate(((None, own), (d4, f4), (d8, f8), (d12, f12))):
        part = keep[4 * u : 4 * u + 4] + got[4 * u : 4 * u + 4].astype(f32)
        if u == 0:
            f[...] = part
        else:
            n = d.shape[1]
            f[0:n] = d[0]
            f[n : 2 * n] = d[1]
            f[2 * n : 2 * n + 288] = part.reshape(288, 128).astype(bf16)


def finish_body(info, offsets, counts, acc_in, r4, r8, r12, part, own, o0, o1, o2, o3, acc):
    place = Place(info, offsets, counts)
    acc[...] = acc_in[...]
    p3, p4 = place.offs(1), place.offs(2)
    for i in (0, 1):
        rd, wr = reader(acc, i + 1), writer(acc, i + 1)
        put(rd, wr, r4[i * 384 : i * 384 + 256].astype(f32), 1, p3, True)
        far = r4[i * 384 + 256 : i * 384 + 384].astype(f32)
        far = far + r8[i * 128 : i * 128 + 128].astype(f32) + r12[i * 128 : i * 128 + 128].astype(f32)
        put(rd, wr, far, 2, p4, True)
    grads = [r[n : n + 288].astype(f32).reshape(4, 72, 128) for r, n in ((r4, 768), (r8, 256), (r12, 256))]
    total = part[...] + grads[0] + (grads[1] + grads[2])
    own[...] = total[0]
    for slot, o in enumerate((o0, o1, o2, o3)):
        o[0:256] = (slot_rows(acc, slot, 0) * 0.125).astype(bf16)
        o[256:512] = slot_rows(acc, slot, 1).astype(bf16)
        o[512:768] = slot_rows(acc, slot, 2).astype(bf16)
        o[768:848] = jnp.concatenate([total[slot], jnp.zeros((8, 128), f32)], axis=0).astype(bf16)


def home_body(info, m0, m1, m2, m3, dq, dk, dv, wide):
    order = row_order(True)
    for d, m in enumerate((m0, m1, m2, m3)):
        c = pl.multiple_of((info[1] ^ d) * 128, 128)
        for i in range(3):
            wide[i, :, pl.ds(c, 128)] = m[256 * i : 256 * i + 256]
    for i, o in enumerate((dq, dk, dv)):
        o[...] = dot_nn(order, wide[i, :, 0:384]).astype(bf16)


def near_sum_body(own, m1, m2, m3, o):
    a, b, c = [m[768:848].astype(f32)[0:72] for m in (m1, m2, m3)]
    o[...] = (own[...] + a + (b + c)).astype(bf16)


def widen(info, msgs, wide):
    for d, m in enumerate(msgs):
        wide[:, pl.ds(pl.multiple_of((info[1] ^ d) * 128, 128), 128)] = m[0:256]


def project_body(info, m0, m1, m2, m3, og, send, keep, wide, both, away):
    widen(info, (m0, m1, m2, m3), wide)
    both[...] = dot_tn(wide[:, 0:384], og[...])
    for s in range(16):
        for t in range(3):
            at = slice(t * 24, t * 24 + 24)
            there = pl.multiple_of((1 - info[2]) * 384 + t * 128, 128)
            here = pl.multiple_of(info[2] * 384 + t * 128, 128)
            away[s ^ info[0], at] = both[s * 24 : s * 24 + 24, pl.ds(there, 128)]
            keep[s ^ info[0], at] = both[s * 24 : s * 24 + 24, pl.ds(here, 128)]
    send[...] = away[...].astype(bf16)


def attended_body(info, m0, m1, m2, m3, w, o, wide):
    widen(info, (m0, m1, m2, m3), wide)
    mixed = dot_nn(row_order(True), wide[:, 0:384]).astype(bf16)
    o[...] = dot_nn(mixed, w[...]).astype(bf16)


def sum_body(a, b, c, d, o):
    one = a[...].astype(f32) + b[...].astype(f32)
    o[...] = (one + (c[...].astype(f32) + d[...].astype(f32))).astype(o.dtype)


def pair_body(a, b, o):
    o[...] = (a[...].astype(f32) + b[...].astype(f32)).astype(o.dtype)


def join_body(info, a, b, o):
    for t in range(3):
        at = slice(t * 24, t * 24 + 24)
        o[:, pl.ds(pl.multiple_of(info[2] * 384 + t * 128, 128), 128)] = a[at]
        o[:, pl.ds(pl.multiple_of((1 - info[2]) * 384 + t * 128, 128), 128)] = b[at]


smem = pl.BlockSpec(memory_space=pltpu.SMEM)
vmem = pl.BlockSpec(memory_space=pltpu.VMEM)
hbm = pl.BlockSpec(memory_space=pltpu.HBM)


def call(body, scalars, arrays, outs, scratch=(), flops=0, space=vmem, sems=0, limit=12):
    shapes = [jax.ShapeDtypeStruct(s, t) for s, t in outs]
    moved = sum(a.size * a.dtype.itemsize for a in arrays) + sum(s.size * s.dtype.itemsize for s in shapes)
    return pl.pallas_call(
        body,
        out_shape=shapes,
        in_specs=[smem] * len(scalars) + [space] * len(arrays),
        out_specs=[vmem] * len(shapes),
        scratch_shapes=[pltpu.VMEM(s, t) for s, t in scratch] + [pltpu.SemaphoreType.DMA((sems,))] * (sems > 0),
        compiler_params=pltpu.CompilerParams(vmem_limit_bytes=limit * 1024 * 1024),
        cost_estimate=pl.CostEstimate(flops=flops, bytes_accessed=moved, transcendentals=0),
    )(*scalars, *arrays)


def routes(seq_step, keep=None):
    pairs = []
    for dp in range(16):
        for s in range(16):
            t = s ^ seq_step
            if keep is not None and (keep(s, t) & 3) ^ (3 * (dp & 1)) == 3:
                continue
            pairs.append((dp * 16 + s, dp * 16 + t))
    return pairs


def shift(block, pairs):
    return lax.ppermute(block, ("dp", "seq"), pairs)


def dp_step(block, step):
    return lax.ppermute(block, "dp", [(i, i ^ step) for i in range(16)])


def seq_step(block, step):
    return lax.ppermute(block, "seq", [(i, i ^ step) for i in range(16)])


def per_device(queries, keys, values, out_weight, out_grad, offsets, counts):
    seq_rank = lax.axis_index("seq").astype(jnp.int32)
    core = lax.axis_index("dp").astype(jnp.int32) & 1
    info = jnp.stack([seq_rank, (seq_rank & 3) ^ (3 * core), core])
    places = [info, offsets, counts]

    chunk = ((3, 256, 128), bf16)
    third = ((256, 384), bf16)
    cube = (8, 128, 128)
    block = (72, 128)
    active = lambda s, t: s

    msgs = call(
        prep_body,
        [info],
        [queries[0], keys[0], values[0]],
        [chunk] * 4,
        [((3, 256, 384), bf16), third, third, third],
        space=hbm,
        sems=3,
        limit=57,
    )
    got = [shift(msgs[d], routes(d, lambda s, t: t)) for d in (1, 2, 3)]
    og, g0, g1, g2, g3, own = call(
        grad_body,
        [info],
        [out_grad[0], out_weight, msgs[0]],
        [((256, 768), bf16)] + [((256, 128), bf16)] * 4 + [chunk],
        [((256, 384), bf16)],
        flops=3 * 10**8,
    )
    x, s4, s8 = call(
        collect_body,
        places,
        [own] + got,
        [((3, *cube), bf16), ((2, 384, 128), bf16), ((2, 128, 128), bf16)],
    )
    r4 = shift(s4, routes(4, active))
    top, num, den, m1, m2, e1, e2 = call(
        near_body,
        places,
        [x],
        [(cube, f32)] * 4 + [((512, 128), f32), ((4, 2, 256, 256), bf16), ((2, 512, 512), bf16)],
        flops=10**9,
    )
    top, r4 = lax.optimization_barrier((top, r4))
    (s12,) = call(relay_body, [], [s8, r4], [((4, 128, 128), bf16)])
    r12 = shift(s12, routes(12, active))
    top, norm, mx0, mx1, mx2, mx3, m3, m4, e3, e4 = call(
        far_body,
        places,
        [x, r4, r12, top, num, den, g0, g1, g2, g3],
        [(cube, f32)] * 2
        + [((512, 128), bf16)] * 4
        + [((256, 128), f32), ((128, 128), f32), ((2, 256, 512), bf16), ((2, 128, 512), bf16)],
        [(cube, f32)] * 2,
        flops=10**9,
    )
    mixed = [mx0] + [shift(b, routes(d)) for d, b in ((1, mx1), (2, mx2), (3, mx3))]
    send, keep = call(
        project_body,
        [info],
        mixed + [og],
        [((16, *block), bf16), ((16, *block), f32)],
        [((256, 512), bf16), ((384, 768), f32), ((16, *block), f32)],
        flops=3 * 10**8,
    )
    arrived = dp_step(send, 1)
    keep, *mixed = lax.optimization_barrier([keep] + mixed)
    g, delta, acc, d4, d8, d12 = call(
        far_back_body,
        places,
        [x, r4, r12, top, norm, m3, m4, e3, e4, mx0, mx1, mx2, mx3] + mixed,
        [(cube, bf16), (cube, f32), ((3, *cube), f32)]
        + [((2, 384, 128), bf16), ((2, 128, 128), bf16), ((2, 128, 128), bf16)],
        flops=10**9,
    )
    state = [x, g, top, norm, delta]
    part, f4, f8, f12 = call(
        cores_body,
        [],
        [keep, arrived, d4, d8, d12],
        [((4, *block), f32), ((1056, 128), bf16), ((544, 128), bf16), ((544, 128), bf16)],
    )
    f4, f8, f12 = [shift(b, routes(d)) for d, b in ((4, f4), (8, f8), (12, f12))]
    acc, part, *mixed = lax.optimization_barrier([acc, part] + mixed)
    (attended,) = call(
        attended_body, [info], mixed + [out_weight], [((256, 768), bf16)], [((256, 512), bf16)], flops=3 * 10**8
    )
    acc, attended = lax.optimization_barrier((acc, attended))
    (acc,) = call(back_two_body, places, state + [acc, m2, e2], [((3, *cube), f32)], flops=10**9)
    (acc,) = call(back_one_body, places, state + [acc, m1, e1], [((3, *cube), f32)], flops=10**9)
    own, *outs = call(
        finish_body,
        places,
        [acc, f4, f8, f12, part],
        [(block, f32)] + [((848, 128), bf16)] * 4,
        [((3, *cube), f32)],
    )
    home = [outs[0]] + [shift(outs[d], routes(d)) for d in (1, 2, 3)]
    (own,) = call(near_sum_body, [], [own] + home[1:], [(block, bf16)])
    arrived = dp_step(own, 2)
    home = lax.optimization_barrier([own] + home)[1:]
    grads = call(home_body, [info], home, [third] * 3, [((3, 256, 512), bf16)])
    (own,) = call(pair_body, [], [own, arrived], [(block, bf16)])
    rest = [dp_step(own, d) for d in (4, 8, 12)]
    *grads, own = lax.optimization_barrier([*grads, own])
    (own,) = call(sum_body, [], [own] + rest, [(block, f32)])
    (grad_weight,) = call(join_body, [info], [own, dp_step(own, 1)], [((24, 768), f32)])
    return (attended[None], grads[0][None], grads[1][None], grads[2][None], grad_weight)


def solution(mesh):
    tiles = P("dp", "seq", None)
    return jax.shard_map(
        per_device,
        mesh=mesh,
        in_specs=(tiles, tiles, tiles, P(), tiles, P(), P("dp")),
        out_specs=(tiles, tiles, tiles, tiles, P("seq", None)),
        check_vma=False,
    )
```

```python
import jax
import jax.numpy as jnp
from jax import lax
from jax.experimental import pallas as pl
from jax.experimental.pallas import tpu as pltpu
from jax.sharding import PartitionSpec as P

bf16 = jnp.bfloat16
f32 = jnp.float32
low_bias = -1e30


def dot_nn(a, b):
    return lax.dot_general(a, b, (((1,), (0,)), ((), ())), preferred_element_type=f32)


def dot_nt(a, b):
    return lax.dot_general(a, b, (((1,), (1,)), ((), ())), preferred_element_type=f32)


def dot_tn(a, b):
    return lax.dot_general(a, b, (((0,), (0,)), ((), ())), preferred_element_type=f32)


def first_half(rows):
    return lax.broadcasted_iota(jnp.int32, (rows, 128), 1) < 64


def half_of(x, h):
    m = first_half(x.shape[0])
    z = jnp.zeros_like(x)
    return jnp.where(m, x, z) if h == 0 else jnp.where(m, z, x)


def row_order(back):
    a = lax.broadcasted_iota(jnp.int32, (256, 256), 0 if not back else 1)
    b = lax.broadcasted_iota(jnp.int32, (256, 256), 1 if not back else 0)
    return jnp.where(b == (a & 31) * 8 + (a >> 5), 1.0, 0.0).astype(bf16)


class Place:
    def __init__(self, info, offsets, counts):
        self.j = info[0] & 3
        self.base = (info[0] >> 2) * 1024
        self.quarter = info[0] >> 2
        self.chunk = jnp.minimum(info[1], 2)
        self.count = counts[0]
        self.offsets = offsets

    def offs(self, pair):
        r = 2 << pair
        return [self.offsets[pair, 2 * self.chunk + h] & (r - 1) for h in (0, 1)]

    def bias(self, n, step, o, base):
        kk = lax.broadcasted_iota(jnp.int32, (1, n), 1)
        pos = base + ((self.j ^ ((kk >> 5) & 3)) << 8) + (kk & 31) * 8 + o + step * (kk >> 7)
        return jnp.where(pos < self.count, 0.0, low_bias)

    def bias_slot(self, slot):
        kk = lax.broadcasted_iota(jnp.int32, (1, 256), 1)
        pos = self.base + ((self.j ^ slot) << 8) + (kk & 31) * 8 + (kk >> 5)
        return jnp.where(pos < self.count, 0.0, low_bias)

    def valid(self, res):
        rr = lax.broadcasted_iota(jnp.int32, (128, 128), 0)
        pos = self.base + ((self.j ^ (rr >> 5)) << 8) + (rr & 31) * 8 + res
        return jnp.where(pos < self.count, 1.0, 0.0)


def pick(read, pair, oo):
    r = 2 << pair
    m = first_half(128)
    parts = [jnp.where(m, read(oo[0] + r * i), read(oo[1] + r * i)) for i in range(8 // r)]
    return parts[0] if len(parts) == 1 else jnp.concatenate(parts, axis=0)


def put(read, write, val, pair, oo, add):
    r = 2 << pair
    m = first_half(128)
    for i in range(8 // r):
        blk = val[i * 128 : (i + 1) * 128]
        for h in (0, 1):
            mine = m if h == 0 else ~m
            old = read(oo[h] + r * i)
            write(oo[h] + r * i, jnp.where(mine, old + blk if add else blk, old))


def reader(ref, *lead):
    return lambda i: ref[(*lead, i)]


def writer(ref, *lead):
    def w(i, val):
        ref[(*lead, i)] = val

    return w


def slot_rows(ref, slot, *lead):
    return ref[(*lead, slice(None), slice(slot * 32, slot * 32 + 32), slice(None))].reshape(256, 128)


def attend(q2, k2, v2, bias):
    nk = k2.shape[0]
    out, es, ms = None, [], []
    one = jnp.ones((nk, 128), bf16)
    for h in (0, 1):
        s = dot_nt(q2, half_of(k2, h)) + bias[h]
        m = jnp.max(s, axis=1, keepdims=True)
        e = jnp.exp(s - m).astype(bf16)
        o = dot_nn(e, jnp.concatenate([half_of(v2, h), half_of(one, h)], axis=1))
        out = o if out is None else out + o
        es.append(e)
        ms.append(m)
    n = q2.shape[0]
    top = jnp.where(first_half(n), jnp.broadcast_to(ms[0], (n, 128)), jnp.broadcast_to(ms[1], (n, 128)))
    return es, top, out


def back(q2, k2, v2, gf2, fd2, es):
    dq = dk = dv = None
    for h in (0, 1):
        kh, vh = half_of(k2, h), half_of(v2, h)
        e = es[h]
        dp = dot_nt(gf2, vh)
        ds = (e.astype(f32) * (dp - fd2[:, 64 * h : 64 * h + 1])).astype(bf16)
        a, b, c = dot_nn(ds, kh), dot_tn(ds, half_of(q2, h)), dot_tn(e, half_of(gf2, h))
        dq, dk, dv = (a, b, c) if dq is None else (dq + a, dk + b, dv + c)
    return dq, dk, dv


def copies(pairs, sems):
    moves = [pltpu.make_async_copy(src, dst, sems.at[i]) for i, (src, dst) in enumerate(pairs)]
    for m in moves:
        m.start()
    return moves


def prep_body(info, q_in, k_in, v_in, o0, o1, o2, o3, px, q, k, v, sems):
    moves = copies(((q_in, q), (k_in, k), (v_in, v)), sems)
    order = row_order(False)
    for i, src in enumerate((q, k, v)):
        moves[i].wait()
        rows = dot_nn(order, src[...])
        px[i] = (rows * 0.125 if i == 0 else rows).astype(bf16)
    for d, o in enumerate((o0, o1, o2, o3)):
        c = pl.multiple_of(jnp.minimum(info[1] ^ d, 2) * 128, 128)
        for i in range(3):
            o[i] = px[i, :, pl.ds(c, 128)]


def grad_body(info, og, w, m_in, og_out, o0, o1, o2, o3, m_out, gx):
    m_out[...] = m_in[...]
    ordered = dot_nn(row_order(False), og[...]).astype(bf16)
    og_out[...] = ordered
    gx[...] = dot_nt(ordered, w[...]).astype(bf16)
    for d, o in enumerate((o0, o1, o2, o3)):
        o[...] = gx[:, pl.ds(pl.multiple_of(jnp.minimum(info[1] ^ d, 2) * 128, 128), 128)]


def collect_body(info, offsets, counts, m0, m1, m2, m3, x, s4, s8):
    place = Place(info, offsets, counts)
    for slot, m in enumerate((m0, m1, m2, m3)):
        for i in range(3):
            x[i, :, slot * 32 : slot * 32 + 32, :] = m[i].reshape(8, 32, 128)
    o3, o4 = place.offs(1), place.offs(2)
    for i in (0, 1):
        s4[i, 0:256] = pick(reader(x, i + 1), 1, o3)
        last = pick(reader(x, i + 1), 2, o4)
        s4[i, 256:384] = last
        s8[i] = last


def relay_body(s8, r4, o):
    for i in (0, 1):
        o[i] = s8[i]
        o[2 + i] = r4[i, 256:384]


def near_body(
    info, offsets, counts, x, top, num, den, m1, m2, e1, e2,
):
    place = Place(info, offsets, counts)
    for slot in range(4):
        b = place.bias_slot(slot)
        sl = slice(slot * 32, slot * 32 + 32)
        es, t, o = attend(*[slot_rows(x, slot, i) for i in range(3)], [b, b])
        e1[slot, 0], e1[slot, 1] = es
        t = t.reshape(8, 32, 128)
        top[:, sl, :] = t
        m1[:, sl, :] = t
        num[:, sl, :] = o[:, :128].reshape(8, 32, 128)
        den[:, sl, :] = o[:, 128:].reshape(8, 32, 128)
    oo = place.offs(0)
    q2, k2, v2 = [pick(reader(x, i), 0, oo) for i in range(3)]
    bias = [place.bias(512, 2, oo[h], place.base) for h in (0, 1)]
    es, t, o = attend(q2, k2, v2, bias)
    e2[0], e2[1] = es
    m2[...] = t
    merge(top, num, den, t, o, 0, oo)


def merge(top, num, den, t, o, pair, oo):
    old = pick(reader(top), pair, oo)
    new = jnp.maximum(old, t)
    a, b = jnp.exp(old - new), jnp.exp(t - new)
    n = pick(reader(num), pair, oo) * a + o[:, :128] * b
    d = pick(reader(den), pair, oo) * a + o[:, 128:] * b
    put(reader(top), writer(top), new, pair, oo, False)
    put(reader(num), writer(num), n, pair, oo, False)
    put(reader(den), writer(den), d, pair, oo, False)


def keys3(place, x, r4):
    oo = place.offs(1)
    return [oo] + [jnp.concatenate([pick(reader(x, i + 1), 1, oo), r4[i, 0:256]], axis=0) for i in (0, 1)]


def keys4(place, x, r4, r12):
    oo = place.offs(2)
    return [oo] + [
        jnp.concatenate([pick(reader(x, i + 1), 2, oo), r4[i, 256:384], r12[2 + i], r12[i]], axis=0)
        for i in (0, 1)
    ]


def mid_body(info, offsets, counts, x, r4, top_in, num_in, den_in, top, num, den, m3, e3):
    place = Place(info, offsets, counts)
    top[...] = top_in[...]
    num[...] = num_in[...]
    den[...] = den_in[...]
    oo, k2, v2 = keys3(place, x, r4)
    at = [(place.quarter ^ i) * 1024 for i in (0, 1)]
    bias = [jnp.concatenate([place.bias(256, 4, oo[h], b) for b in at], axis=1) for h in (0, 1)]
    es, t, out = attend(pick(reader(x, 0), 1, oo), k2, v2, bias)
    e3[0], e3[1] = es
    m3[...] = t
    merge(top, num, den, t, out, 1, oo)


def far_body(
    info, offsets, counts, x, r4, r12, top_in, num_in, den_in, g0, g1, g2, g3,
    top, norm, mx0, mx1, mx2, mx3, m4, e4, num, den,
):
    place = Place(info, offsets, counts)
    top[...] = top_in[...]
    num[...] = num_in[...]
    den[...] = den_in[...]
    oo, k2, v2 = keys4(place, x, r4, r12)
    at = [(place.quarter ^ i) * 1024 for i in range(4)]
    bias = [jnp.concatenate([place.bias(128, 8, oo[h], b) for b in at], axis=1) for h in (0, 1)]
    es, t, out = attend(pick(reader(x, 0), 2, oo), k2, v2, bias)
    e4[0], e4[1] = es
    m4[...] = t
    merge(top, num, den, t, out, 2, oo)
    outs = (mx0, mx1, mx2, mx3)
    for res in range(8):
        ok = place.valid(res)
        scale = ok / (den[res] + 1.0 - ok)
        norm[res] = scale
        mixed = (num[res] * scale).astype(bf16)
        for slot, mx in enumerate(outs):
            mx[res * 32 : res * 32 + 32] = mixed[slot * 32 : slot * 32 + 32]
    for mx, g in zip(outs, (g0, g1, g2, g3)):
        mx[256:512] = g[...]


def pair_back(place, x, g, top, norm, delta, t, es, pair, oo, k2, v2):
    f2 = jnp.exp(t - pick(reader(top), pair, oo)) * pick(reader(norm), pair, oo)
    gf2 = (pick(reader(g), pair, oo).astype(f32) * f2).astype(bf16)
    fd2 = f2 * pick(reader(delta), pair, oo)
    return back(pick(reader(x, 0), pair, oo), k2, v2, gf2, fd2, es)


def far_back_body(
    info, offsets, counts, x, r4, r12, top, norm, m3, m4, e3, e4, mx0, mx1, mx2, mx3, in0, in1, in2, in3,
    g, delta, acc, d4, d8, d12,
):
    place = Place(info, offsets, counts)
    ri = lax.broadcasted_iota(jnp.int32, (128, 128), 0) >> 6
    ci = lax.broadcasted_iota(jnp.int32, (128, 128), 1) >> 6
    same = jnp.where(ri == ci, 1.0, 0.0)
    for slot, (mx, got) in enumerate(((mx0, in0), (mx1, in1), (mx2, in2), (mx3, in3))):
        sl = slice(slot * 32, slot * 32 + 32)
        rows = got[256:512]
        g[:, sl, :] = rows.reshape(8, 32, 128)
        prod = rows.astype(f32) * mx[0:256].astype(f32)
        sums = lax.dot_general(
            prod, same, (((1,), (0,)), ((), ())), precision=lax.Precision.HIGHEST, preferred_element_type=f32
        )
        delta[:, sl, :] = sums.reshape(8, 32, 128)
    o3, k3, v3 = keys3(place, x, r4)
    o4, k4, v4 = keys4(place, x, r4, r12)
    acc[...] = jnp.zeros_like(acc)
    for pair, oo, k2, v2, m, e, parts in (
        (1, o3, k3, v3, m3, e3, ((d4, 0, 256),)),
        (2, o4, k4, v4, m4, e4, ((d4, 256, 128), (d8, 0, 128), (d12, 0, 128))),
    ):
        grads = pair_back(place, x, g, top, norm, delta, m[...], [e[0], e[1]], pair, oo, k2, v2)
        at_row = m.shape[0]
        for i in range(3):
            put(reader(acc, i), writer(acc, i), grads[i][:at_row], pair, oo, True)
        for ref, start, rows in parts:
            for i in (0, 1):
                ref[i, start : start + rows] = grads[i + 1][at_row : at_row + rows].astype(bf16)
            at_row += rows


def back_two_body(info, offsets, counts, x, g, top, norm, delta, acc_in, m2, e2, acc):
    place = Place(info, offsets, counts)
    acc[...] = acc_in[...]
    oo = place.offs(0)
    k2, v2 = pick(reader(x, 1), 0, oo), pick(reader(x, 2), 0, oo)
    grads = pair_back(place, x, g, top, norm, delta, m2[...], [e2[0], e2[1]], 0, oo, k2, v2)
    for i in range(3):
        put(reader(acc, i), writer(acc, i), grads[i], 0, oo, True)


def back_one_body(info, offsets, counts, x, g, top, norm, delta, acc_in, m1, e1, acc):
    for slot in range(4):
        sl = slice(slot * 32, slot * 32 + 32)
        f2 = jnp.exp(slot_rows(m1, slot) - slot_rows(top, slot)) * slot_rows(norm, slot)
        q2, k2, v2 = [slot_rows(x, slot, i) for i in range(3)]
        g2 = slot_rows(g, slot)
        gf2 = (g2.astype(f32) * f2).astype(bf16)
        fd2 = f2 * slot_rows(delta, slot)
        grads = back(q2, k2, v2, gf2, fd2, [e1[slot, 0], e1[slot, 1]])
        for i in range(3):
            acc[i, :, sl, :] = acc_in[i, :, sl, :] + grads[i].reshape(8, 32, 128)


def cores_body(keep, got, d4, d8, d12, own, f4, f8, f12):
    for u, (d, f) in enumerate(((None, own), (d4, f4), (d8, f8), (d12, f12))):
        part = keep[4 * u : 4 * u + 4] + got[4 * u : 4 * u + 4].astype(f32)
        if u == 0:
            f[...] = part
        else:
            n = d.shape[1]
            f[0:n] = d[0]
            f[n : 2 * n] = d[1]
            f[2 * n : 2 * n + 288] = part.reshape(288, 128).astype(bf16)


def far_sum_body(part, f4, f8, f12, low):
    a, b, c = [r[n : n + 288].astype(f32) for r, n in ((f4, 768), (f8, 256), (f12, 256))]
    low[...] = (part[...].reshape(288, 128) + a + (b + c)).astype(bf16)


def finish_body(info, offsets, counts, acc_in, r4, r8, r12, o0, o1, o2, o3, acc):
    place = Place(info, offsets, counts)
    acc[...] = acc_in[...]
    p3, p4 = place.offs(1), place.offs(2)
    for i in (0, 1):
        rd, wr = reader(acc, i + 1), writer(acc, i + 1)
        put(rd, wr, r4[i * 384 : i * 384 + 256].astype(f32), 1, p3, True)
        far = r4[i * 384 + 256 : i * 384 + 384].astype(f32)
        far = far + r8[i * 128 : i * 128 + 128].astype(f32) + r12[i * 128 : i * 128 + 128].astype(f32)
        put(rd, wr, far, 2, p4, True)
    for slot, o in enumerate((o0, o1, o2, o3)):
        o[0:256] = (slot_rows(acc, slot, 0) * 0.125).astype(bf16)
        o[256:512] = slot_rows(acc, slot, 1).astype(bf16)
        o[512:768] = slot_rows(acc, slot, 2).astype(bf16)


def home_body(info, m0, m1, m2, m3, dq, dk, dv, wide):
    order = row_order(True)
    for d, m in enumerate((m0, m1, m2, m3)):
        c = pl.multiple_of((info[1] ^ d) * 128, 128)
        for i in range(3):
            wide[i, :, pl.ds(c, 128)] = m[256 * i : 256 * i + 256]
    for i, o in enumerate((dq, dk, dv)):
        o[...] = dot_nn(order, wide[i, :, 0:384]).astype(bf16)


def halves_body(mine, other, own, s1, s2, s3):
    a, b = mine[...].astype(f32), other[...].astype(f32)
    for d, o in enumerate((own, s1, s2, s3)):
        at = slice(72 * d, 72 * d + 72)
        o[...] = jnp.concatenate([a[at], b[at]], axis=0).astype(o.dtype)


def widen(info, msgs, wide):
    for d, m in enumerate(msgs):
        wide[:, pl.ds(pl.multiple_of((info[1] ^ d) * 128, 128), 128)] = m[0:256]


def project_body(info, m0, m1, m2, m3, og, send, keep, wide, both, away):
    widen(info, (m0, m1, m2, m3), wide)
    both[...] = dot_tn(wide[:, 0:384], og[...])
    for s in range(16):
        for t in range(3):
            at = slice(t * 24, t * 24 + 24)
            there = pl.multiple_of((1 - info[2]) * 384 + t * 128, 128)
            here = pl.multiple_of(info[2] * 384 + t * 128, 128)
            away[s ^ info[0], at] = both[s * 24 : s * 24 + 24, pl.ds(there, 128)]
            keep[s ^ info[0], at] = both[s * 24 : s * 24 + 24, pl.ds(here, 128)]
    send[...] = away[...].astype(bf16)


def attended_body(info, m0, m1, m2, m3, w, o, wide):
    widen(info, (m0, m1, m2, m3), wide)
    mixed = dot_nn(row_order(True), wide[:, 0:384]).astype(bf16)
    o[...] = dot_nn(mixed, w[...]).astype(bf16)


def sum_body(a, b, c, d, o):
    one = a[...].astype(f32) + b[...].astype(f32)
    o[...] = (one + (c[...].astype(f32) + d[...].astype(f32))).astype(o.dtype)


def pair_body(a, b, o):
    o[...] = (a[...].astype(f32) + b[...].astype(f32)).astype(o.dtype)


def join_body(info, own, a, b, c, o):
    total = own[...] + a[...].astype(f32) + (b[...].astype(f32) + c[...].astype(f32))
    for h in (0, 1):
        for t in range(3):
            col = pl.multiple_of((info[2] ^ h) * 384 + t * 128, 128)
            o[:, pl.ds(col, 128)] = total[72 * h + 24 * t : 72 * h + 24 * t + 24]


smem = pl.BlockSpec(memory_space=pltpu.SMEM)
vmem = pl.BlockSpec(memory_space=pltpu.VMEM)
hbm = pl.BlockSpec(memory_space=pltpu.HBM)


def call(body, scalars, arrays, outs, scratch=(), flops=0, space=vmem, sems=0, limit=12):
    shapes = [jax.ShapeDtypeStruct(s, t) for s, t in outs]
    moved = sum(a.size * a.dtype.itemsize for a in arrays) + sum(s.size * s.dtype.itemsize for s in shapes)
    return pl.pallas_call(
        body,
        out_shape=shapes,
        in_specs=[smem] * len(scalars) + [space] * len(arrays),
        out_specs=[vmem] * len(shapes),
        scratch_shapes=[pltpu.VMEM(s, t) for s, t in scratch] + [pltpu.SemaphoreType.DMA((sems,))] * (sems > 0),
        compiler_params=pltpu.CompilerParams(vmem_limit_bytes=limit * 1024 * 1024),
        cost_estimate=pl.CostEstimate(flops=flops, bytes_accessed=moved, transcendentals=0),
    )(*scalars, *arrays)


def routes(seq_step, keep=None):
    pairs = []
    for dp in range(16):
        for s in range(16):
            t = s ^ seq_step
            if keep is not None and (keep(s, t) & 3) ^ (3 * (dp & 1)) == 3:
                continue
            pairs.append((dp * 16 + s, dp * 16 + t))
    return pairs


def shift(block, pairs):
    return lax.ppermute(block, ("dp", "seq"), pairs)


def dp_step(block, step):
    return lax.ppermute(block, "dp", [(i, i ^ step) for i in range(16)])


def seq_step(block, step):
    return lax.ppermute(block, "seq", [(i, i ^ step) for i in range(16)])


def per_device(queries, keys, values, out_weight, out_grad, offsets, counts):
    seq_rank = lax.axis_index("seq").astype(jnp.int32)
    core = lax.axis_index("dp").astype(jnp.int32) & 1
    info = jnp.stack([seq_rank, (seq_rank & 3) ^ (3 * core), core])
    places = [info, offsets, counts]

    chunk = ((3, 256, 128), bf16)
    third = ((256, 384), bf16)
    cube = (8, 128, 128)
    block = (72, 128)
    active = lambda s, t: s

    msgs = call(
        prep_body,
        [info],
        [queries[0], keys[0], values[0]],
        [chunk] * 4,
        [((3, 256, 384), bf16), third, third, third],
        space=hbm,
        sems=3,
        limit=57,
    )
    got = [shift(msgs[d], routes(d)) for d in (1, 2, 3)]
    og, g0, g1, g2, g3, own = call(
        grad_body,
        [info],
        [out_grad[0], out_weight, msgs[0]],
        [((256, 768), bf16)] + [((256, 128), bf16)] * 4 + [chunk],
        [((256, 384), bf16)],
        flops=3 * 10**8,
    )
    x, s4, s8 = call(
        collect_body,
        places,
        [own] + got,
        [((3, *cube), bf16), ((2, 384, 128), bf16), ((2, 128, 128), bf16)],
    )
    r4 = shift(s4, routes(4))
    top, num, den, m1, m2, e1, e2 = call(
        near_body,
        places,
        [x],
        [(cube, f32)] * 4 + [((512, 128), f32), ((4, 2, 256, 256), bf16), ((2, 512, 512), bf16)],
        flops=10**9,
    )
    top, r4 = lax.optimization_barrier((top, r4))
    (s12,) = call(relay_body, [], [s8, r4], [((4, 128, 128), bf16)])
    r12 = shift(s12, routes(12))
    top, s12 = lax.optimization_barrier((top, s12))
    top, num, den, m3, e3 = call(
        mid_body,
        places,
        [x, r4, top, num, den],
        [(cube, f32)] * 3 + [((256, 128), f32), ((2, 256, 512), bf16)],
        flops=10**9,
    )
    top, norm, mx0, mx1, mx2, mx3, m4, e4 = call(
        far_body,
        places,
        [x, r4, r12, top, num, den, g0, g1, g2, g3],
        [(cube, f32)] * 2 + [((512, 128), bf16)] * 4 + [((128, 128), f32), ((2, 128, 512), bf16)],
        [(cube, f32)] * 2,
        flops=10**9,
    )
    mixed = [mx0] + [shift(b, routes(d)) for d, b in ((1, mx1), (2, mx2), (3, mx3))]
    send, keep = call(
        project_body,
        [info],
        mixed + [og],
        [((16, *block), bf16), ((16, *block), f32)],
        [((256, 512), bf16), ((384, 768), f32), ((16, *block), f32)],
        flops=3 * 10**8,
    )
    arrived = dp_step(send, 1)
    keep, *mixed = lax.optimization_barrier([keep] + mixed)
    g, delta, acc, d4, d8, d12 = call(
        far_back_body,
        places,
        [x, r4, r12, top, norm, m3, m4, e3, e4, mx0, mx1, mx2, mx3] + mixed,
        [(cube, bf16), (cube, f32), ((3, *cube), f32)]
        + [((2, 384, 128), bf16), ((2, 128, 128), bf16), ((2, 128, 128), bf16)],
        flops=10**9,
    )
    state = [x, g, top, norm, delta]
    part, f4, f8, f12 = call(
        cores_body,
        [],
        [keep, arrived, d4, d8, d12],
        [((4, *block), f32), ((1056, 128), bf16), ((544, 128), bf16), ((544, 128), bf16)],
    )
    f4, f8, f12 = [shift(b, routes(d)) for d, b in ((4, f4), (8, f8), (12, f12))]
    acc, part, *mixed = lax.optimization_barrier([acc, part] + mixed)
    (attended,) = call(
        attended_body, [info], mixed + [out_weight], [((256, 768), bf16)], [((256, 512), bf16)], flops=3 * 10**8
    )
    acc, attended = lax.optimization_barrier((acc, attended))
    (acc,) = call(back_two_body, places, state + [acc, m2, e2], [((3, *cube), f32)], flops=10**9)
    (acc,) = call(back_one_body, places, state + [acc, m1, e1], [((3, *cube), f32)], flops=10**9)
    (low,) = call(far_sum_body, [], [part, f4, f8, f12], [((288, 128), bf16)])
    acc, low = lax.optimization_barrier((acc, low))
    arrived = dp_step(low, 2)
    outs = call(
        finish_body, places, [acc, f4, f8, f12], [((768, 128), bf16)] * 4, [((3, *cube), f32)]
    )
    first, low = lax.optimization_barrier((outs[0], low))
    home = [first] + [shift(outs[d], routes(d)) for d in (1, 2, 3)]
    (low,) = call(pair_body, [], [low, arrived], [((288, 128), bf16)])
    rest = [dp_step(low, d) for d in (4, 8, 12)]
    (low,) = call(sum_body, [], [low] + rest, [((288, 128), bf16)])
    grads = call(home_body, [info], home, [third] * 3, [((3, 256, 512), bf16)])
    own, s1, s2, s3 = call(
        halves_body, [], [low, dp_step(low, 1)], [((144, 128), f32)] + [((144, 128), bf16)] * 3
    )
    near = [seq_step(b, d) for d, b in ((1, s1), (2, s2), (3, s3))]
    *grads, own = lax.optimization_barrier([*grads, own])
    (grad_weight,) = call(join_body, [info], [own] + near, [((24, 768), f32)])
    return (attended[None], grads[0][None], grads[1][None], grads[2][None], grad_weight)


def solution(mesh):
    tiles = P("dp", "seq", None)
    return jax.shard_map(
        per_device,
        mesh=mesh,
        in_specs=(tiles, tiles, tiles, P(), tiles, P(), P("dp")),
        out_specs=(tiles, tiles, tiles, tiles, P("seq", None)),
        check_vma=False,
    )
```

```python
import jax
import jax.numpy as jnp
from jax import lax
from jax.experimental import pallas as pl
from jax.experimental.pallas import tpu as pltpu
from jax.sharding import PartitionSpec as P

bf16 = jnp.bfloat16
f32 = jnp.float32
low_bias = -1e30


def dot_nn(a, b):
    return lax.dot_general(a, b, (((1,), (0,)), ((), ())), preferred_element_type=f32)


def dot_nt(a, b):
    return lax.dot_general(a, b, (((1,), (1,)), ((), ())), preferred_element_type=f32)


def dot_tn(a, b):
    return lax.dot_general(a, b, (((0,), (0,)), ((), ())), preferred_element_type=f32)


def first_half(rows):
    return lax.broadcasted_iota(jnp.int32, (rows, 128), 1) < 64


def half_of(x, h):
    m = first_half(x.shape[0])
    z = jnp.zeros_like(x)
    return jnp.where(m, x, z) if h == 0 else jnp.where(m, z, x)


def row_order(back):
    a = lax.broadcasted_iota(jnp.int32, (256, 256), 0 if not back else 1)
    b = lax.broadcasted_iota(jnp.int32, (256, 256), 1 if not back else 0)
    return jnp.where(b == (a & 31) * 8 + (a >> 5), 1.0, 0.0).astype(bf16)


class Place:
    def __init__(self, info, offsets, counts):
        self.j = info[0] & 3
        self.base = (info[0] >> 2) * 1024
        self.quarter = info[0] >> 2
        self.chunk = jnp.minimum(info[1], 2)
        self.count = counts[0]
        self.offsets = offsets

    def offs(self, pair):
        r = 2 << pair
        return [self.offsets[pair, 2 * self.chunk + h] & (r - 1) for h in (0, 1)]

    def bias(self, n, step, o, base):
        kk = lax.broadcasted_iota(jnp.int32, (1, n), 1)
        pos = base + ((self.j ^ ((kk >> 5) & 3)) << 8) + (kk & 31) * 8 + o + step * (kk >> 7)
        return jnp.where(pos < self.count, 0.0, low_bias)

    def bias_slot(self, slot):
        kk = lax.broadcasted_iota(jnp.int32, (1, 256), 1)
        pos = self.base + ((self.j ^ slot) << 8) + (kk & 31) * 8 + (kk >> 5)
        return jnp.where(pos < self.count, 0.0, low_bias)

    def valid(self, res):
        rr = lax.broadcasted_iota(jnp.int32, (128, 128), 0)
        pos = self.base + ((self.j ^ (rr >> 5)) << 8) + (rr & 31) * 8 + res
        return jnp.where(pos < self.count, 1.0, 0.0)


def pick(read, pair, oo):
    r = 2 << pair
    m = first_half(128)
    parts = [jnp.where(m, read(oo[0] + r * i), read(oo[1] + r * i)) for i in range(8 // r)]
    return parts[0] if len(parts) == 1 else jnp.concatenate(parts, axis=0)


def put(read, write, val, pair, oo, add):
    r = 2 << pair
    m = first_half(128)
    for i in range(8 // r):
        blk = val[i * 128 : (i + 1) * 128]
        for h in (0, 1):
            mine = m if h == 0 else ~m
            old = read(oo[h] + r * i)
            write(oo[h] + r * i, jnp.where(mine, old + blk if add else blk, old))


def reader(ref, *lead):
    return lambda i: ref[(*lead, i)]


def writer(ref, *lead):
    def w(i, val):
        ref[(*lead, i)] = val

    return w


def slot_rows(ref, slot, *lead):
    return ref[(*lead, slice(None), slice(slot * 32, slot * 32 + 32), slice(None))].reshape(256, 128)


def attend(q2, k2, v2, bias):
    nk = k2.shape[0]
    out, es, ms = None, [], []
    one = jnp.ones((nk, 128), bf16)
    for h in (0, 1):
        s = dot_nt(q2, half_of(k2, h)) + bias[h]
        m = jnp.max(s, axis=1, keepdims=True)
        e = jnp.exp(s - m).astype(bf16)
        o = dot_nn(e, jnp.concatenate([half_of(v2, h), half_of(one, h)], axis=1))
        out = o if out is None else out + o
        es.append(e)
        ms.append(m)
    n = q2.shape[0]
    top = jnp.where(first_half(n), jnp.broadcast_to(ms[0], (n, 128)), jnp.broadcast_to(ms[1], (n, 128)))
    return es, top, out


def back(q2, k2, v2, gf2, fd2, es):
    low = gf2.astype(bf16)
    qt, gt = q2.astype(f32).T.astype(bf16), gf2.T.astype(bf16)
    dq, dks, dvs = None, [], []
    for h in (0, 1):
        e, at = es[h], slice(64 * h, 64 * h + 64)
        dp = dot_nt(low, half_of(v2, h))
        ds = (e.astype(f32) * (dp - fd2[:, 64 * h : 64 * h + 1])).astype(bf16)
        a = dot_nn(ds, half_of(k2, h))
        dq = a if dq is None else dq + a
        dks.append(dot_nn(qt[at], ds))
        dvs.append(dot_nn(gt[at], e))
    return dq, jnp.concatenate(dks, axis=0).T, jnp.concatenate(dvs, axis=0).T


def copies(pairs, sems):
    moves = [pltpu.make_async_copy(src, dst, sems.at[i]) for i, (src, dst) in enumerate(pairs)]
    for m in moves:
        m.start()
    return moves


def prep_body(q_in, k_in, v_in, o0, o1, o2, o3, px, q, k, v, sems):
    moves = copies(((q_in, q), (k_in, k), (v_in, v)), sems)
    chunk = (lax.axis_index("seq") & 3) ^ (3 * (lax.axis_index("dp") & 1))
    order = row_order(False)
    for i, src in enumerate((q, k, v)):
        moves[i].wait()
        rows = dot_nn(order, src[...])
        px[i] = (rows * 0.125 if i == 0 else rows).astype(bf16)
    for d, o in enumerate((o0, o1, o2, o3)):
        c = pl.multiple_of(jnp.minimum(chunk ^ d, 2) * 128, 128)
        for i in range(3):
            o[i] = px[i, :, pl.ds(c, 128)]


def grad_body(info, og, w, m_in, og_out, o0, o1, o2, o3, m_out, gx):
    m_out[...] = m_in[...]
    ordered = dot_nn(row_order(False), og[...]).astype(bf16)
    og_out[...] = ordered
    gx[...] = dot_nt(ordered, w[...]).astype(bf16)
    for d, o in enumerate((o0, o1, o2, o3)):
        o[...] = gx[:, pl.ds(pl.multiple_of(jnp.minimum(info[1] ^ d, 2) * 128, 128), 128)]


def collect_body(info, offsets, counts, m0, m1, m2, m3, x, s4, s8):
    place = Place(info, offsets, counts)
    for slot, m in enumerate((m0, m1, m2, m3)):
        for i in range(3):
            x[i, :, slot * 32 : slot * 32 + 32, :] = m[i].reshape(8, 32, 128)
    o3, o4 = place.offs(1), place.offs(2)
    for i in (0, 1):
        s4[i, 0:256] = pick(reader(x, i + 1), 1, o3)
        last = pick(reader(x, i + 1), 2, o4)
        s4[i, 256:384] = last
        s8[i] = last


def relay_body(s8, r4, o):
    for i in (0, 1):
        o[i] = s8[i]
        o[2 + i] = r4[i, 256:384]


def near_body(
    info, offsets, counts, x, top, num, den, m1, m2, e1, e2,
):
    place = Place(info, offsets, counts)
    for slot in range(4):
        b = place.bias_slot(slot)
        sl = slice(slot * 32, slot * 32 + 32)
        es, t, o = attend(*[slot_rows(x, slot, i) for i in range(3)], [b, b])
        e1[slot, 0], e1[slot, 1] = es
        t = t.reshape(8, 32, 128)
        top[:, sl, :] = t
        m1[:, sl, :] = t
        num[:, sl, :] = o[:, :128].reshape(8, 32, 128)
        den[:, sl, :] = o[:, 128:].reshape(8, 32, 128)
    oo = place.offs(0)
    q2, k2, v2 = [pick(reader(x, i), 0, oo) for i in range(3)]
    bias = [place.bias(512, 2, oo[h], place.base) for h in (0, 1)]
    es, t, o = attend(q2, k2, v2, bias)
    e2[0], e2[1] = es
    m2[...] = t
    merge(top, num, den, t, o, 0, oo)


def merge(top, num, den, t, o, pair, oo):
    old = pick(reader(top), pair, oo)
    new = jnp.maximum(old, t)
    a, b = jnp.exp(old - new), jnp.exp(t - new)
    n = pick(reader(num), pair, oo) * a + o[:, :128] * b
    d = pick(reader(den), pair, oo) * a + o[:, 128:] * b
    put(reader(top), writer(top), new, pair, oo, False)
    put(reader(num), writer(num), n, pair, oo, False)
    put(reader(den), writer(den), d, pair, oo, False)


def keys3(place, x, r4):
    oo = place.offs(1)
    return [oo] + [jnp.concatenate([pick(reader(x, i + 1), 1, oo), r4[i, 0:256]], axis=0) for i in (0, 1)]


def keys4(place, x, r4, r12):
    oo = place.offs(2)
    return [oo] + [
        jnp.concatenate([pick(reader(x, i + 1), 2, oo), r4[i, 256:384], r12[2 + i], r12[i]], axis=0)
        for i in (0, 1)
    ]


def mid_body(info, offsets, counts, x, r4, top_in, num_in, den_in, top, num, den, m3, e3):
    place = Place(info, offsets, counts)
    top[...] = top_in[...]
    num[...] = num_in[...]
    den[...] = den_in[...]
    oo, k2, v2 = keys3(place, x, r4)
    at = [(place.quarter ^ i) * 1024 for i in (0, 1)]
    bias = [jnp.concatenate([place.bias(256, 4, oo[h], b) for b in at], axis=1) for h in (0, 1)]
    es, t, out = attend(pick(reader(x, 0), 1, oo), k2, v2, bias)
    e3[0], e3[1] = es
    m3[...] = t
    merge(top, num, den, t, out, 1, oo)


def far_body(
    info, offsets, counts, x, r4, r12, top_in, num_in, den_in, g0, g1, g2, g3,
    top, norm, mx0, mx1, mx2, mx3, m4, e4, num, den,
):
    place = Place(info, offsets, counts)
    top[...] = top_in[...]
    num[...] = num_in[...]
    den[...] = den_in[...]
    oo, k2, v2 = keys4(place, x, r4, r12)
    at = [(place.quarter ^ i) * 1024 for i in range(4)]
    bias = [jnp.concatenate([place.bias(128, 8, oo[h], b) for b in at], axis=1) for h in (0, 1)]
    es, t, out = attend(pick(reader(x, 0), 2, oo), k2, v2, bias)
    e4[0], e4[1] = es
    m4[...] = t
    merge(top, num, den, t, out, 2, oo)
    outs = (mx0, mx1, mx2, mx3)
    for res in range(8):
        ok = place.valid(res)
        scale = ok / (den[res] + 1.0 - ok)
        norm[res] = scale
        mixed = (num[res] * scale).astype(bf16)
        for slot, mx in enumerate(outs):
            mx[res * 32 : res * 32 + 32] = mixed[slot * 32 : slot * 32 + 32]
    for mx, g in zip(outs, (g0, g1, g2, g3)):
        mx[256:512] = g[...]


def pair_back(place, x, g, top, norm, delta, t, es, pair, oo, k2, v2):
    f2 = jnp.exp(t - pick(reader(top), pair, oo)) * pick(reader(norm), pair, oo)
    gf2 = pick(reader(g), pair, oo).astype(f32) * f2
    fd2 = f2 * pick(reader(delta), pair, oo)
    return back(pick(reader(x, 0), pair, oo), k2, v2, gf2, fd2, es)


def far_back_body(
    info, offsets, counts, x, r4, r12, top, norm, m3, m4, e3, e4, mx0, mx1, mx2, mx3, in0, in1, in2, in3,
    g, delta, acc, d4, d8, d12,
):
    place = Place(info, offsets, counts)
    ri = lax.broadcasted_iota(jnp.int32, (128, 128), 0) >> 6
    ci = lax.broadcasted_iota(jnp.int32, (128, 128), 1) >> 6
    same = jnp.where(ri == ci, 1.0, 0.0)
    for slot, (mx, got) in enumerate(((mx0, in0), (mx1, in1), (mx2, in2), (mx3, in3))):
        sl = slice(slot * 32, slot * 32 + 32)
        rows = got[256:512]
        g[:, sl, :] = rows.reshape(8, 32, 128)
        prod = rows.astype(f32) * mx[0:256].astype(f32)
        sums = lax.dot_general(
            prod, same, (((1,), (0,)), ((), ())), precision=lax.Precision.HIGHEST, preferred_element_type=f32
        )
        delta[:, sl, :] = sums.reshape(8, 32, 128)
    o3, k3, v3 = keys3(place, x, r4)
    o4, k4, v4 = keys4(place, x, r4, r12)
    acc[...] = jnp.zeros_like(acc)
    for pair, oo, k2, v2, m, e, parts in (
        (1, o3, k3, v3, m3, e3, ((d4, 0, 256),)),
        (2, o4, k4, v4, m4, e4, ((d4, 256, 128), (d8, 0, 128), (d12, 0, 128))),
    ):
        grads = pair_back(place, x, g, top, norm, delta, m[...], [e[0], e[1]], pair, oo, k2, v2)
        at_row = m.shape[0]
        for i in range(3):
            put(reader(acc, i), writer(acc, i), grads[i][:at_row], pair, oo, True)
        for ref, start, rows in parts:
            for i in (0, 1):
                ref[i, start : start + rows] = grads[i + 1][at_row : at_row + rows].astype(bf16)
            at_row += rows


def back_two_body(info, offsets, counts, x, g, top, norm, delta, acc_in, m2, e2, acc):
    place = Place(info, offsets, counts)
    acc[...] = acc_in[...]
    oo = place.offs(0)
    k2, v2 = pick(reader(x, 1), 0, oo), pick(reader(x, 2), 0, oo)
    grads = pair_back(place, x, g, top, norm, delta, m2[...], [e2[0], e2[1]], 0, oo, k2, v2)
    for i in range(3):
        put(reader(acc, i), writer(acc, i), grads[i], 0, oo, True)


def back_one_body(info, offsets, counts, x, g, top, norm, delta, acc_in, m1, e1, acc):
    for slot in range(4):
        sl = slice(slot * 32, slot * 32 + 32)
        f2 = jnp.exp(slot_rows(m1, slot) - slot_rows(top, slot)) * slot_rows(norm, slot)
        q2, k2, v2 = [slot_rows(x, slot, i) for i in range(3)]
        g2 = slot_rows(g, slot)
        gf2 = g2.astype(f32) * f2
        fd2 = f2 * slot_rows(delta, slot)
        grads = back(q2, k2, v2, gf2, fd2, [e1[slot, 0], e1[slot, 1]])
        for i in range(3):
            acc[i, :, sl, :] = acc_in[i, :, sl, :] + grads[i].reshape(8, 32, 128)


def cores_body(keep, got, own, s1, s2, s3):
    for d, o in enumerate((own, s1, s2, s3)):
        parts = [keep[4 * u + d] + got[4 * u + d].astype(f32) for u in range(4)]
        o[...] = jnp.concatenate(parts, axis=0).astype(o.dtype)


def quarters_body(a, b, c, d, own, s4, s8, s12):
    one = a[...].astype(f32) + b[...].astype(f32)
    total = one + (c[...].astype(f32) + d[...].astype(f32))
    for u, o in enumerate((own, s4, s8, s12)):
        o[...] = total[72 * u : 72 * u + 72].astype(o.dtype)


def finish_body(info, offsets, counts, acc_in, r4, r8, r12, o0, o1, o2, o3, acc):
    place = Place(info, offsets, counts)
    acc[...] = acc_in[...]
    p3, p4 = place.offs(1), place.offs(2)
    for i in (0, 1):
        rd, wr = reader(acc, i + 1), writer(acc, i + 1)
        put(rd, wr, r4[i, 0:256].astype(f32), 1, p3, True)
        far = r4[i, 256:384].astype(f32) + r8[i].astype(f32) + r12[i].astype(f32)
        put(rd, wr, far, 2, p4, True)
    for slot, o in enumerate((o0, o1, o2, o3)):
        o[0:256] = (slot_rows(acc, slot, 0) * 0.125).astype(bf16)
        o[256:512] = slot_rows(acc, slot, 1).astype(bf16)
        o[512:768] = slot_rows(acc, slot, 2).astype(bf16)


def home_body(info, m0, m1, m2, m3, dq, dk, dv, wide):
    order = row_order(True)
    for d, m in enumerate((m0, m1, m2, m3)):
        c = pl.multiple_of((info[1] ^ d) * 128, 128)
        for i in range(3):
            wide[i, :, pl.ds(c, 128)] = m[256 * i : 256 * i + 256]
    for i, o in enumerate((dq, dk, dv)):
        o[...] = dot_nn(order, wide[i, :, 0:384]).astype(bf16)


def widen(info, msgs, wide):
    for d, m in enumerate(msgs):
        wide[:, pl.ds(pl.multiple_of((info[1] ^ d) * 128, 128), 128)] = m[0:256]


def project_body(info, m0, m1, m2, m3, og, send, keep, wide, both, away):
    widen(info, (m0, m1, m2, m3), wide)
    both[...] = dot_tn(wide[:, 0:384], og[...])
    for s in range(16):
        for t in range(3):
            at = slice(t * 24, t * 24 + 24)
            there = pl.multiple_of((1 - info[2]) * 384 + t * 128, 128)
            here = pl.multiple_of(info[2] * 384 + t * 128, 128)
            away[s ^ info[0], at] = both[s * 24 : s * 24 + 24, pl.ds(there, 128)]
            keep[s ^ info[0], at] = both[s * 24 : s * 24 + 24, pl.ds(here, 128)]
    send[...] = away[...].astype(bf16)


def attended_body(info, m0, m1, m2, m3, w, o, wide):
    widen(info, (m0, m1, m2, m3), wide)
    mixed = dot_nn(row_order(True), wide[:, 0:384]).astype(bf16)
    o[...] = dot_nn(mixed, w[...]).astype(bf16)


def sum_body(a, b, c, d, o):
    one = a[...].astype(f32) + b[...].astype(f32)
    o[...] = (one + (c[...].astype(f32) + d[...].astype(f32))).astype(o.dtype)


def pair_body(a, b, o):
    o[...] = (a[...].astype(f32) + b[...].astype(f32)).astype(o.dtype)


def join_body(info, a, b, o):
    for h, m in enumerate((a, b)):
        for t in range(3):
            col = pl.multiple_of((info[2] ^ h) * 384 + t * 128, 128)
            o[:, pl.ds(col, 128)] = m[24 * t : 24 * t + 24]


smem = pl.BlockSpec(memory_space=pltpu.SMEM)
vmem = pl.BlockSpec(memory_space=pltpu.VMEM)
hbm = pl.BlockSpec(memory_space=pltpu.HBM)


def call(body, scalars, arrays, outs, scratch=(), flops=0, space=vmem, sems=0, limit=12):
    shapes = [jax.ShapeDtypeStruct(s, t) for s, t in outs]
    moved = sum(a.size * a.dtype.itemsize for a in arrays) + sum(s.size * s.dtype.itemsize for s in shapes)
    return pl.pallas_call(
        body,
        out_shape=shapes,
        in_specs=[smem] * len(scalars) + [space] * len(arrays),
        out_specs=[vmem] * len(shapes),
        scratch_shapes=[pltpu.VMEM(s, t) for s, t in scratch] + [pltpu.SemaphoreType.DMA((sems,))] * (sems > 0),
        compiler_params=pltpu.CompilerParams(vmem_limit_bytes=limit * 1024 * 1024),
        cost_estimate=pl.CostEstimate(flops=1000, bytes_accessed=1000, transcendentals=0),
    )(*scalars, *arrays)


def routes(seq_step, keep=None):
    pairs = []
    for dp in range(16):
        for s in range(16):
            t = s ^ seq_step
            if keep is not None and (keep(s, t) & 3) ^ (3 * (dp & 1)) == 3:
                continue
            pairs.append((dp * 16 + s, dp * 16 + t))
    return pairs


def shift(block, pairs):
    return lax.ppermute(block, ("dp", "seq"), pairs)


def dp_step(block, step):
    return lax.ppermute(block, "dp", [(i, i ^ step) for i in range(16)])


def seq_step(block, step):
    return lax.ppermute(block, "seq", [(i, i ^ step) for i in range(16)])


def per_device(queries, keys, values, out_weight, out_grad, offsets, counts):
    seq_rank = lax.axis_index("seq").astype(jnp.int32)
    core = lax.axis_index("dp").astype(jnp.int32) & 1
    info = jnp.stack([seq_rank, (seq_rank & 3) ^ (3 * core), core])
    places = [info, offsets, counts]

    chunk = ((3, 256, 128), bf16)
    third = ((256, 384), bf16)
    cube = (8, 128, 128)
    block = (72, 128)
    active = lambda s, t: s

    msgs = call(
        prep_body,
        [],
        [queries[0], keys[0], values[0]],
        [chunk] * 4,
        [((3, 256, 384), bf16), third, third, third],
        space=hbm,
        sems=3,
        limit=57,
    )
    got = [shift(msgs[d], routes(d)) for d in (1, 2, 3)]
    og, g0, g1, g2, g3, own = call(
        grad_body,
        [info],
        [out_grad[0], out_weight, msgs[0]],
        [((256, 768), bf16)] + [((256, 128), bf16)] * 4 + [chunk],
        [((256, 384), bf16)],
        flops=3 * 10**8,
    )
    x, s4, s8 = call(
        collect_body,
        places,
        [own] + got,
        [((3, *cube), bf16), ((2, 384, 128), bf16), ((2, 128, 128), bf16)],
    )
    r4 = shift(s4, routes(4))
    top, num, den, m1, m2, e1, e2 = call(
        near_body,
        places,
        [x],
        [(cube, f32)] * 4 + [((512, 128), f32), ((4, 2, 256, 256), bf16), ((2, 512, 512), bf16)],
        flops=10**9,
    )
    top, r4 = lax.optimization_barrier((top, r4))
    (s12,) = call(relay_body, [], [s8, r4], [((4, 128, 128), bf16)])
    r12 = shift(s12, routes(12))
    top, s12 = lax.optimization_barrier((top, s12))
    top, num, den, m3, e3 = call(
        mid_body,
        places,
        [x, r4, top, num, den],
        [(cube, f32)] * 3 + [((256, 128), f32), ((2, 256, 512), bf16)],
        flops=10**9,
    )
    top, norm, mx0, mx1, mx2, mx3, m4, e4 = call(
        far_body,
        places,
        [x, r4, r12, top, num, den, g0, g1, g2, g3],
        [(cube, f32)] * 2 + [((512, 128), bf16)] * 4 + [((128, 128), f32), ((2, 128, 512), bf16)],
        [(cube, f32)] * 2,
        flops=10**9,
    )
    mixed = [mx0] + [shift(b, routes(d)) for d, b in ((1, mx1), (2, mx2), (3, mx3))]
    send, keep = call(
        project_body,
        [info],
        mixed + [og],
        [((16, *block), bf16), ((16, *block), f32)],
        [((256, 512), bf16), ((384, 768), f32), ((16, *block), f32)],
        flops=3 * 10**8,
    )
    arrived = dp_step(send, 1)
    keep, *mixed = lax.optimization_barrier([keep] + mixed)
    g, delta, acc, d4, d8, d12 = call(
        far_back_body,
        places,
        [x, r4, r12, top, norm, m3, m4, e3, e4, mx0, mx1, mx2, mx3] + mixed,
        [(cube, bf16), (cube, f32), ((3, *cube), f32)]
        + [((2, 384, 128), bf16), ((2, 128, 128), bf16), ((2, 128, 128), bf16)],
        flops=10**9,
    )
    state = [x, g, top, norm, delta]
    flat = ((288, 128), bf16)
    own, s1, s2, s3 = call(cores_body, [], [keep, arrived], [((288, 128), f32)] + [flat] * 3)
    near = [seq_step(b, d) for d, b in ((1, s1), (2, s2), (3, s3))]
    d4, d8, d12, own = lax.optimization_barrier((d4, d8, d12, own))
    far = [shift(b, routes(d)) for d, b in ((4, d4), (8, d8), (12, d12))]
    (low,) = call(sum_body, [], [own] + near, [flat])
    acc, low = lax.optimization_barrier((acc, low))
    arrived = dp_step(low, 2)
    (acc,) = call(back_two_body, places, state + [acc, m2, e2], [((3, *cube), f32)], flops=10**9)
    acc, low = lax.optimization_barrier((acc, low))
    (low,) = call(pair_body, [], [low, arrived], [flat])
    rest = [dp_step(low, d) for d in (4, 8, 12)]
    acc, low = lax.optimization_barrier((acc, low))
    (acc,) = call(back_one_body, places, state + [acc, m1, e1], [((3, *cube), f32)], flops=10**9)
    acc, low = lax.optimization_barrier((acc, low))
    own, s4, s8, s12 = call(quarters_body, [], [low] + rest, [(block, f32)] + [(block, bf16)] * 3)
    acc, own = lax.optimization_barrier((acc, own))
    outs = call(finish_body, places, [acc] + far, [((768, 128), bf16)] * 4, [((3, *cube), f32)])
    home = [outs[0]] + [shift(outs[d], routes(d)) for d in (1, 2, 3)]
    quarters = [seq_step(b, d) for d, b in ((4, s4), (8, s8), (12, s12))]
    first, *mixed = lax.optimization_barrier([outs[0]] + mixed)
    (attended,) = call(
        attended_body, [info], mixed + [out_weight], [((256, 768), bf16)], [((256, 512), bf16)], flops=3 * 10**8
    )
    first, attended = lax.optimization_barrier((first, attended))
    grads = call(home_body, [info], [first] + home[1:], [third] * 3, [((3, 256, 512), bf16)])
    *grads, own = lax.optimization_barrier([*grads, own])
    (own,) = call(sum_body, [], [own] + quarters, [(block, f32)])
    other = dp_step(own, 1)
    (grad_weight,) = call(join_body, [info], [own, other], [((24, 768), f32)])
    return (attended[None], grads[0][None], grads[1][None], grads[2][None], grad_weight)


def solution(mesh):
    tiles = P("dp", "seq", None)
    return jax.shard_map(
        per_device,
        mesh=mesh,
        in_specs=(tiles, tiles, tiles, P(), tiles, P(), P("dp")),
        out_specs=(tiles, tiles, tiles, tiles, P("seq", None)),
        check_vma=False,
    )
```

```python
import jax
import jax.numpy as jnp
from jax import lax
from jax.experimental import pallas as pl
from jax.experimental.pallas import tpu as pltpu
from jax.sharding import PartitionSpec as P

bf16 = jnp.bfloat16
f32 = jnp.float32
low_bias = -1e30


def dot_nn(a, b):
    return lax.dot_general(a, b, (((1,), (0,)), ((), ())), preferred_element_type=f32)


def dot_nt(a, b):
    return lax.dot_general(a, b, (((1,), (1,)), ((), ())), preferred_element_type=f32)


def dot_tn(a, b):
    return lax.dot_general(a, b, (((0,), (0,)), ((), ())), preferred_element_type=f32)


def first_half(rows):
    return lax.broadcasted_iota(jnp.int32, (rows, 128), 1) < 64


def half_of(x, h):
    m = first_half(x.shape[0])
    z = jnp.zeros_like(x)
    return jnp.where(m, x, z) if h == 0 else jnp.where(m, z, x)


def row_order(back):
    a = lax.broadcasted_iota(jnp.int32, (256, 256), 0 if not back else 1)
    b = lax.broadcasted_iota(jnp.int32, (256, 256), 1 if not back else 0)
    return jnp.where(b == (a & 31) * 8 + (a >> 5), 1.0, 0.0).astype(bf16)


class Place:
    def __init__(self, info, offsets, counts):
        self.j = info[0] & 3
        self.base = (info[0] >> 2) * 1024
        self.quarter = info[0] >> 2
        self.chunk = jnp.minimum(info[1], 2)
        self.count = counts[0]
        self.offsets = offsets

    def offs(self, pair):
        r = 2 << pair
        return [self.offsets[pair, 2 * self.chunk + h] & (r - 1) for h in (0, 1)]

    def bias(self, n, step, o, base):
        kk = lax.broadcasted_iota(jnp.int32, (1, n), 1)
        pos = base + ((self.j ^ ((kk >> 5) & 3)) << 8) + (kk & 31) * 8 + o + step * (kk >> 7)
        return jnp.where(pos < self.count, 0.0, low_bias)

    def bias_slot(self, slot):
        kk = lax.broadcasted_iota(jnp.int32, (1, 256), 1)
        pos = self.base + ((self.j ^ slot) << 8) + (kk & 31) * 8 + (kk >> 5)
        return jnp.where(pos < self.count, 0.0, low_bias)

    def valid(self, res):
        rr = lax.broadcasted_iota(jnp.int32, (128, 128), 0)
        pos = self.base + ((self.j ^ (rr >> 5)) << 8) + (rr & 31) * 8 + res
        return jnp.where(pos < self.count, 1.0, 0.0)


def pick(read, pair, oo):
    r = 2 << pair
    m = first_half(128)
    parts = [jnp.where(m, read(oo[0] + r * i), read(oo[1] + r * i)) for i in range(8 // r)]
    return parts[0] if len(parts) == 1 else jnp.concatenate(parts, axis=0)


def put(read, write, val, pair, oo, add):
    r = 2 << pair
    m = first_half(128)
    for i in range(8 // r):
        blk = val[i * 128 : (i + 1) * 128]
        for h in (0, 1):
            mine = m if h == 0 else ~m
            old = read(oo[h] + r * i)
            write(oo[h] + r * i, jnp.where(mine, old + blk if add else blk, old))


def reader(ref, *lead):
    return lambda i: ref[(*lead, i)]


def writer(ref, *lead):
    def w(i, val):
        ref[(*lead, i)] = val

    return w


def slot_rows(ref, slot, *lead):
    return ref[(*lead, slice(None), slice(slot * 32, slot * 32 + 32), slice(None))].reshape(256, 128)


def attend(q2, k2, v2, bias):
    nk = k2.shape[0]
    out, es, ms = None, [], []
    one = jnp.ones((nk, 128), bf16)
    for h in (0, 1):
        s = dot_nt(q2, half_of(k2, h)) + bias[h]
        m = jnp.max(s, axis=1, keepdims=True)
        e = jnp.exp(s - m).astype(bf16)
        o = dot_nn(e, jnp.concatenate([half_of(v2, h), half_of(one, h)], axis=1))
        out = o if out is None else out + o
        es.append(e)
        ms.append(m)
    n = q2.shape[0]
    top = jnp.where(first_half(n), jnp.broadcast_to(ms[0], (n, 128)), jnp.broadcast_to(ms[1], (n, 128)))
    return es, top, out


def back(q2, k2, v2, gf2, fd2, es):
    low = gf2.astype(bf16)
    qt, gt = q2.astype(f32).T.astype(bf16), gf2.T.astype(bf16)
    dq, dks, dvs = None, [], []
    for h in (0, 1):
        e, at = es[h], slice(64 * h, 64 * h + 64)
        dp = dot_nt(low, half_of(v2, h))
        ds = (e.astype(f32) * (dp - fd2[:, 64 * h : 64 * h + 1])).astype(bf16)
        a = dot_nn(ds, half_of(k2, h))
        dq = a if dq is None else dq + a
        dks.append(dot_nn(qt[at], ds))
        dvs.append(dot_nn(gt[at], e))
    return dq, jnp.concatenate(dks, axis=0).T, jnp.concatenate(dvs, axis=0).T


def copies(pairs, sems):
    moves = [pltpu.make_async_copy(src, dst, sems.at[i]) for i, (src, dst) in enumerate(pairs)]
    for m in moves:
        m.start()
    return moves


def prep_body(q_in, k_in, v_in, o0, o1, o2, o3, px, q, k, v, sems):
    moves = copies(((q_in, q), (k_in, k), (v_in, v)), sems)
    chunk = (lax.axis_index("seq") & 3) ^ (3 * (lax.axis_index("dp") & 1))
    order = row_order(False)
    for i, src in enumerate((q, k, v)):
        moves[i].wait()
        rows = dot_nn(order, src[...])
        px[i] = (rows * 0.125 if i == 0 else rows).astype(bf16)
    for d, o in enumerate((o0, o1, o2, o3)):
        c = pl.multiple_of(jnp.minimum(chunk ^ d, 2) * 128, 128)
        for i in range(3):
            o[i] = px[i, :, pl.ds(c, 128)]


def grad_body(info, og, w, m_in, og_out, o0, o1, o2, o3, m_out, gx):
    m_out[...] = m_in[...]
    ordered = dot_nn(row_order(False), og[...]).astype(bf16)
    og_out[...] = ordered
    gx[...] = dot_nt(ordered, w[...]).astype(bf16)
    for d, o in enumerate((o0, o1, o2, o3)):
        o[...] = gx[:, pl.ds(pl.multiple_of(jnp.minimum(info[1] ^ d, 2) * 128, 128), 128)]


def collect_body(info, offsets, counts, m0, m1, m2, m3, x, s4, s8):
    place = Place(info, offsets, counts)
    for slot, m in enumerate((m0, m1, m2, m3)):
        for i in range(3):
            x[i, :, slot * 32 : slot * 32 + 32, :] = m[i].reshape(8, 32, 128)
    o3, o4 = place.offs(1), place.offs(2)
    for i in (0, 1):
        s4[i, 0:256] = pick(reader(x, i + 1), 1, o3)
        last = pick(reader(x, i + 1), 2, o4)
        s4[i, 256:384] = last
        s8[i] = last


def relay_body(s8, r4, o):
    for i in (0, 1):
        o[i] = s8[i]
        o[2 + i] = r4[i, 256:384]


def near_body(
    info, offsets, counts, x, top, num, den, m1, m2, e1, e2,
):
    place = Place(info, offsets, counts)
    for slot in range(4):
        b = place.bias_slot(slot)
        sl = slice(slot * 32, slot * 32 + 32)
        es, t, o = attend(*[slot_rows(x, slot, i) for i in range(3)], [b, b])
        e1[slot, 0], e1[slot, 1] = es
        t = t.reshape(8, 32, 128)
        top[:, sl, :] = t
        m1[:, sl, :] = t
        num[:, sl, :] = o[:, :128].reshape(8, 32, 128)
        den[:, sl, :] = o[:, 128:].reshape(8, 32, 128)
    oo = place.offs(0)
    q2, k2, v2 = [pick(reader(x, i), 0, oo) for i in range(3)]
    bias = [place.bias(512, 2, oo[h], place.base) for h in (0, 1)]
    es, t, o = attend(q2, k2, v2, bias)
    e2[0], e2[1] = es
    m2[...] = t
    merge(top, num, den, t, o, 0, oo)


def merge(top, num, den, t, o, pair, oo):
    old = pick(reader(top), pair, oo)
    new = jnp.maximum(old, t)
    a, b = jnp.exp(old - new), jnp.exp(t - new)
    n = pick(reader(num), pair, oo) * a + o[:, :128] * b
    d = pick(reader(den), pair, oo) * a + o[:, 128:] * b
    put(reader(top), writer(top), new, pair, oo, False)
    put(reader(num), writer(num), n, pair, oo, False)
    put(reader(den), writer(den), d, pair, oo, False)


def keys3(place, x, r4):
    oo = place.offs(1)
    return [oo] + [jnp.concatenate([pick(reader(x, i + 1), 1, oo), r4[i, 0:256]], axis=0) for i in (0, 1)]


def keys4(place, x, r4, r12):
    oo = place.offs(2)
    return [oo] + [
        jnp.concatenate([pick(reader(x, i + 1), 2, oo), r4[i, 256:384], r12[2 + i], r12[i]], axis=0)
        for i in (0, 1)
    ]


def mid_body(info, offsets, counts, x, r4, top_in, num_in, den_in, top, num, den, m3, e3):
    place = Place(info, offsets, counts)
    top[...] = top_in[...]
    num[...] = num_in[...]
    den[...] = den_in[...]
    oo, k2, v2 = keys3(place, x, r4)
    at = [(place.quarter ^ i) * 1024 for i in (0, 1)]
    bias = [jnp.concatenate([place.bias(256, 4, oo[h], b) for b in at], axis=1) for h in (0, 1)]
    es, t, out = attend(pick(reader(x, 0), 1, oo), k2, v2, bias)
    e3[0], e3[1] = es
    m3[...] = t
    merge(top, num, den, t, out, 1, oo)


def far_body(
    info, offsets, counts, x, r4, r12, top_in, num_in, den_in, g0, g1, g2, g3,
    top, norm, mx0, mx1, mx2, mx3, m4, e4, num, den,
):
    place = Place(info, offsets, counts)
    top[...] = top_in[...]
    num[...] = num_in[...]
    den[...] = den_in[...]
    oo, k2, v2 = keys4(place, x, r4, r12)
    at = [(place.quarter ^ i) * 1024 for i in range(4)]
    bias = [jnp.concatenate([place.bias(128, 8, oo[h], b) for b in at], axis=1) for h in (0, 1)]
    es, t, out = attend(pick(reader(x, 0), 2, oo), k2, v2, bias)
    e4[0], e4[1] = es
    m4[...] = t
    merge(top, num, den, t, out, 2, oo)
    outs = (mx0, mx1, mx2, mx3)
    for res in range(8):
        ok = place.valid(res)
        scale = ok / (den[res] + 1.0 - ok)
        norm[res] = scale
        mixed = (num[res] * scale).astype(bf16)
        for slot, mx in enumerate(outs):
            mx[res * 32 : res * 32 + 32] = mixed[slot * 32 : slot * 32 + 32]
    for mx, g in zip(outs, (g0, g1, g2, g3)):
        mx[256:512] = g[...]


def pair_back(place, x, g, top, norm, delta, t, es, pair, oo, k2, v2):
    f2 = jnp.exp(t - pick(reader(top), pair, oo)) * pick(reader(norm), pair, oo)
    gf2 = pick(reader(g), pair, oo).astype(f32) * f2
    fd2 = f2 * pick(reader(delta), pair, oo)
    return back(pick(reader(x, 0), pair, oo), k2, v2, gf2, fd2, es)


def far_back_body(
    info, offsets, counts, x, r4, r12, top, norm, m3, m4, e3, e4, mx0, mx1, mx2, mx3, in0, in1, in2, in3,
    g, delta, acc, d4, d8, d12,
):
    place = Place(info, offsets, counts)
    ri = lax.broadcasted_iota(jnp.int32, (128, 128), 0) >> 6
    ci = lax.broadcasted_iota(jnp.int32, (128, 128), 1) >> 6
    same = jnp.where(ri == ci, 1.0, 0.0)
    for slot, (mx, got) in enumerate(((mx0, in0), (mx1, in1), (mx2, in2), (mx3, in3))):
        sl = slice(slot * 32, slot * 32 + 32)
        rows = got[256:512]
        g[:, sl, :] = rows.reshape(8, 32, 128)
        prod = rows.astype(f32) * mx[0:256].astype(f32)
        sums = lax.dot_general(
            prod, same, (((1,), (0,)), ((), ())), precision=lax.Precision.HIGHEST, preferred_element_type=f32
        )
        delta[:, sl, :] = sums.reshape(8, 32, 128)
    o3, k3, v3 = keys3(place, x, r4)
    o4, k4, v4 = keys4(place, x, r4, r12)
    acc[...] = jnp.zeros_like(acc)
    for pair, oo, k2, v2, m, e, parts in (
        (1, o3, k3, v3, m3, e3, ((d4, 0, 256),)),
        (2, o4, k4, v4, m4, e4, ((d4, 256, 128), (d8, 0, 128), (d12, 0, 128))),
    ):
        grads = pair_back(place, x, g, top, norm, delta, m[...], [e[0], e[1]], pair, oo, k2, v2)
        at_row = m.shape[0]
        for i in range(3):
            put(reader(acc, i), writer(acc, i), grads[i][:at_row], pair, oo, True)
        for ref, start, rows in parts:
            for i in (0, 1):
                ref[i, start : start + rows] = grads[i + 1][at_row : at_row + rows].astype(bf16)
            at_row += rows


def back_two_body(info, offsets, counts, x, g, top, norm, delta, acc_in, m2, e2, acc):
    place = Place(info, offsets, counts)
    acc[...] = acc_in[...]
    oo = place.offs(0)
    k2, v2 = pick(reader(x, 1), 0, oo), pick(reader(x, 2), 0, oo)
    grads = pair_back(place, x, g, top, norm, delta, m2[...], [e2[0], e2[1]], 0, oo, k2, v2)
    for i in range(3):
        put(reader(acc, i), writer(acc, i), grads[i], 0, oo, True)


def back_one_body(info, offsets, counts, x, g, top, norm, delta, acc_in, m1, e1, acc):
    for slot in range(4):
        sl = slice(slot * 32, slot * 32 + 32)
        f2 = jnp.exp(slot_rows(m1, slot) - slot_rows(top, slot)) * slot_rows(norm, slot)
        q2, k2, v2 = [slot_rows(x, slot, i) for i in range(3)]
        g2 = slot_rows(g, slot)
        gf2 = g2.astype(f32) * f2
        fd2 = f2 * slot_rows(delta, slot)
        grads = back(q2, k2, v2, gf2, fd2, [e1[slot, 0], e1[slot, 1]])
        for i in range(3):
            acc[i, :, sl, :] = acc_in[i, :, sl, :] + grads[i].reshape(8, 32, 128)


def cores_body(keep, got, own, s1, s2, s3):
    for d, o in enumerate((own, s1, s2, s3)):
        parts = [keep[4 * u + d] + got[4 * u + d].astype(f32) for u in range(4)]
        o[...] = jnp.concatenate(parts, axis=0).astype(o.dtype)


def halves_body(mine, other, own, s4, s8, s12):
    a, b = mine[...].astype(f32), other[...].astype(f32)
    for u, o in enumerate((own, s4, s8, s12)):
        at = slice(72 * u, 72 * u + 72)
        o[...] = jnp.concatenate([a[at], b[at]], axis=0).astype(o.dtype)


def finish_body(info, offsets, counts, acc_in, r4, r8, r12, o0, o1, o2, o3, acc):
    place = Place(info, offsets, counts)
    acc[...] = acc_in[...]
    p3, p4 = place.offs(1), place.offs(2)
    for i in (0, 1):
        rd, wr = reader(acc, i + 1), writer(acc, i + 1)
        put(rd, wr, r4[i, 0:256].astype(f32), 1, p3, True)
        far = r4[i, 256:384].astype(f32) + r8[i].astype(f32) + r12[i].astype(f32)
        put(rd, wr, far, 2, p4, True)
    for slot, o in enumerate((o0, o1, o2, o3)):
        o[0:256] = (slot_rows(acc, slot, 0) * 0.125).astype(bf16)
        o[256:512] = slot_rows(acc, slot, 1).astype(bf16)
        o[512:768] = slot_rows(acc, slot, 2).astype(bf16)


def home_body(info, m0, m1, m2, m3, dq, dk, dv, wide):
    order = row_order(True)
    for d, m in enumerate((m0, m1, m2, m3)):
        c = pl.multiple_of((info[1] ^ d) * 128, 128)
        for i in range(3):
            wide[i, :, pl.ds(c, 128)] = m[256 * i : 256 * i + 256]
    for i, o in enumerate((dq, dk, dv)):
        o[...] = dot_nn(order, wide[i, :, 0:384]).astype(bf16)


def widen(info, msgs, wide):
    for d, m in enumerate(msgs):
        wide[:, pl.ds(pl.multiple_of((info[1] ^ d) * 128, 128), 128)] = m[0:256]


def project_body(info, m0, m1, m2, m3, og, send, keep, wide, both, away):
    widen(info, (m0, m1, m2, m3), wide)
    both[...] = dot_tn(wide[:, 0:384], og[...])
    for s in range(16):
        for t in range(3):
            at = slice(t * 24, t * 24 + 24)
            there = pl.multiple_of((1 - info[2]) * 384 + t * 128, 128)
            here = pl.multiple_of(info[2] * 384 + t * 128, 128)
            away[s ^ info[0], at] = both[s * 24 : s * 24 + 24, pl.ds(there, 128)]
            keep[s ^ info[0], at] = both[s * 24 : s * 24 + 24, pl.ds(here, 128)]
    send[...] = away[...].astype(bf16)


def attended_body(info, m0, m1, m2, m3, w, o, wide):
    widen(info, (m0, m1, m2, m3), wide)
    mixed = dot_nn(row_order(True), wide[:, 0:384]).astype(bf16)
    o[...] = dot_nn(mixed, w[...]).astype(bf16)


def sum_body(a, b, c, d, o):
    one = a[...].astype(f32) + b[...].astype(f32)
    o[...] = (one + (c[...].astype(f32) + d[...].astype(f32))).astype(o.dtype)


def pair_body(a, b, o):
    o[...] = (a[...].astype(f32) + b[...].astype(f32)).astype(o.dtype)


def join_body(info, own, a, b, c, o):
    total = own[...] + a[...].astype(f32) + (b[...].astype(f32) + c[...].astype(f32))
    for h in (0, 1):
        for t in range(3):
            col = pl.multiple_of((info[2] ^ h) * 384 + t * 128, 128)
            o[:, pl.ds(col, 128)] = total[72 * h + 24 * t : 72 * h + 24 * t + 24]


smem = pl.BlockSpec(memory_space=pltpu.SMEM)
vmem = pl.BlockSpec(memory_space=pltpu.VMEM)
hbm = pl.BlockSpec(memory_space=pltpu.HBM)


def call(body, scalars, arrays, outs, scratch=(), cost=1000, space=vmem, sems=0, limit=12):
    shapes = [jax.ShapeDtypeStruct(s, t) for s, t in outs]
    return pl.pallas_call(
        body,
        out_shape=shapes,
        in_specs=[smem] * len(scalars) + [space] * len(arrays),
        out_specs=[vmem] * len(shapes),
        scratch_shapes=[pltpu.VMEM(s, t) for s, t in scratch] + [pltpu.SemaphoreType.DMA((sems,))] * (sems > 0),
        compiler_params=pltpu.CompilerParams(vmem_limit_bytes=limit * 1024 * 1024),
        cost_estimate=pl.CostEstimate(flops=cost, bytes_accessed=1000, transcendentals=0),
    )(*scalars, *arrays)


def routes(seq_step, keep=None):
    pairs = []
    for dp in range(16):
        for s in range(16):
            t = s ^ seq_step
            if keep is not None and (keep(s, t) & 3) ^ (3 * (dp & 1)) == 3:
                continue
            pairs.append((dp * 16 + s, dp * 16 + t))
    return pairs


def shift(block, pairs):
    return lax.ppermute(block, ("dp", "seq"), pairs)


def dp_step(block, step):
    return lax.ppermute(block, "dp", [(i, i ^ step) for i in range(16)])


def seq_step(block, step):
    return lax.ppermute(block, "seq", [(i, i ^ step) for i in range(16)])


def per_device(queries, keys, values, out_weight, out_grad, offsets, counts):
    seq_rank = lax.axis_index("seq").astype(jnp.int32)
    core = lax.axis_index("dp").astype(jnp.int32) & 1
    info = jnp.stack([seq_rank, (seq_rank & 3) ^ (3 * core), core])
    places = [info, offsets, counts]

    chunk = ((3, 256, 128), bf16)
    third = ((256, 384), bf16)
    cube = (8, 128, 128)
    block = (72, 128)
    active = lambda s, t: s

    msgs = call(
        prep_body,
        [],
        [queries[0], keys[0], values[0]],
        [chunk] * 4,
        [((3, 256, 384), bf16), third, third, third],
        space=hbm,
        sems=3,
        limit=57,
    )
    got = [shift(msgs[d], routes(d)) for d in (1, 2, 3)]
    og, g0, g1, g2, g3, own = call(
        grad_body,
        [info],
        [out_grad[0], out_weight, msgs[0]],
        [((256, 768), bf16)] + [((256, 128), bf16)] * 4 + [chunk],
        [((256, 384), bf16)],
    )
    x, s4, s8 = call(
        collect_body,
        places,
        [own] + got,
        [((3, *cube), bf16), ((2, 384, 128), bf16), ((2, 128, 128), bf16)],
    )
    r4 = shift(s4, routes(4))
    top, num, den, m1, m2, e1, e2 = call(
        near_body,
        places,
        [x],
        [(cube, f32)] * 4 + [((512, 128), f32), ((4, 2, 256, 256), bf16), ((2, 512, 512), bf16)],
    )
    top, r4 = lax.optimization_barrier((top, r4))
    (s12,) = call(relay_body, [], [s8, r4], [((4, 128, 128), bf16)])
    r12 = shift(s12, routes(12))
    top, s12 = lax.optimization_barrier((top, s12))
    top, num, den, m3, e3 = call(
        mid_body,
        places,
        [x, r4, top, num, den],
        [(cube, f32)] * 3 + [((256, 128), f32), ((2, 256, 512), bf16)],
    )
    top, norm, mx0, mx1, mx2, mx3, m4, e4 = call(
        far_body,
        places,
        [x, r4, r12, top, num, den, g0, g1, g2, g3],
        [(cube, f32)] * 2 + [((512, 128), bf16)] * 4 + [((128, 128), f32), ((2, 128, 512), bf16)],
        [(cube, f32)] * 2,
    )
    mixed = [mx0] + [shift(b, routes(d)) for d, b in ((1, mx1), (2, mx2), (3, mx3))]
    send, keep = call(
        project_body,
        [info],
        mixed + [og],
        [((16, *block), bf16), ((16, *block), f32)],
        [((256, 512), bf16), ((384, 768), f32), ((16, *block), f32)],
    )
    arrived = dp_step(send, 1)
    keep, *mixed = lax.optimization_barrier([keep] + mixed)
    g, delta, acc, d4, d8, d12 = call(
        far_back_body,
        places,
        [x, r4, r12, top, norm, m3, m4, e3, e4, mx0, mx1, mx2, mx3] + mixed,
        [(cube, bf16), (cube, f32), ((3, *cube), f32)]
        + [((2, 384, 128), bf16), ((2, 128, 128), bf16), ((2, 128, 128), bf16)],
    )
    state = [x, g, top, norm, delta]
    (attended,) = call(
        attended_body, [info], mixed + [out_weight], [((256, 768), bf16)], [((256, 512), bf16)]
    )
    attended, keep = lax.optimization_barrier((attended, keep))
    flat = ((288, 128), bf16)
    own, s1, s2, s3 = call(cores_body, [], [keep, arrived], [((288, 128), f32)] + [flat] * 3)
    near = [seq_step(b, d) for d, b in ((1, s1), (2, s2), (3, s3))]
    d4, d8, d12, own = lax.optimization_barrier((d4, d8, d12, own))
    far = [shift(b, routes(d)) for d, b in ((4, d4), (8, d8), (12, d12))]
    (low,) = call(sum_body, [], [own] + near, [flat])
    acc, low = lax.optimization_barrier((acc, low))
    arrived = dp_step(low, 2)
    (acc,) = call(back_two_body, places, state + [acc, m2, e2], [((3, *cube), f32)])
    acc, low = lax.optimization_barrier((acc, low))
    (low,) = call(pair_body, [], [low, arrived], [flat])
    rest = [dp_step(low, d) for d in (4, 8, 12)]
    acc, low = lax.optimization_barrier((acc, low))
    (acc,) = call(back_one_body, places, state + [acc, m1, e1], [((3, *cube), f32)])
    acc, low = lax.optimization_barrier((acc, low))
    (low,) = call(sum_body, [], [low] + rest, [flat])
    acc, low = lax.optimization_barrier((acc, low))
    other = dp_step(low, 1)
    outs = call(
        finish_body, places, [acc] + far, [((768, 128), bf16)] * 4, [((3, *cube), f32)], cost=2 * 10**9
    )
    *outs, other = lax.optimization_barrier([*outs, other])
    home = [outs[0]] + [shift(outs[d], routes(d)) for d in (1, 2, 3)]
    both = (144, 128)
    own, s4, s8, s12 = call(halves_body, [], [low, other], [(both, f32)] + [(both, bf16)] * 3)
    quarters = [seq_step(b, d) for d, b in ((4, s4), (8, s8), (12, s12))]
    grads = call(home_body, [info], home, [third] * 3, [((3, 256, 512), bf16)])
    *grads, own = lax.optimization_barrier([*grads, own])
    (grad_weight,) = call(join_body, [info], [own] + quarters, [((24, 768), f32)])
    return (attended[None], grads[0][None], grads[1][None], grads[2][None], grad_weight)


def solution(mesh):
    tiles = P("dp", "seq", None)
    return jax.shard_map(
        per_device,
        mesh=mesh,
        in_specs=(tiles, tiles, tiles, P(), tiles, P(), P("dp")),
        out_specs=(tiles, tiles, tiles, tiles, P("seq", None)),
        check_vma=False,
    )
```

```python
import jax
import jax.numpy as jnp
from jax import lax
from jax.experimental import pallas as pl
from jax.experimental.pallas import tpu as pltpu
from jax.sharding import PartitionSpec as P

bf16 = jnp.bfloat16
f32 = jnp.float32
low_bias = -1e30


def dot_nn(a, b):
    return lax.dot_general(a, b, (((1,), (0,)), ((), ())), preferred_element_type=f32)


def dot_nt(a, b):
    return lax.dot_general(a, b, (((1,), (1,)), ((), ())), preferred_element_type=f32)


def dot_tn(a, b):
    return lax.dot_general(a, b, (((0,), (0,)), ((), ())), preferred_element_type=f32)


def first_half(rows):
    return lax.broadcasted_iota(jnp.int32, (rows, 128), 1) < 64


def half_of(x, h):
    m = first_half(x.shape[0])
    z = jnp.zeros_like(x)
    return jnp.where(m, x, z) if h == 0 else jnp.where(m, z, x)


def row_order(back):
    a = lax.broadcasted_iota(jnp.int32, (256, 256), 0 if not back else 1)
    b = lax.broadcasted_iota(jnp.int32, (256, 256), 1 if not back else 0)
    return jnp.where(b == (a & 31) * 8 + (a >> 5), 1.0, 0.0).astype(bf16)


class Place:
    def __init__(self, info, offsets, counts):
        self.j = info[0] & 3
        self.base = (info[0] >> 2) * 1024
        self.quarter = info[0] >> 2
        self.chunk = jnp.minimum(info[1], 2)
        self.count = counts[0]
        self.offsets = offsets

    def offs(self, pair):
        r = 2 << pair
        return [self.offsets[pair, 2 * self.chunk + h] & (r - 1) for h in (0, 1)]

    def bias(self, n, step, o, base):
        kk = lax.broadcasted_iota(jnp.int32, (1, n), 1)
        pos = base + ((self.j ^ ((kk >> 5) & 3)) << 8) + (kk & 31) * 8 + o + step * (kk >> 7)
        return jnp.where(pos < self.count, 0.0, low_bias)

    def bias_slot(self, slot):
        kk = lax.broadcasted_iota(jnp.int32, (1, 256), 1)
        pos = self.base + ((self.j ^ slot) << 8) + (kk & 31) * 8 + (kk >> 5)
        return jnp.where(pos < self.count, 0.0, low_bias)

    def valid(self, res):
        rr = lax.broadcasted_iota(jnp.int32, (128, 128), 0)
        pos = self.base + ((self.j ^ (rr >> 5)) << 8) + (rr & 31) * 8 + res
        return jnp.where(pos < self.count, 1.0, 0.0)


def pick(read, pair, oo):
    r = 2 << pair
    m = first_half(128)
    parts = [jnp.where(m, read(oo[0] + r * i), read(oo[1] + r * i)) for i in range(8 // r)]
    return parts[0] if len(parts) == 1 else jnp.concatenate(parts, axis=0)


def put(read, write, val, pair, oo, add):
    r = 2 << pair
    m = first_half(128)
    for i in range(8 // r):
        blk = val[i * 128 : (i + 1) * 128]
        for h in (0, 1):
            mine = m if h == 0 else ~m
            old = read(oo[h] + r * i)
            write(oo[h] + r * i, jnp.where(mine, old + blk if add else blk, old))


def reader(ref, *lead):
    return lambda i: ref[(*lead, i)]


def writer(ref, *lead):
    def w(i, val):
        ref[(*lead, i)] = val

    return w


def slot_rows(ref, slot, *lead):
    return ref[(*lead, slice(None), slice(slot * 32, slot * 32 + 32), slice(None))].reshape(256, 128)


def attend(q2, k2, v2, bias):
    nk = k2.shape[0]
    out, es, ms = None, [], []
    one = jnp.ones((nk, 128), bf16)
    for h in (0, 1):
        s = dot_nt(q2, half_of(k2, h)) + bias[h]
        m = jnp.max(s, axis=1, keepdims=True)
        e = jnp.exp(s - m).astype(bf16)
        o = dot_nn(e, jnp.concatenate([half_of(v2, h), half_of(one, h)], axis=1))
        out = o if out is None else out + o
        es.append(e)
        ms.append(m)
    n = q2.shape[0]
    top = jnp.where(first_half(n), jnp.broadcast_to(ms[0], (n, 128)), jnp.broadcast_to(ms[1], (n, 128)))
    return es, top, out


def back(q2, k2, v2, gf2, fd2, es):
    low = gf2.astype(bf16)
    qt, gt = q2.astype(f32).T.astype(bf16), gf2.T.astype(bf16)
    dq, dks, dvs = None, [], []
    for h in (0, 1):
        e, at = es[h], slice(64 * h, 64 * h + 64)
        dp = dot_nt(low, half_of(v2, h))
        ds = (e.astype(f32) * (dp - fd2[:, 64 * h : 64 * h + 1])).astype(bf16)
        a = dot_nn(ds, half_of(k2, h))
        dq = a if dq is None else dq + a
        dks.append(dot_nn(qt[at], ds))
        dvs.append(dot_nn(gt[at], e))
    return dq, jnp.concatenate(dks, axis=0).T, jnp.concatenate(dvs, axis=0).T


def copies(pairs, sems):
    moves = [pltpu.make_async_copy(src, dst, sems.at[i]) for i, (src, dst) in enumerate(pairs)]
    for m in moves:
        m.start()
    return moves


def prep_body(q_in, k_in, v_in, o0, o1, o2, o3, px, q, k, v, sems):
    moves = copies(((q_in, q), (k_in, k), (v_in, v)), sems)
    chunk = (lax.axis_index("seq") & 3) ^ (3 * (lax.axis_index("dp") & 1))
    order = row_order(False)
    for i, src in enumerate((q, k, v)):
        moves[i].wait()
        rows = dot_nn(order, src[...])
        px[i] = (rows * 0.125 if i == 0 else rows).astype(bf16)
    for d, o in enumerate((o0, o1, o2, o3)):
        c = pl.multiple_of(jnp.minimum(chunk ^ d, 2) * 128, 128)
        for i in range(3):
            o[i] = px[i, :, pl.ds(c, 128)]


def grad_body(info, og, w, m_in, og_out, o0, o1, o2, o3, m_out, gx):
    m_out[...] = m_in[...]
    ordered = dot_nn(row_order(False), og[...]).astype(bf16)
    og_out[...] = ordered
    gx[...] = dot_nt(ordered, w[...]).astype(bf16)
    for d, o in enumerate((o0, o1, o2, o3)):
        o[...] = gx[:, pl.ds(pl.multiple_of(jnp.minimum(info[1] ^ d, 2) * 128, 128), 128)]


def collect_body(info, offsets, counts, m0, m1, m2, m3, x, s3, s8):
    place = Place(info, offsets, counts)
    for slot, m in enumerate((m0, m1, m2, m3)):
        for i in range(3):
            x[i, :, slot * 32 : slot * 32 + 32, :] = m[i].reshape(8, 32, 128)
    o3, o4 = place.offs(1), place.offs(2)
    for i in (0, 1):
        s3[i] = pick(reader(x, i + 1), 1, o3)
        s8[i] = pick(reader(x, i + 1), 2, o4)


def relay_body(s8, r4, o):
    for i in (0, 1):
        o[i] = s8[i]
        o[2 + i] = r4[i]


def near_body(
    info, offsets, counts, x, top, num, den, m1, m2, e1, e2,
):
    place = Place(info, offsets, counts)
    for slot in range(4):
        b = place.bias_slot(slot)
        sl = slice(slot * 32, slot * 32 + 32)
        es, t, o = attend(*[slot_rows(x, slot, i) for i in range(3)], [b, b])
        e1[slot, 0], e1[slot, 1] = es
        t = t.reshape(8, 32, 128)
        top[:, sl, :] = t
        m1[:, sl, :] = t
        num[:, sl, :] = o[:, :128].reshape(8, 32, 128)
        den[:, sl, :] = o[:, 128:].reshape(8, 32, 128)
    oo = place.offs(0)
    q2, k2, v2 = [pick(reader(x, i), 0, oo) for i in range(3)]
    bias = [place.bias(512, 2, oo[h], place.base) for h in (0, 1)]
    es, t, o = attend(q2, k2, v2, bias)
    e2[0], e2[1] = es
    m2[...] = t
    merge(top, num, den, t, o, 0, oo)


def merge(top, num, den, t, o, pair, oo):
    old = pick(reader(top), pair, oo)
    new = jnp.maximum(old, t)
    a, b = jnp.exp(old - new), jnp.exp(t - new)
    n = pick(reader(num), pair, oo) * a + o[:, :128] * b
    d = pick(reader(den), pair, oo) * a + o[:, 128:] * b
    put(reader(top), writer(top), new, pair, oo, False)
    put(reader(num), writer(num), n, pair, oo, False)
    put(reader(den), writer(den), d, pair, oo, False)


def keys3(place, x, r3):
    oo = place.offs(1)
    return [oo] + [jnp.concatenate([pick(reader(x, i + 1), 1, oo), r3[i]], axis=0) for i in (0, 1)]


def keys4(place, x, r4, r12):
    oo = place.offs(2)
    return [oo] + [
        jnp.concatenate([pick(reader(x, i + 1), 2, oo), r4[i], r12[2 + i], r12[i]], axis=0)
        for i in (0, 1)
    ]


def mid_body(info, offsets, counts, x, r3, top_in, num_in, den_in, top, num, den, m3, e3):
    place = Place(info, offsets, counts)
    top[...] = top_in[...]
    num[...] = num_in[...]
    den[...] = den_in[...]
    oo, k2, v2 = keys3(place, x, r3)
    at = [(place.quarter ^ i) * 1024 for i in (0, 1)]
    bias = [jnp.concatenate([place.bias(256, 4, oo[h], b) for b in at], axis=1) for h in (0, 1)]
    es, t, out = attend(pick(reader(x, 0), 1, oo), k2, v2, bias)
    e3[0], e3[1] = es
    m3[...] = t
    merge(top, num, den, t, out, 1, oo)


def far_body(
    info, offsets, counts, x, r4, r12, top_in, num_in, den_in, g0, g1, g2, g3,
    top, norm, mx0, mx1, mx2, mx3, m4, e4, num, den,
):
    place = Place(info, offsets, counts)
    top[...] = top_in[...]
    num[...] = num_in[...]
    den[...] = den_in[...]
    oo, k2, v2 = keys4(place, x, r4, r12)
    at = [(place.quarter ^ i) * 1024 for i in range(4)]
    bias = [jnp.concatenate([place.bias(128, 8, oo[h], b) for b in at], axis=1) for h in (0, 1)]
    es, t, out = attend(pick(reader(x, 0), 2, oo), k2, v2, bias)
    e4[0], e4[1] = es
    m4[...] = t
    merge(top, num, den, t, out, 2, oo)
    outs = (mx0, mx1, mx2, mx3)
    for res in range(8):
        ok = place.valid(res)
        scale = ok / (den[res] + 1.0 - ok)
        norm[res] = scale
        mixed = (num[res] * scale).astype(bf16)
        for slot, mx in enumerate(outs):
            mx[res * 32 : res * 32 + 32] = mixed[slot * 32 : slot * 32 + 32]
    for mx, g in zip(outs, (g0, g1, g2, g3)):
        mx[256:512] = g[...]


def pair_back(place, x, g, top, norm, delta, t, es, pair, oo, k2, v2):
    f2 = jnp.exp(t - pick(reader(top), pair, oo)) * pick(reader(norm), pair, oo)
    gf2 = pick(reader(g), pair, oo).astype(f32) * f2
    fd2 = f2 * pick(reader(delta), pair, oo)
    return back(pick(reader(x, 0), pair, oo), k2, v2, gf2, fd2, es)


def far_back_body(
    info, offsets, counts, x, r3, r4, r12, top, norm, m3, m4, e3, e4, mx0, mx1, mx2, mx3, in0, in1, in2, in3,
    g, delta, acc, d4, d8, d12,
):
    place = Place(info, offsets, counts)
    ri = lax.broadcasted_iota(jnp.int32, (128, 128), 0) >> 6
    ci = lax.broadcasted_iota(jnp.int32, (128, 128), 1) >> 6
    same = jnp.where(ri == ci, 1.0, 0.0)
    for slot, (mx, got) in enumerate(((mx0, in0), (mx1, in1), (mx2, in2), (mx3, in3))):
        sl = slice(slot * 32, slot * 32 + 32)
        rows = got[256:512]
        g[:, sl, :] = rows.reshape(8, 32, 128)
        prod = rows.astype(f32) * mx[0:256].astype(f32)
        sums = lax.dot_general(
            prod, same, (((1,), (0,)), ((), ())), precision=lax.Precision.HIGHEST, preferred_element_type=f32
        )
        delta[:, sl, :] = sums.reshape(8, 32, 128)
    o3, k3, v3 = keys3(place, x, r3)
    o4, k4, v4 = keys4(place, x, r4, r12)
    acc[...] = jnp.zeros_like(acc)
    for pair, oo, k2, v2, m, e, parts in (
        (1, o3, k3, v3, m3, e3, ((d4, 0, 256),)),
        (2, o4, k4, v4, m4, e4, ((d4, 256, 128), (d8, 0, 128), (d12, 0, 128))),
    ):
        grads = pair_back(place, x, g, top, norm, delta, m[...], [e[0], e[1]], pair, oo, k2, v2)
        at_row = m.shape[0]
        for i in range(3):
            put(reader(acc, i), writer(acc, i), grads[i][:at_row], pair, oo, True)
        for ref, start, rows in parts:
            for i in (0, 1):
                ref[i, start : start + rows] = grads[i + 1][at_row : at_row + rows].astype(bf16)
            at_row += rows


def back_two_body(info, offsets, counts, x, g, top, norm, delta, acc_in, m2, e2, acc):
    place = Place(info, offsets, counts)
    acc[...] = acc_in[...]
    oo = place.offs(0)
    k2, v2 = pick(reader(x, 1), 0, oo), pick(reader(x, 2), 0, oo)
    grads = pair_back(place, x, g, top, norm, delta, m2[...], [e2[0], e2[1]], 0, oo, k2, v2)
    for i in range(3):
        put(reader(acc, i), writer(acc, i), grads[i], 0, oo, True)


def back_one_body(info, offsets, counts, x, g, top, norm, delta, acc_in, m1, e1, acc):
    for slot in range(4):
        sl = slice(slot * 32, slot * 32 + 32)
        f2 = jnp.exp(slot_rows(m1, slot) - slot_rows(top, slot)) * slot_rows(norm, slot)
        q2, k2, v2 = [slot_rows(x, slot, i) for i in range(3)]
        g2 = slot_rows(g, slot)
        gf2 = g2.astype(f32) * f2
        fd2 = f2 * slot_rows(delta, slot)
        grads = back(q2, k2, v2, gf2, fd2, [e1[slot, 0], e1[slot, 1]])
        for i in range(3):
            acc[i, :, sl, :] = acc_in[i, :, sl, :] + grads[i].reshape(8, 32, 128)


def cores_body(keep, got, own, s1, s2, s3):
    for d, o in enumerate((own, s1, s2, s3)):
        parts = [keep[4 * u + d] + got[4 * u + d].astype(f32) for u in range(4)]
        o[...] = jnp.concatenate(parts, axis=0).astype(o.dtype)


def halves_body(mine, other, own, s4, s8, s12):
    a, b = mine[...].astype(f32), other[...].astype(f32)
    for u, o in enumerate((own, s4, s8, s12)):
        at = slice(72 * u, 72 * u + 72)
        o[...] = jnp.concatenate([a[at], b[at]], axis=0).astype(o.dtype)


def finish_body(info, offsets, counts, acc_in, r4, r8, r12, o0, o1, o2, o3, acc):
    place = Place(info, offsets, counts)
    acc[...] = acc_in[...]
    p3, p4 = place.offs(1), place.offs(2)
    for i in (0, 1):
        rd, wr = reader(acc, i + 1), writer(acc, i + 1)
        put(rd, wr, r4[i, 0:256].astype(f32), 1, p3, True)
        far = r4[i, 256:384].astype(f32) + r8[i].astype(f32) + r12[i].astype(f32)
        put(rd, wr, far, 2, p4, True)
    for slot, o in enumerate((o0, o1, o2, o3)):
        o[0:256] = (slot_rows(acc, slot, 0) * 0.125).astype(bf16)
        o[256:512] = slot_rows(acc, slot, 1).astype(bf16)
        o[512:768] = slot_rows(acc, slot, 2).astype(bf16)


def home_body(info, m0, m1, m2, m3, dq, dk, dv, wide):
    order = row_order(True)
    for d, m in enumerate((m0, m1, m2, m3)):
        c = pl.multiple_of((info[1] ^ d) * 128, 128)
        for i in range(3):
            wide[i, :, pl.ds(c, 128)] = m[256 * i : 256 * i + 256]
    for i, o in enumerate((dq, dk, dv)):
        o[...] = dot_nn(order, wide[i, :, 0:384]).astype(bf16)


def widen(info, msgs, wide):
    for d, m in enumerate(msgs):
        wide[:, pl.ds(pl.multiple_of((info[1] ^ d) * 128, 128), 128)] = m[0:256]


def project_body(info, m0, m1, m2, m3, og, send, keep, wide, both, away):
    widen(info, (m0, m1, m2, m3), wide)
    both[...] = dot_tn(wide[:, 0:384], og[...])
    for s in range(16):
        for t in range(3):
            at = slice(t * 24, t * 24 + 24)
            there = pl.multiple_of((1 - info[2]) * 384 + t * 128, 128)
            here = pl.multiple_of(info[2] * 384 + t * 128, 128)
            away[s ^ info[0], at] = both[s * 24 : s * 24 + 24, pl.ds(there, 128)]
            keep[s ^ info[0], at] = both[s * 24 : s * 24 + 24, pl.ds(here, 128)]
    send[...] = away[...].astype(bf16)


def attended_body(info, m0, m1, m2, m3, w, o, wide):
    widen(info, (m0, m1, m2, m3), wide)
    mixed = dot_nn(row_order(True), wide[:, 0:384]).astype(bf16)
    o[...] = dot_nn(mixed, w[...]).astype(bf16)


def sum_body(a, b, c, d, o):
    one = a[...].astype(f32) + b[...].astype(f32)
    o[...] = (one + (c[...].astype(f32) + d[...].astype(f32))).astype(o.dtype)


def pair_body(a, b, o):
    o[...] = (a[...].astype(f32) + b[...].astype(f32)).astype(o.dtype)


def join_body(info, own, a, b, c, o):
    total = own[...] + a[...].astype(f32) + (b[...].astype(f32) + c[...].astype(f32))
    for h in (0, 1):
        for t in range(3):
            col = pl.multiple_of((info[2] ^ h) * 384 + t * 128, 128)
            o[:, pl.ds(col, 128)] = total[72 * h + 24 * t : 72 * h + 24 * t + 24]


smem = pl.BlockSpec(memory_space=pltpu.SMEM)
vmem = pl.BlockSpec(memory_space=pltpu.VMEM)
hbm = pl.BlockSpec(memory_space=pltpu.HBM)


def call(body, scalars, arrays, outs, scratch=(), cost=1000, space=vmem, sems=0, limit=12):
    shapes = [jax.ShapeDtypeStruct(s, t) for s, t in outs]
    return pl.pallas_call(
        body,
        out_shape=shapes,
        in_specs=[smem] * len(scalars) + [space] * len(arrays),
        out_specs=[vmem] * len(shapes),
        scratch_shapes=[pltpu.VMEM(s, t) for s, t in scratch] + [pltpu.SemaphoreType.DMA((sems,))] * (sems > 0),
        compiler_params=pltpu.CompilerParams(vmem_limit_bytes=limit * 1024 * 1024),
        cost_estimate=pl.CostEstimate(flops=cost, bytes_accessed=1000, transcendentals=0),
    )(*scalars, *arrays)


def routes(seq_step, keep=None):
    pairs = []
    for dp in range(16):
        for s in range(16):
            t = s ^ seq_step
            if keep is not None and (keep(s, t) & 3) ^ (3 * (dp & 1)) == 3:
                continue
            pairs.append((dp * 16 + s, dp * 16 + t))
    return pairs


def shift(block, pairs):
    return lax.ppermute(block, ("dp", "seq"), pairs)


def dp_step(block, step):
    return lax.ppermute(block, "dp", [(i, i ^ step) for i in range(16)])


def seq_step(block, step):
    return lax.ppermute(block, "seq", [(i, i ^ step) for i in range(16)])


def per_device(queries, keys, values, out_weight, out_grad, offsets, counts):
    seq_rank = lax.axis_index("seq").astype(jnp.int32)
    core = lax.axis_index("dp").astype(jnp.int32) & 1
    info = jnp.stack([seq_rank, (seq_rank & 3) ^ (3 * core), core])
    places = [info, offsets, counts]

    chunk = ((3, 256, 128), bf16)
    third = ((256, 384), bf16)
    cube = (8, 128, 128)
    block = (72, 128)
    active = lambda s, t: s

    msgs = call(
        prep_body,
        [],
        [queries[0], keys[0], values[0]],
        [chunk] * 4,
        [((3, 256, 384), bf16), third, third, third],
        space=hbm,
        sems=3,
        limit=57,
    )
    got = [shift(msgs[d], routes(d)) for d in (1, 2, 3)]
    og, g0, g1, g2, g3, own = call(
        grad_body,
        [info],
        [out_grad[0], out_weight, msgs[0]],
        [((256, 768), bf16)] + [((256, 128), bf16)] * 4 + [chunk],
        [((256, 384), bf16)],
    )
    x, s3, s8 = call(
        collect_body,
        places,
        [own] + got,
        [((3, *cube), bf16), ((2, 256, 128), bf16), ((2, 128, 128), bf16)],
    )
    r4 = shift(s8, routes(4))
    r3 = shift(s3, routes(4))
    top, num, den, m1, m2, e1, e2 = call(
        near_body,
        places,
        [x],
        [(cube, f32)] * 4 + [((512, 128), f32), ((4, 2, 256, 256), bf16), ((2, 512, 512), bf16)],
    )
    top, r4 = lax.optimization_barrier((top, r4))
    (s12,) = call(relay_body, [], [s8, r4], [((4, 128, 128), bf16)])
    r12 = shift(s12, routes(12))
    top, s12 = lax.optimization_barrier((top, s12))
    top, num, den, m3, e3 = call(
        mid_body,
        places,
        [x, r3, top, num, den],
        [(cube, f32)] * 3 + [((256, 128), f32), ((2, 256, 512), bf16)],
    )
    top, norm, mx0, mx1, mx2, mx3, m4, e4 = call(
        far_body,
        places,
        [x, r4, r12, top, num, den, g0, g1, g2, g3],
        [(cube, f32)] * 2 + [((512, 128), bf16)] * 4 + [((128, 128), f32), ((2, 128, 512), bf16)],
        [(cube, f32)] * 2,
    )
    mixed = [mx0] + [shift(b, routes(d)) for d, b in ((1, mx1), (2, mx2), (3, mx3))]
    send, keep = call(
        project_body,
        [info],
        mixed + [og],
        [((16, *block), bf16), ((16, *block), f32)],
        [((256, 512), bf16), ((384, 768), f32), ((16, *block), f32)],
    )
    arrived = dp_step(send, 1)
    keep, *mixed = lax.optimization_barrier([keep] + mixed)
    g, delta, acc, d4, d8, d12 = call(
        far_back_body,
        places,
        [x, r3, r4, r12, top, norm, m3, m4, e3, e4, mx0, mx1, mx2, mx3] + mixed,
        [(cube, bf16), (cube, f32), ((3, *cube), f32)]
        + [((2, 384, 128), bf16), ((2, 128, 128), bf16), ((2, 128, 128), bf16)],
    )
    state = [x, g, top, norm, delta]
    (attended,) = call(
        attended_body, [info], mixed + [out_weight], [((256, 768), bf16)], [((256, 512), bf16)]
    )
    attended, keep = lax.optimization_barrier((attended, keep))
    flat = ((288, 128), bf16)
    own, s1, s2, s3 = call(cores_body, [], [keep, arrived], [((288, 128), f32)] + [flat] * 3)
    near = [seq_step(b, d) for d, b in ((1, s1), (2, s2), (3, s3))]
    d4, d8, d12, own = lax.optimization_barrier((d4, d8, d12, own))
    far = [shift(b, routes(d)) for d, b in ((4, d4), (8, d8), (12, d12))]
    (low,) = call(sum_body, [], [own] + near, [flat])
    acc, low = lax.optimization_barrier((acc, low))
    arrived = dp_step(low, 2)
    (acc,) = call(back_two_body, places, state + [acc, m2, e2], [((3, *cube), f32)])
    acc, low = lax.optimization_barrier((acc, low))
    (low,) = call(pair_body, [], [low, arrived], [flat])
    rest = [dp_step(low, d) for d in (4, 8, 12)]
    acc, low = lax.optimization_barrier((acc, low))
    (acc,) = call(back_one_body, places, state + [acc, m1, e1], [((3, *cube), f32)])
    acc, low = lax.optimization_barrier((acc, low))
    (low,) = call(sum_body, [], [low] + rest, [flat])
    acc, low = lax.optimization_barrier((acc, low))
    other = dp_step(low, 1)
    outs = call(
        finish_body, places, [acc] + far, [((768, 128), bf16)] * 4, [((3, *cube), f32)], cost=2 * 10**9
    )
    *outs, other = lax.optimization_barrier([*outs, other])
    home = [outs[0]] + [shift(outs[d], routes(d)) for d in (1, 2, 3)]
    both = (144, 128)
    own, s4, s8, s12 = call(halves_body, [], [low, other], [(both, f32)] + [(both, bf16)] * 3)
    quarters = [seq_step(b, d) for d, b in ((4, s4), (8, s8), (12, s12))]
    grads = call(home_body, [info], home, [third] * 3, [((3, 256, 512), bf16)])
    *grads, own = lax.optimization_barrier([*grads, own])
    (grad_weight,) = call(join_body, [info], [own] + quarters, [((24, 768), f32)])
    return (attended[None], grads[0][None], grads[1][None], grads[2][None], grad_weight)


def solution(mesh):
    tiles = P("dp", "seq", None)
    return jax.shard_map(
        per_device,
        mesh=mesh,
        in_specs=(tiles, tiles, tiles, P(), tiles, P(), P("dp")),
        out_specs=(tiles, tiles, tiles, tiles, P("seq", None)),
        check_vma=False,
    )
```

```python
import jax
import jax.numpy as jnp
from jax import lax
from jax.experimental import pallas as pl
from jax.experimental.pallas import tpu as pltpu
from jax.sharding import PartitionSpec as P

bf16 = jnp.bfloat16
f32 = jnp.float32
low_bias = -1e30


def dot_nn(a, b):
    return lax.dot_general(a, b, (((1,), (0,)), ((), ())), preferred_element_type=f32)


def dot_nt(a, b):
    return lax.dot_general(a, b, (((1,), (1,)), ((), ())), preferred_element_type=f32)


def dot_tn(a, b):
    return lax.dot_general(a, b, (((0,), (0,)), ((), ())), preferred_element_type=f32)


def first_half(rows):
    return lax.broadcasted_iota(jnp.int32, (rows, 128), 1) < 64


def half_of(x, h):
    m = first_half(x.shape[0])
    z = jnp.zeros_like(x)
    return jnp.where(m, x, z) if h == 0 else jnp.where(m, z, x)


def row_order(back):
    a = lax.broadcasted_iota(jnp.int32, (256, 256), 0 if not back else 1)
    b = lax.broadcasted_iota(jnp.int32, (256, 256), 1 if not back else 0)
    return jnp.where(b == (a & 31) * 8 + (a >> 5), 1.0, 0.0).astype(bf16)


class Place:
    def __init__(self, info, offsets, counts):
        self.j = info[0] & 3
        self.base = (info[0] >> 2) * 1024
        self.quarter = info[0] >> 2
        self.chunk = jnp.minimum(info[1], 2)
        self.count = counts[0]
        self.offsets = offsets

    def offs(self, pair):
        r = 2 << pair
        return [self.offsets[pair, 2 * self.chunk + h] & (r - 1) for h in (0, 1)]

    def bias(self, n, step, o, base):
        kk = lax.broadcasted_iota(jnp.int32, (1, n), 1)
        pos = base + ((self.j ^ ((kk >> 5) & 3)) << 8) + (kk & 31) * 8 + o + step * (kk >> 7)
        return jnp.where(pos < self.count, 0.0, low_bias)

    def bias_slot(self, slot):
        kk = lax.broadcasted_iota(jnp.int32, (1, 256), 1)
        pos = self.base + ((self.j ^ slot) << 8) + (kk & 31) * 8 + (kk >> 5)
        return jnp.where(pos < self.count, 0.0, low_bias)

    def valid(self, res):
        rr = lax.broadcasted_iota(jnp.int32, (128, 128), 0)
        pos = self.base + ((self.j ^ (rr >> 5)) << 8) + (rr & 31) * 8 + res
        return jnp.where(pos < self.count, 1.0, 0.0)


def pick(read, pair, oo):
    r = 2 << pair
    m = first_half(128)
    parts = [jnp.where(m, read(oo[0] + r * i), read(oo[1] + r * i)) for i in range(8 // r)]
    return parts[0] if len(parts) == 1 else jnp.concatenate(parts, axis=0)


def put(read, write, val, pair, oo, add):
    r = 2 << pair
    m = first_half(128)
    for i in range(8 // r):
        blk = val[i * 128 : (i + 1) * 128]
        for h in (0, 1):
            mine = m if h == 0 else ~m
            old = read(oo[h] + r * i)
            write(oo[h] + r * i, jnp.where(mine, old + blk if add else blk, old))


def reader(ref, *lead):
    return lambda i: ref[(*lead, i)]


def writer(ref, *lead):
    def w(i, val):
        ref[(*lead, i)] = val

    return w


def slot_rows(ref, slot, *lead):
    return ref[(*lead, slice(None), slice(slot * 32, slot * 32 + 32), slice(None))].reshape(256, 128)


def attend(q2, k2, v2, bias):
    nk = k2.shape[0]
    out, es, ms = None, [], []
    one = jnp.ones((nk, 128), bf16)
    for h in (0, 1):
        s = dot_nt(q2, half_of(k2, h)) + bias[h]
        m = jnp.max(s, axis=1, keepdims=True)
        e = jnp.exp(s - m).astype(bf16)
        o = dot_nn(e, jnp.concatenate([half_of(v2, h), half_of(one, h)], axis=1))
        out = o if out is None else out + o
        es.append(e)
        ms.append(m)
    n = q2.shape[0]
    top = jnp.where(first_half(n), jnp.broadcast_to(ms[0], (n, 128)), jnp.broadcast_to(ms[1], (n, 128)))
    return es, top, out


def back(q2, k2, v2, gf2, fd2, es):
    low = gf2.astype(bf16)
    qt, gt = q2.astype(f32).T.astype(bf16), gf2.T.astype(bf16)
    dq, dks, dvs = None, [], []
    for h in (0, 1):
        e, at = es[h], slice(64 * h, 64 * h + 64)
        dp = dot_nt(low, half_of(v2, h))
        ds = (e.astype(f32) * (dp - fd2[:, 64 * h : 64 * h + 1])).astype(bf16)
        a = dot_nn(ds, half_of(k2, h))
        dq = a if dq is None else dq + a
        dks.append(dot_nn(qt[at], ds))
        dvs.append(dot_nn(gt[at], e))
    return dq, jnp.concatenate(dks, axis=0).T, jnp.concatenate(dvs, axis=0).T


def copies(pairs, sems):
    moves = [pltpu.make_async_copy(src, dst, sems.at[i]) for i, (src, dst) in enumerate(pairs)]
    for m in moves:
        m.start()
    return moves


def prep_body(q_in, k_in, v_in, o0, o1, o2, o3, px, q, k, v, sems):
    moves = copies(((q_in, q), (k_in, k), (v_in, v)), sems)
    chunk = (lax.axis_index("seq") & 3) ^ (3 * (lax.axis_index("dp") & 1))
    order = row_order(False)
    for i, src in enumerate((q, k, v)):
        moves[i].wait()
        rows = dot_nn(order, src[...])
        px[i] = (rows * 0.125 if i == 0 else rows).astype(bf16)
    for d, o in enumerate((o0, o1, o2, o3)):
        c = pl.multiple_of(jnp.minimum(chunk ^ d, 2) * 128, 128)
        for i in range(3):
            o[i] = px[i, :, pl.ds(c, 128)]


def grad_body(info, og, w, m_in, og_out, o0, o1, o2, o3, m_out, gx):
    m_out[...] = m_in[...]
    ordered = dot_nn(row_order(False), og[...]).astype(bf16)
    og_out[...] = ordered
    gx[...] = dot_nt(ordered, w[...]).astype(bf16)
    for d, o in enumerate((o0, o1, o2, o3)):
        o[...] = gx[:, pl.ds(pl.multiple_of(jnp.minimum(info[1] ^ d, 2) * 128, 128), 128)]


def collect_body(info, offsets, counts, m0, m1, m2, m3, x, s3, s8):
    place = Place(info, offsets, counts)
    for slot, m in enumerate((m0, m1, m2, m3)):
        for i in range(3):
            x[i, :, slot * 32 : slot * 32 + 32, :] = m[i].reshape(8, 32, 128)
    o3, o4 = place.offs(1), place.offs(2)
    for i in (0, 1):
        s3[i] = pick(reader(x, i + 1), 1, o3)
        s8[i] = pick(reader(x, i + 1), 2, o4)


def relay_body(s8, r4, o):
    for i in (0, 1):
        o[i] = s8[i]
        o[2 + i] = r4[i]


def near_body(
    info, offsets, counts, x, top, num, den, m1, m2, e1, e2,
):
    place = Place(info, offsets, counts)
    for slot in range(4):
        b = place.bias_slot(slot)
        sl = slice(slot * 32, slot * 32 + 32)
        es, t, o = attend(*[slot_rows(x, slot, i) for i in range(3)], [b, b])
        e1[slot, 0], e1[slot, 1] = es
        t = t.reshape(8, 32, 128)
        top[:, sl, :] = t
        m1[:, sl, :] = t
        num[:, sl, :] = o[:, :128].reshape(8, 32, 128)
        den[:, sl, :] = o[:, 128:].reshape(8, 32, 128)
    oo = place.offs(0)
    q2, k2, v2 = [pick(reader(x, i), 0, oo) for i in range(3)]
    bias = [place.bias(512, 2, oo[h], place.base) for h in (0, 1)]
    es, t, o = attend(q2, k2, v2, bias)
    e2[0], e2[1] = es
    m2[...] = t
    merge(top, num, den, t, o, 0, oo)


def merge(top, num, den, t, o, pair, oo):
    old = pick(reader(top), pair, oo)
    new = jnp.maximum(old, t)
    a, b = jnp.exp(old - new), jnp.exp(t - new)
    n = pick(reader(num), pair, oo) * a + o[:, :128] * b
    d = pick(reader(den), pair, oo) * a + o[:, 128:] * b
    put(reader(top), writer(top), new, pair, oo, False)
    put(reader(num), writer(num), n, pair, oo, False)
    put(reader(den), writer(den), d, pair, oo, False)


def keys3(place, x, r3):
    oo = place.offs(1)
    return [oo] + [jnp.concatenate([pick(reader(x, i + 1), 1, oo), r3[i]], axis=0) for i in (0, 1)]


def keys4(place, x, r4, r12):
    oo = place.offs(2)
    return [oo] + [
        jnp.concatenate([pick(reader(x, i + 1), 2, oo), r4[i], r12[2 + i], r12[i]], axis=0)
        for i in (0, 1)
    ]


def mid_body(info, offsets, counts, x, r3, top_in, num_in, den_in, top, num, den, m3, e3):
    place = Place(info, offsets, counts)
    top[...] = top_in[...]
    num[...] = num_in[...]
    den[...] = den_in[...]
    oo, k2, v2 = keys3(place, x, r3)
    at = [(place.quarter ^ i) * 1024 for i in (0, 1)]
    bias = [jnp.concatenate([place.bias(256, 4, oo[h], b) for b in at], axis=1) for h in (0, 1)]
    es, t, out = attend(pick(reader(x, 0), 1, oo), k2, v2, bias)
    e3[0], e3[1] = es
    m3[...] = t
    merge(top, num, den, t, out, 1, oo)


def far_body(
    info, offsets, counts, x, r4, r12, top_in, num_in, den_in, g0, g1, g2, g3,
    top, norm, mx0, mx1, mx2, mx3, m4, e4, num, den,
):
    place = Place(info, offsets, counts)
    top[...] = top_in[...]
    num[...] = num_in[...]
    den[...] = den_in[...]
    oo, k2, v2 = keys4(place, x, r4, r12)
    at = [(place.quarter ^ i) * 1024 for i in range(4)]
    bias = [jnp.concatenate([place.bias(128, 8, oo[h], b) for b in at], axis=1) for h in (0, 1)]
    es, t, out = attend(pick(reader(x, 0), 2, oo), k2, v2, bias)
    e4[0], e4[1] = es
    m4[...] = t
    merge(top, num, den, t, out, 2, oo)
    outs = (mx0, mx1, mx2, mx3)
    for res in range(8):
        ok = place.valid(res)
        scale = ok / (den[res] + 1.0 - ok)
        norm[res] = scale
        mixed = (num[res] * scale).astype(bf16)
        for slot, mx in enumerate(outs):
            mx[res * 32 : res * 32 + 32] = mixed[slot * 32 : slot * 32 + 32]
    for mx, g in zip(outs, (g0, g1, g2, g3)):
        mx[256:512] = g[...]


def pair_back(place, x, g, top, norm, delta, t, es, pair, oo, k2, v2):
    f2 = jnp.exp(t - pick(reader(top), pair, oo)) * pick(reader(norm), pair, oo)
    gf2 = pick(reader(g), pair, oo).astype(f32) * f2
    fd2 = f2 * pick(reader(delta), pair, oo)
    return back(pick(reader(x, 0), pair, oo), k2, v2, gf2, fd2, es)


def far_back_body(
    info, offsets, counts, x, r3, r4, r12, top, norm, m3, m4, e3, e4, mx0, mx1, mx2, mx3, in0, in1, in2, in3,
    g, delta, acc, d4, d8, d12,
):
    place = Place(info, offsets, counts)
    ri = lax.broadcasted_iota(jnp.int32, (128, 128), 0) >> 6
    ci = lax.broadcasted_iota(jnp.int32, (128, 128), 1) >> 6
    same = jnp.where(ri == ci, 1.0, 0.0).astype(bf16)
    for slot, (mx, got) in enumerate(((mx0, in0), (mx1, in1), (mx2, in2), (mx3, in3))):
        sl = slice(slot * 32, slot * 32 + 32)
        rows = got[256:512]
        g[:, sl, :] = rows.reshape(8, 32, 128)
        prod = rows.astype(f32) * mx[0:256].astype(f32)
        high = prod.astype(bf16)
        rest = (prod - high.astype(f32)).astype(bf16)
        sums = dot_nn(jnp.concatenate([high, rest], axis=1), jnp.concatenate([same, same], axis=0))
        delta[:, sl, :] = sums.reshape(8, 32, 128)
    o3, k3, v3 = keys3(place, x, r3)
    o4, k4, v4 = keys4(place, x, r4, r12)
    acc[...] = jnp.zeros_like(acc)
    for pair, oo, k2, v2, m, e, parts in (
        (1, o3, k3, v3, m3, e3, ((d4, 0, 256),)),
        (2, o4, k4, v4, m4, e4, ((d4, 256, 128), (d8, 0, 128), (d12, 0, 128))),
    ):
        grads = pair_back(place, x, g, top, norm, delta, m[...], [e[0], e[1]], pair, oo, k2, v2)
        at_row = m.shape[0]
        for i in range(3):
            put(reader(acc, i), writer(acc, i), grads[i][:at_row], pair, oo, True)
        for ref, start, rows in parts:
            for i in (0, 1):
                ref[i, start : start + rows] = grads[i + 1][at_row : at_row + rows].astype(bf16)
            at_row += rows


def back_two_body(info, offsets, counts, x, g, top, norm, delta, acc_in, m2, e2, acc):
    place = Place(info, offsets, counts)
    acc[...] = acc_in[...]
    oo = place.offs(0)
    k2, v2 = pick(reader(x, 1), 0, oo), pick(reader(x, 2), 0, oo)
    grads = pair_back(place, x, g, top, norm, delta, m2[...], [e2[0], e2[1]], 0, oo, k2, v2)
    for i in range(3):
        put(reader(acc, i), writer(acc, i), grads[i], 0, oo, True)


def back_one_body(info, offsets, counts, x, g, top, norm, delta, acc_in, m1, e1, acc):
    for slot in range(4):
        sl = slice(slot * 32, slot * 32 + 32)
        f2 = jnp.exp(slot_rows(m1, slot) - slot_rows(top, slot)) * slot_rows(norm, slot)
        q2, k2, v2 = [slot_rows(x, slot, i) for i in range(3)]
        g2 = slot_rows(g, slot)
        gf2 = g2.astype(f32) * f2
        fd2 = f2 * slot_rows(delta, slot)
        grads = back(q2, k2, v2, gf2, fd2, [e1[slot, 0], e1[slot, 1]])
        for i in range(3):
            acc[i, :, sl, :] = acc_in[i, :, sl, :] + grads[i].reshape(8, 32, 128)


def cores_body(keep, got, own, s1, s2, s3):
    for d, o in enumerate((own, s1, s2, s3)):
        parts = [keep[4 * u + d] + got[4 * u + d].astype(f32) for u in range(4)]
        o[...] = jnp.concatenate(parts, axis=0).astype(o.dtype)


def halves_body(mine, other, own, s4, s8, s12):
    a, b = mine[...].astype(f32), other[...].astype(f32)
    for u, o in enumerate((own, s4, s8, s12)):
        at = slice(72 * u, 72 * u + 72)
        o[...] = jnp.concatenate([a[at], b[at]], axis=0).astype(o.dtype)


def finish_body(info, offsets, counts, acc_in, r4, r8, r12, o0, o1, o2, o3, acc):
    place = Place(info, offsets, counts)
    acc[...] = acc_in[...]
    p3, p4 = place.offs(1), place.offs(2)
    for i in (0, 1):
        rd, wr = reader(acc, i + 1), writer(acc, i + 1)
        put(rd, wr, r4[i, 0:256].astype(f32), 1, p3, True)
        far = r4[i, 256:384].astype(f32) + r8[i].astype(f32) + r12[i].astype(f32)
        put(rd, wr, far, 2, p4, True)
    for slot, o in enumerate((o0, o1, o2, o3)):
        o[0:256] = (slot_rows(acc, slot, 0) * 0.125).astype(bf16)
        o[256:512] = slot_rows(acc, slot, 1).astype(bf16)
        o[512:768] = slot_rows(acc, slot, 2).astype(bf16)


def home_body(info, m0, m1, m2, m3, dq, dk, dv, wide):
    order = row_order(True)
    for d, m in enumerate((m0, m1, m2, m3)):
        c = pl.multiple_of((info[1] ^ d) * 128, 128)
        for i in range(3):
            wide[i, :, pl.ds(c, 128)] = m[256 * i : 256 * i + 256]
    for i, o in enumerate((dq, dk, dv)):
        o[...] = dot_nn(order, wide[i, :, 0:384]).astype(bf16)


def widen(info, msgs, wide):
    for d, m in enumerate(msgs):
        wide[:, pl.ds(pl.multiple_of((info[1] ^ d) * 128, 128), 128)] = m[0:256]


def project_body(info, m0, m1, m2, m3, og, send, keep, wide, both, away):
    widen(info, (m0, m1, m2, m3), wide)
    both[...] = dot_tn(wide[:, 0:384], og[...])
    for s in range(16):
        for t in range(3):
            at = slice(t * 24, t * 24 + 24)
            there = pl.multiple_of((1 - info[2]) * 384 + t * 128, 128)
            here = pl.multiple_of(info[2] * 384 + t * 128, 128)
            away[s ^ info[0], at] = both[s * 24 : s * 24 + 24, pl.ds(there, 128)]
            keep[s ^ info[0], at] = both[s * 24 : s * 24 + 24, pl.ds(here, 128)]
    send[...] = away[...].astype(bf16)


def attended_body(info, m0, m1, m2, m3, w, o, wide):
    widen(info, (m0, m1, m2, m3), wide)
    mixed = dot_nn(row_order(True), wide[:, 0:384]).astype(bf16)
    o[...] = dot_nn(mixed, w[...]).astype(bf16)


def sum_body(a, b, c, d, o):
    one = a[...].astype(f32) + b[...].astype(f32)
    o[...] = (one + (c[...].astype(f32) + d[...].astype(f32))).astype(o.dtype)


def pair_body(a, b, o):
    o[...] = (a[...].astype(f32) + b[...].astype(f32)).astype(o.dtype)


def join_body(info, own, a, b, c, o):
    total = own[...] + a[...].astype(f32) + (b[...].astype(f32) + c[...].astype(f32))
    for h in (0, 1):
        for t in range(3):
            col = pl.multiple_of((info[2] ^ h) * 384 + t * 128, 128)
            o[:, pl.ds(col, 128)] = total[72 * h + 24 * t : 72 * h + 24 * t + 24]


smem = pl.BlockSpec(memory_space=pltpu.SMEM)
vmem = pl.BlockSpec(memory_space=pltpu.VMEM)
hbm = pl.BlockSpec(memory_space=pltpu.HBM)


def call(body, scalars, arrays, outs, scratch=(), cost=1000, space=vmem, sems=0, limit=12):
    shapes = [jax.ShapeDtypeStruct(s, t) for s, t in outs]
    return pl.pallas_call(
        body,
        out_shape=shapes,
        in_specs=[smem] * len(scalars) + [space] * len(arrays),
        out_specs=[vmem] * len(shapes),
        scratch_shapes=[pltpu.VMEM(s, t) for s, t in scratch] + [pltpu.SemaphoreType.DMA((sems,))] * (sems > 0),
        compiler_params=pltpu.CompilerParams(vmem_limit_bytes=limit * 1024 * 1024),
        cost_estimate=pl.CostEstimate(flops=cost, bytes_accessed=1000, transcendentals=0),
    )(*scalars, *arrays)


def routes(seq_step, keep=None):
    pairs = []
    for dp in range(16):
        for s in range(16):
            t = s ^ seq_step
            if keep is not None and (keep(s, t) & 3) ^ (3 * (dp & 1)) == 3:
                continue
            pairs.append((dp * 16 + s, dp * 16 + t))
    return pairs


def shift(block, pairs):
    return lax.ppermute(block, ("dp", "seq"), pairs)


def dp_step(block, step):
    return lax.ppermute(block, "dp", [(i, i ^ step) for i in range(16)])


def seq_step(block, step):
    return lax.ppermute(block, "seq", [(i, i ^ step) for i in range(16)])


def per_device(queries, keys, values, out_weight, out_grad, offsets, counts):
    seq_rank = lax.axis_index("seq").astype(jnp.int32)
    core = lax.axis_index("dp").astype(jnp.int32) & 1
    info = jnp.stack([seq_rank, (seq_rank & 3) ^ (3 * core), core])
    places = [info, offsets, counts]

    chunk = ((3, 256, 128), bf16)
    third = ((256, 384), bf16)
    cube = (8, 128, 128)
    block = (72, 128)
    active = lambda s, t: s

    msgs = call(
        prep_body,
        [],
        [queries[0], keys[0], values[0]],
        [chunk] * 4,
        [((3, 256, 384), bf16), third, third, third],
        space=hbm,
        sems=3,
        limit=57,
    )
    got = [shift(msgs[d], routes(d)) for d in (1, 2, 3)]
    og, g0, g1, g2, g3, own = call(
        grad_body,
        [info],
        [out_grad[0], out_weight, msgs[0]],
        [((256, 768), bf16)] + [((256, 128), bf16)] * 4 + [chunk],
        [((256, 384), bf16)],
    )
    x, s3, s8 = call(
        collect_body,
        places,
        [own] + got,
        [((3, *cube), bf16), ((2, 256, 128), bf16), ((2, 128, 128), bf16)],
    )
    r4 = shift(s8, routes(4))
    r3 = shift(s3, routes(4))
    top, num, den, m1, m2, e1, e2 = call(
        near_body,
        places,
        [x],
        [(cube, f32)] * 4 + [((512, 128), f32), ((4, 2, 256, 256), bf16), ((2, 512, 512), bf16)],
    )
    top, r4 = lax.optimization_barrier((top, r4))
    (s12,) = call(relay_body, [], [s8, r4], [((4, 128, 128), bf16)])
    r12 = shift(s12, routes(12))
    top, s12 = lax.optimization_barrier((top, s12))
    top, num, den, m3, e3 = call(
        mid_body,
        places,
        [x, r3, top, num, den],
        [(cube, f32)] * 3 + [((256, 128), f32), ((2, 256, 512), bf16)],
    )
    top, norm, mx0, mx1, mx2, mx3, m4, e4 = call(
        far_body,
        places,
        [x, r4, r12, top, num, den, g0, g1, g2, g3],
        [(cube, f32)] * 2 + [((512, 128), bf16)] * 4 + [((128, 128), f32), ((2, 128, 512), bf16)],
        [(cube, f32)] * 2,
    )
    mixed = [mx0] + [shift(b, routes(d)) for d, b in ((1, mx1), (2, mx2), (3, mx3))]
    send, keep = call(
        project_body,
        [info],
        mixed + [og],
        [((16, *block), bf16), ((16, *block), f32)],
        [((256, 512), bf16), ((384, 768), f32), ((16, *block), f32)],
    )
    arrived = dp_step(send, 1)
    keep, *mixed = lax.optimization_barrier([keep] + mixed)
    g, delta, acc, d4, d8, d12 = call(
        far_back_body,
        places,
        [x, r3, r4, r12, top, norm, m3, m4, e3, e4, mx0, mx1, mx2, mx3] + mixed,
        [(cube, bf16), (cube, f32), ((3, *cube), f32)]
        + [((2, 384, 128), bf16), ((2, 128, 128), bf16), ((2, 128, 128), bf16)],
    )
    state = [x, g, top, norm, delta]
    (attended,) = call(
        attended_body, [info], mixed + [out_weight], [((256, 768), bf16)], [((256, 512), bf16)]
    )
    attended, keep = lax.optimization_barrier((attended, keep))
    flat = ((288, 128), bf16)
    own, s1, s2, s3 = call(cores_body, [], [keep, arrived], [((288, 128), f32)] + [flat] * 3)
    near = [seq_step(b, d) for d, b in ((1, s1), (2, s2), (3, s3))]
    d4, d8, d12, own = lax.optimization_barrier((d4, d8, d12, own))
    far = [shift(b, routes(d)) for d, b in ((8, d8), (12, d12), (4, d4))]
    far = [far[2], far[0], far[1]]
    (low,) = call(sum_body, [], [own] + near, [flat])
    acc, low = lax.optimization_barrier((acc, low))
    arrived = dp_step(low, 2)
    (acc,) = call(back_two_body, places, state + [acc, m2, e2], [((3, *cube), f32)])
    acc, low = lax.optimization_barrier((acc, low))
    (low,) = call(pair_body, [], [low, arrived], [flat])
    rest = [dp_step(low, d) for d in (4, 8, 12)]
    acc, low = lax.optimization_barrier((acc, low))
    (acc,) = call(back_one_body, places, state + [acc, m1, e1], [((3, *cube), f32)])
    acc, low = lax.optimization_barrier((acc, low))
    (low,) = call(sum_body, [], [low] + rest, [flat])
    acc, low = lax.optimization_barrier((acc, low))
    other = dp_step(low, 1)
    outs = call(
        finish_body, places, [acc] + far, [((768, 128), bf16)] * 4, [((3, *cube), f32)], cost=2 * 10**9
    )
    *outs, other = lax.optimization_barrier([*outs, other])
    home = [outs[0]] + [shift(outs[d], routes(d)) for d in (1, 2, 3)]
    both = (144, 128)
    own, s4, s8, s12 = call(halves_body, [], [low, other], [(both, f32)] + [(both, bf16)] * 3)
    quarters = [seq_step(b, d) for d, b in ((4, s4), (8, s8), (12, s12))]
    grads = call(home_body, [info], home, [third] * 3, [((3, 256, 512), bf16)])
    *grads, own = lax.optimization_barrier([*grads, own])
    (grad_weight,) = call(join_body, [info], [own] + quarters, [((24, 768), f32)])
    return (attended[None], grads[0][None], grads[1][None], grads[2][None], grad_weight)


def solution(mesh):
    tiles = P("dp", "seq", None)
    return jax.shard_map(
        per_device,
        mesh=mesh,
        in_specs=(tiles, tiles, tiles, P(), tiles, P(), P("dp")),
        out_specs=(tiles, tiles, tiles, tiles, P("seq", None)),
        check_vma=False,
    )
```
